32 devices in a mesh: expert: 8 (over z, y), seq: 4 (over x, core).
Axes of the slice: x: 2, y: 2, z: 4, core: 2. Of those that a mesh axis runs over, the one named last changes fastest.
Arguments:
- inputs: bfloat16 [16, 1024, 1024], P('expert', 'seq'), may hold values from -6 to 6
- query_key_value_weight: bfloat16 [1024, 3072], replicated, may hold values from -0.25 to 0.25
- output_weight: bfloat16 [1024, 1024], replicated, may hold values from -1.5 to 1.5
- gain_attn: float32 [1024], replicated, may hold values from 0.25 to 1.75
- gain_ffn: float32 [1024], replicated, may hold values from 0.25 to 1.75
- w_up: bfloat16 [8, 4096, 1024], P('expert', 'seq'), may hold values from -0.1875 to 0.1875
- w_down: bfloat16 [8, 4096, 1024], P('expert', 'seq'), may hold values from -0.1875 to 0.1875
- expert_of: int32 [16, 1024], P('expert', 'seq'), may hold values from 0 to 7, as said below
- cotangent: bfloat16 [16, 1024, 1024], P('expert', 'seq'), may hold values from -6 to 6
Outputs:
- block_out: bfloat16 [16, 1024, 1024], P('expert', 'seq')
- input_grad: float32 [16, 1024, 1024], P('expert', 'seq')
- qkv_grad: float32 [1024, 3072], replicated
- out_grad: float32 [1024, 1024], replicated
- attn_gain_grad: float32 [1024], replicated
- ffn_gain_grad: float32 [1024], replicated
- up_grad: float32 [8, 4096, 1024], P('expert', 'seq')
- down_grad: float32 [8, 4096, 1024], P('expert', 'seq')
The draws below stay inside these ranges and needn't reach their ends.
Inputs may be any that keep to these rules, and one draw needn't show every extreme that they name: `expert_of`: in every draw at most 128 tokens of one device (one index of each axis) name the same expert, and one expert is named by exactly 128 tokens of every device.
All inputs are finite; a program needn't handle non-finite values.
Results may differ from the reference program's by a relative error of at most 0.013.
The reference program's roundings to bfloat16 on the way count: a program that leaves them out, or rounds other values in their place, can miss the bound.
Values may be sent and summed in bfloat16 or wider, within the bound.
No kernel may reach another device: no remote copies, remote signals or barrier semaphores. Data moves between devices by JAX's collectives and lax.ppermute only.
A program may use at most 320 MiB of HBM per device.

```python
import jax
import jax.numpy as jnp
from jax import lax

D = 1024
HEAD_DIM = 64
FF = 4096
SEQ_LEN = 1024
SEQ_GROUP = 2
TOK_DEV = 512
SEQS = 16
EXPERTS = 8
CAP = 128
N_EXPERT = 8
N_SEQ = 4


def draw_expert_of(key, part):
    key = jax.random.fold_in(key, 11)
    hot_key, level_key, score_key, order_key = jax.random.split(key, 4)
    blocks = N_EXPERT * N_SEQ
    slot_count = EXPERTS * CAP
    local_len = SEQ_LEN // N_SEQ
    slot_expert = jnp.arange(slot_count, dtype=jnp.int32) // CAP
    hottest = jax.random.randint(hot_key, (), 0, EXPERTS, dtype=jnp.int32)
    levels = jax.random.randint(level_key, (EXPERTS,), 0, 4, dtype=jnp.int32)
    base_score = jnp.where(slot_expert == hottest, 65536, levels[slot_expert] * 4096)
    noise_part = jax.random.randint(score_key, (blocks, slot_count), 0, 16384, dtype=jnp.int32)
    scores = (base_score[None, :] + noise_part) * slot_count + jnp.arange(slot_count, dtype=jnp.int32)[None, :]
    chosen = lax.top_k(scores, TOK_DEV)[1]
    experts = (chosen // CAP).astype(jnp.int32)
    shuffle = jax.random.randint(order_key, (blocks, TOK_DEV), 0, 262144, dtype=jnp.int32) * TOK_DEV
    shuffle = shuffle + jnp.arange(TOK_DEV, dtype=jnp.int32)[None, :]
    row_order = jnp.argsort(shuffle, axis=1)
    experts = jnp.take_along_axis(experts, row_order, axis=1)
    experts = experts.reshape(N_EXPERT, N_SEQ, SEQ_GROUP, local_len)
    return experts.transpose(0, 2, 1, 3).reshape(SEQS, SEQ_LEN)


def shard_levels(key, dims, cuts, low, top_value):
    loudness = 1.0
    for dim, parts in cuts:
        steps = jax.random.uniform(jax.random.fold_in(jax.random.fold_in(key, 6), dim), (parts,), jnp.float32, low / len(cuts), top_value / len(cuts))
        loudness = loudness * jnp.repeat(jnp.exp(steps), dims[dim] // parts).reshape((-1,) + (1,) * (len(dims) - 1 - dim))
    return loudness


def noise(rng, dims, width, most, cuts=(), held_as=jnp.bfloat16):
    level = shard_levels(rng, dims, cuts, -0.22, 0.18) if cuts else 1.0
    values = jax.random.normal(rng, dims, jnp.float32) * width * level
    return jnp.minimum(jnp.maximum(values, -most), most).astype(held_as)


def setup_inputs(seed: int = 0) -> dict:
    seeds = jax.random.split(jax.random.key(seed), 10)
    inputs = noise(seeds[0], (SEQS, SEQ_LEN, D), 1.0, 6.0, ((0, 8), (1, 4)))
    query_key_value_weight = noise(seeds[1], (D, 3 * D), (D // 2) ** -0.5, 0.25)
    output_weight = noise(seeds[2], (D, D), (D // 64) ** -0.5, 1.5)
    gain_attn = jnp.clip(1.0 + 0.15 * jax.random.normal(seeds[3], (D,), jnp.float32), 0.25, 1.75)
    gain_ffn = jnp.clip(1.0 + 0.15 * jax.random.normal(seeds[4], (D,), jnp.float32), 0.25, 1.75)
    w_up = noise(seeds[5], (EXPERTS, FF, D), D ** -0.5, 0.1875, ((0, 8), (1, 4)))
    w_down = noise(seeds[6], (EXPERTS, FF, D), (FF // 4) ** -0.5, 0.1875, ((0, 8), (1, 4)))
    expert_of = draw_expert_of(jax.random.fold_in(seeds[9], 71), 0)
    cotangent = noise(seeds[8], (SEQS, SEQ_LEN, D), 1.0, 6.0, ((0, 8), (1, 4)))
    return dict(inputs=inputs, query_key_value_weight=query_key_value_weight, output_weight=output_weight, gain_attn=gain_attn, gain_ffn=gain_ffn, w_up=w_up, w_down=w_down, expert_of=expert_of, cotangent=cotangent)


epsilon = 1e-06
highest_precision = lax.Precision.HIGHEST

@jax.custom_vjp
def reduced_precision(v):
    return lax.optimization_barrier(v.astype(jnp.bfloat16)).astype(jnp.float32)

@jax.custom_vjp
def reduced_backward(v):
    return v

def low_keep(v):
    return (reduced_precision(v), None)

def low_pass(kept, grad):
    return (grad,)

def back_keep(v):
    return (v, None)

def back_low(kept, grad):
    return (reduced_precision(grad),)
reduced_precision.defvjp(low_keep, low_pass)
reduced_backward.defvjp(back_keep, back_low)

def rms_norm(values, scale_gain):
    inverse = lax.rsqrt(lax.optimization_barrier(jnp.mean(values * values, axis=-1, keepdims=True)) + epsilon)
    return values * inverse * scale_gain

def attend_sequence(triple):
    queries, key_rows, value_rows = triple
    length = queries.shape[0]
    scores = jnp.einsum('qhd,khd->hqk', queries, key_rows, precision=highest_precision) * 0.125
    scores = reduced_backward(scores)
    places = jnp.arange(length, dtype=jnp.int32)
    causal = places[:, None] >= places[None, :]
    scores = jnp.where(causal[None, :, :], scores, -1e+30)
    row_max = lax.optimization_barrier(jnp.max(scores, axis=-1, keepdims=True))
    raised = jnp.exp(scores - row_max)
    weights = reduced_precision(raised / lax.optimization_barrier(jnp.sum(raised, axis=-1, keepdims=True)))
    return jnp.einsum('hqk,khd->qhd', weights, value_rows, precision=highest_precision)

def expert_block(rows_in, up_rows, down_rows):
    pre_act = reduced_backward(jnp.einsum('rd,fd->rf', rows_in, up_rows, precision=highest_precision))
    activated = reduced_precision(jax.nn.gelu(pre_act, approximate=False))
    return reduced_backward(reduced_precision(jnp.einsum('rf,fd->rd', activated, down_rows, precision=highest_precision)))

def block_forward(inputs, query_key_value_weight, output_weight, gain_attn, gain_ffn, w_up, w_down, expert_of):
    seq_total, length, model_width = inputs.shape
    head_count = model_width // HEAD_DIM
    normed_input = reduced_precision(rms_norm(inputs, gain_attn))
    projected_output = reduced_backward(reduced_precision(jnp.einsum('cix,xw->ciw', normed_input, query_key_value_weight, precision=highest_precision)))
    projected_output = projected_output.reshape(seq_total, length, 3, head_count, HEAD_DIM)
    attention_result = lax.map(jax.checkpoint(attend_sequence), (projected_output[:, :, 0], projected_output[:, :, 1], projected_output[:, :, 2]))
    attention_result = reduced_backward(reduced_precision(attention_result.reshape(seq_total, length, model_width)))
    hidden_state = inputs + reduced_backward(jnp.einsum('cix,xw->ciw', attention_result, output_weight, precision=highest_precision))
    ffn_input = reduced_backward(reduced_precision(rms_norm(hidden_state, gain_ffn)))
    token_count = seq_total * length
    padded = jnp.concatenate([ffn_input.reshape(token_count, model_width), jnp.zeros((1, model_width), ffn_input.dtype)], axis=0)
    routes = expert_of.reshape(token_count)
    most_rows = N_EXPERT * N_SEQ * CAP

    def pick_rows(number):
        return jnp.nonzero(routes == number, size=most_rows, fill_value=token_count)[0].astype(jnp.int32)
    picked_all = lax.map(pick_rows, jnp.arange(EXPERTS, dtype=jnp.int32))

    def one_expert(pieces):
        picked, up_rows, down_rows = pieces
        return expert_block(padded[picked], up_rows, down_rows)
    results = lax.map(jax.checkpoint(one_expert), (picked_all, w_up, w_down))
    summed = jnp.zeros((token_count + 1, model_width), ffn_input.dtype)
    summed = summed.at[picked_all.reshape(-1)].add(results.reshape(-1, model_width))
    return hidden_state + summed[:token_count].reshape(seq_total, length, model_width)

def reference(inputs, query_key_value_weight, output_weight, gain_attn, gain_ffn, w_up, w_down, expert_of, cotangent):
    floats = (inputs.astype(jnp.float32), query_key_value_weight.astype(jnp.float32), output_weight.astype(jnp.float32), gain_attn.astype(jnp.float32), gain_ffn.astype(jnp.float32), w_up.astype(jnp.float32), w_down.astype(jnp.float32))

    def forward_only(*params):
        return block_forward(*params, expert_of)
    output, pullback = jax.vjp(forward_only, *floats)
    gradients = pullback(cotangent.astype(jnp.float32))
    return (output.astype(jnp.bfloat16), gradients[0], gradients[1], gradients[2], gradients[3], gradients[4], gradients[5], gradients[6])
```

```python
import jax
import jax.numpy as jnp
from jax import lax
from jax.experimental import pallas as pl
from jax.experimental.pallas import tpu as pltpu
from jax.sharding import PartitionSpec as P

HEAD_DIM = 64
EPSILON = 1e-06
SCORE_SCALE = 0.125 * 1.4426950408889634
bf16, f32 = jnp.bfloat16, jnp.float32

NN = (((1,), (0,)), ((), ()))
NT = (((1,), (1,)), ((), ()))
TN = (((0,), (0,)), ((), ()))


def dot(left, right, dims=NN):
    return lax.dot_general(left, right, dims, preferred_element_type=f32)


def sds(shape, dtype):
    return jax.ShapeDtypeStruct(shape, dtype)


def whole(shape):
    return pl.BlockSpec(shape, lambda *_: (0,) * len(shape))


def kernel_call(body, grid, ids, ins, outs, scratch=(), flops=0, moved=0, vmem=56):
    in_specs = [whole(a.shape) if sp is None else sp for a, sp in ins]
    out_specs = [whole(sh) if sp is None else sp for sh, _, sp in outs]
    return pl.pallas_call(
        body,
        grid_spec=pltpu.PrefetchScalarGridSpec(
            num_scalar_prefetch=1,
            grid=grid,
            in_specs=in_specs,
            out_specs=out_specs,
            scratch_shapes=list(scratch),
        ),
        out_shape=[sds(sh, dt) for sh, dt, _ in outs],
        compiler_params=pltpu.CompilerParams(
            vmem_limit_bytes=vmem << 20, dimension_semantics=("arbitrary",) * len(grid)
        ),
        cost_estimate=pl.CostEstimate(flops=flops, bytes_accessed=moved, transcendentals=0),
    )(ids, *[a for a, _ in ins])


def swap(value, axis, step):
    size = lax.axis_size(axis)
    return lax.ppermute(value, axis, [(i, i ^ step) for i in range(size)])


def norm_scale(values):
    return lax.rsqrt(jnp.mean(values * values, axis=-1, keepdims=True) + EPSILON)


def route(ids, routes, rows, groups, capacity):
    tokens, width = rows.shape
    slots = groups * capacity

    def body(ids_ref, routes_ref, rows_ref, slot_ref, column_ref, *send_refs):
        me = ids_ref[1]
        route_row = routes_ref[...]
        named = lax.broadcasted_iota(jnp.int32, (groups, tokens), 0) == route_row
        ones = jnp.where(named, 1.0, 0.0)
        earlier = lax.broadcasted_iota(jnp.int32, (tokens, tokens), 0)
        later = lax.broadcasted_iota(jnp.int32, (tokens, tokens), 1)
        upto = jnp.where(earlier <= later, 1.0, 0.0)
        count = dot(ones, upto)
        place = jnp.sum(count * ones, axis=0, keepdims=True) - 1.0
        slot = (route_row ^ me) * capacity + place.astype(jnp.int32)
        slot_ref[...] = slot
        column_ref[...] = jnp.transpose(jnp.broadcast_to(slot.astype(f32), (128, tokens)))
        pick = lax.broadcasted_iota(jnp.int32, (slots, tokens), 0) == slot
        laid = dot(jnp.where(pick, 1.0, 0.0).astype(bf16), rows_ref[...])
        for k in range(groups):
            send_refs[k][...] = laid[k * capacity : (k + 1) * capacity].astype(bf16)

    out = kernel_call(
        body,
        (1,),
        ids,
        [(routes, None), (rows, None)],
        [((1, tokens), jnp.int32, None), ((tokens, 128), f32, None)]
        + [((capacity, width), bf16, None)] * groups,
        flops=2 * slots * tokens * width,
        moved=4 << 20,
    )
    return out[0], out[1], out[2:]


def one_hot_columns(column, slots):
    wide = jnp.concatenate([column] * (slots // 128), axis=1)
    lanes = lax.broadcasted_iota(jnp.int32, wide.shape, 1).astype(f32)
    return jnp.where(wide == lanes, 1.0, 0.0).astype(bf16)


def project(ids, rows, gain, weight):
    tokens, width = rows.shape
    part = width // lax.axis_size("seq")
    heads = width // part

    def body(ids_ref, x_ref, gain_ref, wq_ref, wk_ref, wv_ref, n_ref, q_ref, k_ref, v_ref):
        values = x_ref[...].astype(f32)
        normed = (values * norm_scale(values) * gain_ref[...]).astype(bf16)
        n_ref[...] = normed
        q_ref[...] = dot(normed, wq_ref[...]).astype(bf16)
        k_ref[...] = dot(normed, wk_ref[...]).astype(bf16)
        v_ref[...] = dot(normed, wv_ref[...]).astype(bf16)

    half = tokens // 2
    column = lambda which: pl.BlockSpec((width, part), lambda i, d: (0, d[0] + which * heads))
    row_spec = lambda n: pl.BlockSpec((half, n), lambda i, d: (i, 0))
    return kernel_call(
        body,
        (2,),
        ids,
        [(rows, row_spec(width)), (gain, None)] + [(weight, column(w)) for w in range(3)],
        [((tokens, width), bf16, row_spec(width))]
        + [((tokens, part), bf16, row_spec(part))] * 3,
        flops=6 * tokens * width * part,
        moved=5 << 20,
    )


def head_lanes(block, head):
    lanes = lax.broadcasted_iota(jnp.int32, block.shape, 1)
    inside = (lanes >= head * HEAD_DIM) & (lanes < (head + 1) * HEAD_DIM)
    return jnp.where(inside, block, jnp.zeros_like(block))


def fold_rows(values, how):
    return how(values.reshape(values.shape[0] // 8, 8, values.shape[1]), axis=0)


def attention(ids, queries, keys, values):
    blocks = len(queries)
    tokens, part = queries[0].shape
    length = tokens // 2
    heads = part // HEAD_DIM
    total = blocks * length

    def body(ids_ref, *refs):
        ins, refs = refs[: 3 * blocks], refs[3 * blocks :]
        out_refs, refs = refs[:blocks], refs[blocks:]
        ot_ref, lse_ref, q_all, k_all, vt_all, stacked, scores, result = refs
        me = ids_ref[0]
        for j in range(blocks):
            rows = pl.ds(pl.multiple_of((me ^ j) * length, length), length)
            q_all[rows, :] = ins[j][...]
            k_all[rows, :] = ins[blocks + j][...]
            vt_all[:, rows] = jnp.transpose(ins[2 * blocks + j][...].astype(f32)).astype(bf16)
        hidden = lax.broadcasted_iota(jnp.int32, (length, length), 0) > lax.broadcasted_iota(
            jnp.int32, (length, length), 1
        )
        for qa in range(blocks):
            here = slice(qa * length, (qa + 1) * length)
            q_block = q_all[here, :]
            for h in range(heads):
                stacked[h * length : (h + 1) * length, :] = head_lanes(q_block, h)
            for h in range(heads):
                lanes = slice(h * length, (h + 1) * length)
                most = None
                for kb in range(qa + 1):
                    there = slice(kb * length, (kb + 1) * length)
                    found = dot(k_all[there, :], stacked[lanes, :], NT)
                    if kb == qa:
                        found = jnp.where(hidden, -1e30, found)
                    scores[there, lanes] = found
                    top = fold_rows(found, jnp.max)
                    most = top if most is None else jnp.maximum(most, top)
                peak = jnp.max(most, axis=0, keepdims=True) * SCORE_SCALE
                summed, gathered = None, None
                for kb in range(qa + 1):
                    there = slice(kb * length, (kb + 1) * length)
                    raised = jnp.exp2(scores[there, lanes] * SCORE_SCALE - peak)
                    part_sum = fold_rows(raised, jnp.sum)
                    summed = part_sum if summed is None else summed + part_sum
                    piece = dot(
                        vt_all[h * HEAD_DIM : (h + 1) * HEAD_DIM, there], raised.astype(bf16)
                    )
                    gathered = piece if gathered is None else gathered + piece
                weight = jnp.sum(summed, axis=0, keepdims=True)
                ot_ref[0, h * HEAD_DIM : (h + 1) * HEAD_DIM, here] = gathered * (1.0 / weight)
                lse_ref[0, qa : qa + 1, lanes] = peak + jnp.log2(weight)
            result[here, :] = jnp.transpose(ot_ref[0, :, here]).astype(bf16)
        for j in range(blocks):
            rows = pl.ds(pl.multiple_of((me ^ j) * length, length), length)
            out_refs[j][...] = result[rows, :]

    spec = pl.BlockSpec((length, part), lambda i, d: (i, 0))
    out = kernel_call(
        body,
        (2,),
        ids,
        [(a, spec) for a in (*queries, *keys, *values)],
        [((tokens, part), bf16, spec)] * blocks
        + [
            ((2, part, total), f32, pl.BlockSpec((1, part, total), lambda i, d: (i, 0, 0))),
            (
                (2, blocks, heads * length),
                f32,
                pl.BlockSpec((1, blocks, heads * length), lambda i, d: (i, 0, 0)),
            ),
        ],
        [
            pltpu.VMEM((total, part), bf16),
            pltpu.VMEM((total, part), bf16),
            pltpu.VMEM((part, total), bf16),
            pltpu.VMEM((heads * length, part), bf16),
            pltpu.VMEM((total, heads * length), f32),
            pltpu.VMEM((total, part), bf16),
        ],
        flops=2 * 10 * heads * 4 * length * length * part,
        moved=8 << 20,
    )
    return out[:blocks], out[blocks], out[blocks + 1]


def attention_back(ids, queries, keys, values, grads, ot, lse):
    blocks = len(queries)
    tokens, part = queries[0].shape
    length = tokens // 2
    heads = part // HEAD_DIM
    total = blocks * length

    def body(ids_ref, *refs):
        ins, refs = refs[: 4 * blocks], refs[4 * blocks :]
        ot_ref, lse_ref, refs = refs[0], refs[1], refs[2:]
        out_refs, refs = refs[:blocks], refs[blocks:]
        q_all, k_all, v_all, g_all, kt_all, q_stack, g_stack, low, ds_low, dk, dv, dqt, dq = refs
        me = ids_ref[0]
        for j in range(blocks):
            rows = pl.ds(pl.multiple_of((me ^ j) * length, length), length)
            q_all[rows, :] = ins[j][...]
            k_all[rows, :] = ins[blocks + j][...]
            v_all[rows, :] = ins[2 * blocks + j][...]
            g_all[rows, :] = ins[3 * blocks + j][...]
            kt_all[:, rows] = jnp.transpose(ins[blocks + j][...].astype(f32)).astype(bf16)
        dk[...] = jnp.zeros_like(dk)
        dv[...] = jnp.zeros_like(dv)
        hidden = lax.broadcasted_iota(jnp.int32, (length, length), 0) > lax.broadcasted_iota(
            jnp.int32, (length, length), 1
        )
        for qa in range(blocks):
            here = slice(qa * length, (qa + 1) * length)
            q_block, g_block = q_all[here, :], g_all[here, :]
            for h in range(heads):
                lanes = slice(h * length, (h + 1) * length)
                q_stack[lanes, :] = head_lanes(q_block, h)
                g_stack[lanes, :] = head_lanes(g_block, h)
            product = jnp.transpose(g_block.astype(f32)) * ot_ref[0, :, here]
            totals = [
                jnp.sum(product[h * HEAD_DIM : (h + 1) * HEAD_DIM], axis=0, keepdims=True)
                for h in range(heads)
            ]
            for kb in range(qa + 1):
                there = slice(kb * length, (kb + 1) * length)
                for h in range(heads):
                    lanes = slice(h * length, (h + 1) * length)
                    found = dot(k_all[there, :], q_stack[lanes, :], NT)
                    if kb == qa:
                        found = jnp.where(hidden, -1e30, found)
                    probs = jnp.exp2(found * SCORE_SCALE - lse_ref[0, qa : qa + 1, lanes])
                    grad_probs = dot(v_all[there, :], g_stack[lanes, :], NT)
                    low[:, lanes] = probs.astype(bf16)
                    ds_low[:, lanes] = (probs * (grad_probs - totals[h])).astype(bf16)
                dv[there, :] += dot(low[...], g_stack[...])
                dk[there, :] += dot(ds_low[...], q_stack[...])
                for h in range(heads):
                    lanes = slice(h * length, (h + 1) * length)
                    rows = slice(h * HEAD_DIM, (h + 1) * HEAD_DIM)
                    piece = dot(kt_all[rows, there], ds_low[:, lanes])
                    if kb == 0:
                        dqt[rows, :] = piece
                    else:
                        dqt[rows, :] += piece
            dq[here, :] = (0.125 * jnp.transpose(dqt[...])).astype(bf16)
        for j in range(blocks):
            rows = pl.ds(pl.multiple_of((me ^ j) * length, length), length)
            out_refs[j][:, 0:part] = dq[rows, :]
            out_refs[j][:, part : 2 * part] = (0.125 * dk[rows, :]).astype(bf16)
            out_refs[j][:, 2 * part : 3 * part] = dv[rows, :].astype(bf16)

    spec = pl.BlockSpec((length, part), lambda i, d: (i, 0))
    return kernel_call(
        body,
        (2,),
        ids,
        [(a, spec) for a in (*queries, *keys, *values, *grads)]
        + [
            (ot, pl.BlockSpec((1, part, total), lambda i, d: (i, 0, 0))),
            (lse, pl.BlockSpec((1, blocks, heads * length), lambda i, d: (i, 0, 0))),
        ],
        [((tokens, 3 * part), bf16, pl.BlockSpec((length, 3 * part), lambda i, d: (i, 0)))]
        * blocks,
        [pltpu.VMEM((total, part), bf16)] * 4
        + [
            pltpu.VMEM((part, total), bf16),
            pltpu.VMEM((heads * length, part), bf16),
            pltpu.VMEM((heads * length, part), bf16),
            pltpu.VMEM((length, heads * length), bf16),
            pltpu.VMEM((length, heads * length), bf16),
            pltpu.VMEM((total, part), f32),
            pltpu.VMEM((total, part), f32),
            pltpu.VMEM((part, length), f32),
            pltpu.VMEM((total, part), bf16),
        ],
        flops=2 * 10 * heads * 10 * length * length * part,
        moved=10 << 20,
    )


def head_rows(weight, j):
    part = weight.shape[0] // lax.axis_size("seq")
    return (weight, pl.BlockSpec((part, weight.shape[1]), lambda i, d: (d[0] ^ j, 0)))


def attention_out(ids, rows, attended, weight, gain, slot, groups, capacity):
    tokens, width = rows.shape
    slots = groups * capacity
    blocks = len(attended)

    def body(ids_ref, x_ref, gain_ref, slot_ref, *refs):
        att, weights, refs = refs[:blocks], refs[blocks : 2 * blocks], refs[2 * blocks :]
        h_ref, send_refs = refs[0], refs[1:]
        hidden = x_ref[...].astype(f32)
        for j in range(blocks):
            hidden += dot(att[j][...], weights[j][...])
        h_ref[...] = hidden
        normed = (hidden * norm_scale(hidden) * gain_ref[...]).astype(bf16)
        pick = lax.broadcasted_iota(jnp.int32, (slots, tokens), 0) == slot_ref[...]
        laid = dot(jnp.where(pick, 1.0, 0.0).astype(bf16), normed)
        for k in range(groups):
            send_refs[k][...] = laid[k * capacity : (k + 1) * capacity].astype(bf16)

    out = kernel_call(
        body,
        (1,),
        ids,
        [(rows, None), (gain, None), (slot, None)]
        + [(a, None) for a in attended]
        + [head_rows(weight, j) for j in range(blocks)],
        [((tokens, width), f32, None)] + [((capacity, width), bf16, None)] * groups,
        flops=2 * tokens * width * width + 2 * slots * tokens * width,
        moved=9 << 20,
    )
    return out[0], out[1:]


def normal_parts(values):
    size = jnp.abs(values)
    near = 1.0 + 0.23164189 * size
    t = pl.reciprocal(near, approx=True)
    t = t * (2.0 - near * t)
    fall = jnp.exp2(values * values * -0.7213475204444817)
    tail = t * (
        0.127414796
        + t * (-0.142248368 + t * (0.7107068705 + t * (-0.7265760135 + t * 0.5307027145)))
    )
    tail = tail * fall
    below = jnp.where(values >= 0.0, 1.0 - tail, tail)
    return below, values * fall * 0.3989422804014327


def expert_grad_act(ids, grads, weight):
    groups = len(grads)
    capacity, width = grads[0].shape
    slots, hidden = groups * capacity, weight.shape[0]
    step = 512

    def body(ids_ref, *refs):
        g_refs, (w_ref, out_ref, rows) = refs[:groups], refs[groups:]

        @pl.when(pl.program_id(0) == 0)
        def _():
            for k in range(groups):
                rows[k * capacity : (k + 1) * capacity, :] = g_refs[k][...]

        out_ref[...] = dot(rows[...], w_ref[...], NT)

    return kernel_call(
        body,
        (hidden // step,),
        ids,
        [(g, None) for g in grads] + [(weight, pl.BlockSpec((step, width), lambda i, d: (i, 0)))],
        [((slots, hidden), f32, pl.BlockSpec((slots, step), lambda i, d: (0, i)))],
        [pltpu.VMEM((slots, width), bf16)],
        flops=2 * slots * hidden * width,
        moved=26 << 20,
    )[0]


def expert_main(ids, rows_in, grad_act, weight):
    groups = len(rows_in)
    capacity, width = rows_in[0].shape
    slots, hidden = groups * capacity, weight.shape[0]
    step, chunk = 512, 256

    def body(ids_ref, *refs):
        x_refs, (ga_ref, w_ref, act_ref, gp_ref), refs = (
            refs[:groups],
            refs[groups : groups + 4],
            refs[groups + 4 :],
        )
        out_refs, (rows, total) = refs[:groups], refs[groups:]
        here = pl.program_id(0)

        @pl.when(here == 0)
        def _():
            for k in range(groups):
                rows[k * capacity : (k + 1) * capacity, :] = x_refs[k][...]
            total[...] = jnp.zeros_like(total)

        for r in range(slots // chunk):
            part = slice(r * chunk, (r + 1) * chunk)
            pre = dot(rows[part, :], w_ref[...], NT)
            below, dense = normal_parts(pre)
            act_ref[part, :] = (pre * below).astype(bf16)
            grad_pre = (ga_ref[part, :] * (below + dense)).astype(bf16)
            gp_ref[part, :] = grad_pre
            total[part, :] += dot(grad_pre, w_ref[...])

        @pl.when(here == pl.num_programs(0) - 1)
        def _():
            for k in range(groups):
                out_refs[k][...] = total[k * capacity : (k + 1) * capacity, :].astype(bf16)

    wide = pl.BlockSpec((slots, step), lambda i, d: (0, i))
    out = kernel_call(
        body,
        (hidden // step,),
        ids,
        [(x, None) for x in rows_in]
        + [(grad_act, wide), (weight, pl.BlockSpec((step, width), lambda i, d: (i, 0)))],
        [((slots, hidden), bf16, wide)] * 2 + [((capacity, width), bf16, None)] * groups,
        [pltpu.VMEM((slots, width), bf16), pltpu.VMEM((slots, width), f32)],
        flops=4 * slots * hidden * width,
        moved=44 << 20,
    )
    return out[0], out[1], out[2:]


def block_result(ids, hidden, returned, column):
    tokens, width = hidden.shape
    groups, capacity = len(returned), returned[0].shape[0]

    def body(ids_ref, h_ref, c_ref, *refs):
        back, (out_ref, rows) = refs[:groups], refs[groups:]
        for k in range(groups):
            rows[k * capacity : (k + 1) * capacity, :] = back[k][...]
        pick = one_hot_columns(c_ref[...], groups * capacity)
        out_ref[...] = (h_ref[...] + dot(pick, rows[...])).astype(bf16)

    return kernel_call(
        body,
        (1,),
        ids,
        [(hidden, None), (column, None)] + [(a, None) for a in returned],
        [((tokens, width), bf16, None)],
        [pltpu.VMEM((groups * capacity, width), bf16)],
        flops=2 * groups * capacity * tokens * width,
        moved=5 << 20,
    )[0]


def norm_back(values, gain, grads):
    scale = norm_scale(values)
    scaled = grads * gain
    along = jnp.mean(values * scaled, axis=-1, keepdims=True)
    through = scale * scaled - values * (scale * scale * scale * along)
    return through, jnp.sum(grads * (values * scale), axis=0, keepdims=True)


def hidden_back(ids, hidden, cotangent, gain, returned, column, weight):
    tokens, width = hidden.shape
    groups, capacity = len(returned), returned[0].shape[0]
    blocks = lax.axis_size("seq")
    part = width // blocks

    def body(ids_ref, h_ref, c_ref, gain_ref, col_ref, *refs):
        back, weights, refs = refs[:groups], refs[groups : groups + blocks], refs[groups + blocks :]
        gh_ref, gb_ref, gain_out, refs = refs[0], refs[1], refs[2], refs[3:]
        out_refs, rows = refs[:blocks], refs[blocks]
        for k in range(groups):
            rows[k * capacity : (k + 1) * capacity, :] = back[k][...]
        pick = one_hot_columns(col_ref[...], groups * capacity)
        grads = dot(pick, rows[...])
        through, gain_grad = norm_back(h_ref[...], gain_ref[...], grads)
        grad_hidden = c_ref[...].astype(f32) + through
        gh_ref[...] = grad_hidden
        low = grad_hidden.astype(bf16)
        gb_ref[...] = low
        gain_out[...] = gain_grad
        for j in range(blocks):
            out_refs[j][...] = dot(low, weights[j][...], NT).astype(bf16)

    out = kernel_call(
        body,
        (1,),
        ids,
        [(hidden, None), (cotangent, None), (gain, None), (column, None)]
        + [(a, None) for a in returned]
        + [head_rows(weight, j) for j in range(blocks)],
        [((tokens, width), f32, None), ((tokens, width), bf16, None), ((1, width), f32, None)]
        + [((tokens, part), bf16, None)] * blocks,
        [pltpu.VMEM((groups * capacity, width), bf16)],
        flops=2 * groups * capacity * tokens * width + 2 * tokens * width * width,
        moved=11 << 20,
    )
    return out[0], out[1], out[2], out[3:]


def projection_back(ids, grads, weight):
    blocks = len(grads)
    tokens = grads[0].shape[0]
    width = weight.shape[0]
    part = grads[0].shape[1] // 3
    heads = width // part
    kinds = [f32 if j % 2 == 0 else bf16 for j in range(blocks)]

    def body(ids_ref, *refs):
        g_refs, w_refs, out_refs = refs[:blocks], refs[blocks : blocks + 3], refs[blocks + 3 :]
        for j in (1, 3, 2, 0):
            total = None
            for w in range(3):
                piece = dot(g_refs[j][:, w * part : (w + 1) * part], w_refs[w][...], NT)
                total = piece if total is None else total + piece
            out_refs[j][...] = total.astype(kinds[j])

    column = lambda which: pl.BlockSpec((width, part), lambda i, d: (0, d[0] + which * heads))
    return kernel_call(
        body,
        (1,),
        ids,
        [(g, None) for g in grads] + [(weight, column(w)) for w in range(3)],
        [((tokens, width), kind, None) for kind in kinds],
        flops=2 * blocks * tokens * width * 3 * part,
        moved=12 << 20,
    )


def projection_grad(ids, normed, grads, groups):
    blocks = len(grads)
    tokens, width = normed[0].shape
    columns = grads[0].shape[1]
    rows = width // groups

    def body(ids_ref, *refs):
        n_refs, g_refs, refs = refs[:blocks], refs[blocks : 2 * blocks], refs[2 * blocks :]
        out_refs, total = refs[:groups], refs[groups]
        me = ids_ref[1]
        for j in range(blocks):
            piece = dot(n_refs[j][...], g_refs[j][...], TN)
            if j == 0:
                total[...] = piece
            else:
                total[...] += piece
        for k in range(groups):
            here = pl.ds(pl.multiple_of((me ^ k) * rows, rows), rows)
            out_refs[k][...] = total[here, :].astype(bf16)

    return kernel_call(
        body,
        (1,),
        ids,
        [(a, None) for a in (*normed, *grads)],
        [((rows, columns), bf16, None)] * groups,
        [pltpu.VMEM((width, columns), f32)],
        flops=2 * blocks * tokens * width * columns,
        moved=10 << 20,
    )


def input_back(ids, rows, gain, grad_hidden, pieces):
    tokens, width = rows.shape

    def body(ids_ref, x_ref, gain_ref, gh_ref, a_ref, b_ref, c_ref, out_ref, gain_out):
        grads = a_ref[...] + b_ref[...].astype(f32) + c_ref[...].astype(f32)
        through, gain_grad = norm_back(x_ref[...].astype(f32), gain_ref[...], grads)
        out_ref[...] = gh_ref[...] + through
        gain_out[...] = gain_grad

    return kernel_call(
        body,
        (1,),
        ids,
        [(rows, None), (gain, None), (grad_hidden, None)] + [(a, None) for a in pieces],
        [((tokens, width), f32, None), ((1, width), f32, None)],
        flops=0,
        moved=10 << 20,
    )


def sum_over_seq(parts):
    near_1 = swap(parts[1].astype(bf16), "seq", 1)
    near_3 = swap(parts[3].astype(bf16), "seq", 1)
    far = (parts[2] + near_3.astype(f32)).astype(bf16)
    return parts[0], near_1, swap(far, "seq", 2)


def sum_over_expert(pieces):
    groups = len(pieces)
    total = pieces[0].astype(f32)
    for k in range(1, groups):
        total += swap(pieces[k], "expert", k).astype(f32)
    return total


def sum_everywhere(value):
    for axis in ("seq", "expert"):
        step = 1
        while step < lax.axis_size(axis):
            value = value + swap(value, axis, step)
            step *= 2
    return value


def shards(
    inputs,
    query_key_value_weight,
    output_weight,
    gain_attn,
    gain_ffn,
    w_up,
    w_down,
    expert_of,
    cotangent,
):
    groups = lax.axis_size("expert")
    blocks = lax.axis_size("seq")
    seq_count, local_len, width = inputs.shape
    tokens = seq_count * local_len
    capacity = max(2, 2 * tokens // groups)
    ids = jnp.stack([lax.axis_index("seq"), lax.axis_index("expert")]).astype(jnp.int32)
    gain_a, gain_f = gain_attn.reshape(1, width), gain_ffn.reshape(1, width)
    rows = inputs.reshape(tokens, width)
    cot = cotangent.reshape(tokens, width)

    rows_2 = swap(rows, "seq", 2)
    rows_1 = swap(rows, "seq", 1)
    rows_3 = swap(rows_2, "seq", 1)
    all_rows = [rows, rows_1, rows_2, rows_3]

    slot, column, send = route(ids, expert_of.reshape(1, tokens), cot, groups, capacity)
    grads_in = [send[0]] + [swap(send[k], "expert", k) for k in range(1, groups)]

    def all_units(weight, after):
        weight = weight[0]
        weight, _ = lax.optimization_barrier((weight, after))
        far = swap(weight, "seq", 2)
        return jnp.concatenate([weight, swap(weight, "seq", 1), far, swap(far, "seq", 1)], axis=0)

    down_all = all_units(w_down, rows_2)
    up_all = all_units(w_up, down_all)
    grad_act = expert_grad_act(ids, grads_in, down_all)

    projected = [project(ids, r, gain_a, query_key_value_weight) for r in all_rows]
    normed, queries, keys, values = (list(p) for p in zip(*projected))
    out, ot, lse = attention(ids, queries, keys, values)
    attended = [out[0]] + [swap(out[j], "seq", j) for j in range(1, blocks)]
    hidden, send = attention_out(
        ids, rows, attended, output_weight, gain_f, slot, groups, capacity
    )
    rows_in = [send[0]] + [swap(send[k], "expert", k) for k in range(1, groups)]

    activated, grad_pre, back = expert_main(ids, rows_in, grad_act, up_all)
    returned_grad = [back[0]] + [swap(back[k], "expert", k) for k in range(1, groups)]
    expert_out = dot(activated, down_all).astype(bf16)
    outs = [expert_out[k * capacity : (k + 1) * capacity] for k in range(groups)]
    returned = [outs[0]] + [swap(outs[k], "expert", k) for k in range(1, groups)]
    units = grad_pre.shape[1] // blocks
    rows_cat, grads_cat = jnp.concatenate(rows_in, axis=0), jnp.concatenate(grads_in, axis=0)

    def unit_grads(left, right):
        cuts = [left[:, j * units : (j + 1) * units] for j in range(blocks)]
        own, near, far = sum_over_seq([dot(c, right, TN) for c in cuts])
        return (own + near.astype(f32) + far.astype(f32))[None]

    up_grad = unit_grads(grad_pre, rows_cat)
    down_grad = unit_grads(activated, grads_cat)

    block_out = block_result(ids, hidden, returned, column)
    grad_hidden, low, ffn_gain_part, grad_att = hidden_back(
        ids, hidden, cot, gain_f, returned_grad, column, output_weight
    )
    grad_att = [grad_att[0]] + [swap(grad_att[j], "seq", j) for j in range(1, blocks)]
    own, near, far = sum_over_seq([dot(a, low, TN) for a in attended])
    out_part = own + near.astype(f32) + far.astype(f32)
    height = out_part.shape[0] // groups
    me = lax.axis_index("expert")
    out_piece = sum_over_expert(
        [
            lax.dynamic_slice_in_dim(out_part, (me ^ k) * height, height, 0).astype(bf16)
            for k in range(groups)
        ]
    ).astype(bf16)

    grad_proj = attention_back(ids, queries, keys, values, grad_att, ot, lse)
    grad_normed = sum_over_seq(projection_back(ids, grad_proj, query_key_value_weight))
    input_grad, attn_gain_part = input_back(ids, rows, gain_a, grad_hidden, grad_normed)
    qkv_piece = sum_over_expert(projection_grad(ids, normed, grad_proj, groups)).astype(bf16)

    part = width // blocks
    high = width // groups
    gathered = lax.all_gather(qkv_piece, ("expert", "seq"), axis=0, tiled=False)
    gathered = gathered.reshape(groups, blocks, high, 3, part).transpose(0, 2, 3, 1, 4)
    qkv_grad = gathered.reshape(width, 3 * width).astype(f32)
    gathered = lax.all_gather(out_piece, ("expert", "seq"), axis=0, tiled=False)
    gathered = gathered.reshape(groups, blocks, height, width).transpose(1, 0, 2, 3)
    out_grad = gathered.reshape(width, width).astype(f32)
    gains = sum_everywhere(jnp.concatenate([attn_gain_part, ffn_gain_part], axis=0))

    return (
        block_out.reshape(inputs.shape),
        input_grad.reshape(inputs.shape),
        qkv_grad,
        out_grad,
        gains[0],
        gains[1],
        up_grad,
        down_grad,
    )


def solution(mesh):
    tokens = P("expert", "seq", None)
    units = P("expert", "seq", None)
    in_specs = (tokens, P(), P(), P(), P(), units, units, P("expert", "seq"), tokens)
    out_specs = (tokens, tokens, P(), P(), P(), P(), units, units)
    return jax.shard_map(shards, mesh=mesh, in_specs=in_specs, out_specs=out_specs, check_vma=False)
```

```python
import jax
import jax.numpy as jnp
from jax import lax
from jax.experimental import pallas as pl
from jax.experimental.pallas import tpu as pltpu
from jax.sharding import PartitionSpec as P

HEAD_DIM = 64
EPSILON = 1e-06
SCORE_SCALE = 0.125 * 1.4426950408889634
bf16, f32 = jnp.bfloat16, jnp.float32

NN = (((1,), (0,)), ((), ()))
NT = (((1,), (1,)), ((), ()))
TN = (((0,), (0,)), ((), ()))


def dot(left, right, dims=NN):
    return lax.dot_general(left, right, dims, preferred_element_type=f32)


def sds(shape, dtype):
    return jax.ShapeDtypeStruct(shape, dtype)


def whole(shape):
    return pl.BlockSpec(shape, lambda *_: (0,) * len(shape))


def kernel_call(body, grid, ids, ins, outs, scratch=(), vmem=60, aliases=None):
    in_specs = [whole(a.shape) if sp is None else sp for a, sp in ins]
    out_specs = [whole(sh) if sp is None else sp for sh, _, sp in outs]
    return pl.pallas_call(
        body,
        grid_spec=pltpu.PrefetchScalarGridSpec(
            num_scalar_prefetch=1,
            grid=grid,
            in_specs=in_specs,
            out_specs=out_specs,
            scratch_shapes=list(scratch),
        ),
        out_shape=[sds(sh, dt) for sh, dt, _ in outs],
        input_output_aliases=aliases or {},
        compiler_params=pltpu.CompilerParams(
            vmem_limit_bytes=vmem << 20, dimension_semantics=("arbitrary",) * len(grid)
        ),
        cost_estimate=pl.CostEstimate(flops=1, bytes_accessed=1, transcendentals=0),
    )(ids, *[a for a, _ in ins])


def swap(value, axis, step):
    size = lax.axis_size(axis)
    return lax.ppermute(value, axis, [(i, i ^ step) for i in range(size)])


def norm_scale(values):
    return lax.rsqrt(jnp.mean(values * values, axis=-1, keepdims=True) + EPSILON)


def route(ids, routes, rows, groups, capacity):
    tokens, width = rows.shape
    slots = groups * capacity

    def body(ids_ref, routes_ref, rows_ref, slot_ref, column_ref, send_ref):
        route_row = routes_ref[...]
        named = lax.broadcasted_iota(jnp.int32, (groups, tokens), 0) == route_row
        ones = jnp.where(named, 1.0, 0.0)
        earlier = lax.broadcasted_iota(jnp.int32, (tokens, tokens), 0)
        later = lax.broadcasted_iota(jnp.int32, (tokens, tokens), 1)
        upto = jnp.where(earlier <= later, 1.0, 0.0)
        count = dot(ones, upto)
        place = jnp.sum(count * ones, axis=0, keepdims=True) - 1.0
        slot = route_row * capacity + place.astype(jnp.int32)
        slot_ref[...] = slot
        column_ref[...] = jnp.transpose(jnp.broadcast_to(slot.astype(f32), (128, tokens)))
        pick = lax.broadcasted_iota(jnp.int32, (slots, tokens), 0) == slot
        laid = dot(jnp.where(pick, 1.0, 0.0).astype(bf16), rows_ref[...])
        send_ref[...] = laid.astype(bf16)

    return kernel_call(
        body,
        (1,),
        ids,
        [(routes, None), (rows, None)],
        [
            ((1, tokens), jnp.int32, None),
            ((tokens, 128), f32, None),
            ((slots, width), bf16, None),
        ],
    )


def to_groups(rows):
    groups = lax.axis_size("expert")
    cut = rows.reshape(groups, rows.shape[0] // groups, rows.shape[1])
    return lax.all_to_all(cut, "expert", split_axis=0, concat_axis=0, tiled=True).reshape(rows.shape)


def one_hot_columns(column, slots):
    wide = jnp.concatenate([column] * (slots // 128), axis=1)
    lanes = lax.broadcasted_iota(jnp.int32, wide.shape, 1).astype(f32)
    return jnp.where(wide == lanes, 1.0, 0.0).astype(bf16)


def project(ids, rows, gain, weight):
    tokens, width = rows[0].shape
    part = width // lax.axis_size("seq")
    heads = width // part
    count = len(rows)

    def body(ids_ref, gain_ref, wq_ref, wk_ref, wv_ref, *refs):
        x_refs, refs = refs[:count], refs[count:]
        for x_ref, outs in zip(x_refs, (refs[4 * r : 4 * r + 4] for r in range(count))):
            values = x_ref[...].astype(f32)
            normed = (values * norm_scale(values) * gain_ref[...]).astype(bf16)
            outs[0][...] = normed
            for w_ref, out in zip((wq_ref, wk_ref, wv_ref), outs[1:]):
                out[...] = dot(normed, w_ref[...]).astype(bf16)

    half = tokens // 2
    column = lambda which: pl.BlockSpec((width, part), lambda i, d: (0, d[0] + which * heads))
    row_spec = lambda n: pl.BlockSpec((half, n), lambda i, d: (i, 0))
    out = kernel_call(
        body,
        (2,),
        ids,
        [(gain, None)] + [(weight, column(w)) for w in range(3)] + [(r, row_spec(width)) for r in rows],
        (
            [((tokens, width), bf16, row_spec(width))]
            + [((tokens, part), bf16, row_spec(part))] * 3
        )
        * count,
    )
    return [out[4 * r : 4 * r + 4] for r in range(count)]


def head_lanes(block, head):
    lanes = lax.broadcasted_iota(jnp.int32, block.shape, 1)
    inside = (lanes >= head * HEAD_DIM) & (lanes < (head + 1) * HEAD_DIM)
    return jnp.where(inside, block, jnp.zeros_like(block))


def fold_rows(values, how):
    return how(values.reshape(values.shape[0] // 8, 8, values.shape[1]), axis=0)


def attention(ids, queries, keys, values):
    blocks = len(queries)
    tokens, part = queries[0].shape
    length = tokens // 2
    heads = part // HEAD_DIM
    total = blocks * length

    def body(ids_ref, *refs):
        ins, refs = refs[: 3 * blocks], refs[3 * blocks :]
        out_refs, refs = refs[:blocks], refs[blocks:]
        ot_ref, lse_ref, q_all, k_all, vt_all, stacked, scores, result = refs
        me = ids_ref[0]
        for j in range(blocks):
            rows = pl.ds(pl.multiple_of((me ^ j) * length, length), length)
            q_all[rows, :] = ins[j][...]
            k_all[rows, :] = ins[blocks + j][...]
            vt_all[:, rows] = jnp.transpose(ins[2 * blocks + j][...].astype(f32)).astype(bf16)
        hidden = lax.broadcasted_iota(jnp.int32, (length, length), 0) > lax.broadcasted_iota(
            jnp.int32, (length, length), 1
        )
        for qa in range(blocks):
            here = slice(qa * length, (qa + 1) * length)
            q_block = q_all[here, :]
            for h in range(heads):
                stacked[h * length : (h + 1) * length, :] = head_lanes(q_block, h)
            for h in range(heads):
                lanes = slice(h * length, (h + 1) * length)
                most = None
                for kb in range(qa + 1):
                    there = slice(kb * length, (kb + 1) * length)
                    found = dot(k_all[there, :], stacked[lanes, :], NT)
                    if kb == qa:
                        found = jnp.where(hidden, -1e30, found)
                    scores[there, lanes] = found
                    top = fold_rows(found, jnp.max)
                    most = top if most is None else jnp.maximum(most, top)
                peak = jnp.max(most, axis=0, keepdims=True) * SCORE_SCALE
                summed, gathered = None, None
                for kb in range(qa + 1):
                    there = slice(kb * length, (kb + 1) * length)
                    raised = jnp.exp2(scores[there, lanes] * SCORE_SCALE - peak)
                    part_sum = fold_rows(raised, jnp.sum)
                    summed = part_sum if summed is None else summed + part_sum
                    piece = dot(
                        vt_all[h * HEAD_DIM : (h + 1) * HEAD_DIM, there], raised.astype(bf16)
                    )
                    gathered = piece if gathered is None else gathered + piece
                weight = jnp.sum(summed, axis=0, keepdims=True)
                ot_ref[0, h * HEAD_DIM : (h + 1) * HEAD_DIM, here] = gathered * (1.0 / weight)
                lse_ref[0, qa : qa + 1, lanes] = peak + jnp.log2(weight)
            result[here, :] = jnp.transpose(ot_ref[0, :, here]).astype(bf16)
        for j in range(blocks):
            rows = pl.ds(pl.multiple_of((me ^ j) * length, length), length)
            out_refs[j][...] = result[rows, :]

    spec = pl.BlockSpec((length, part), lambda i, d: (i, 0))
    out = kernel_call(
        body,
        (2,),
        ids,
        [(a, spec) for a in (*queries, *keys, *values)],
        [((tokens, part), bf16, spec)] * blocks
        + [
            ((2, part, total), f32, pl.BlockSpec((1, part, total), lambda i, d: (i, 0, 0))),
            (
                (2, blocks, heads * length),
                f32,
                pl.BlockSpec((1, blocks, heads * length), lambda i, d: (i, 0, 0)),
            ),
        ],
        [
            pltpu.VMEM((total, part), bf16),
            pltpu.VMEM((total, part), bf16),
            pltpu.VMEM((part, total), bf16),
            pltpu.VMEM((heads * length, part), bf16),
            pltpu.VMEM((total, heads * length), f32),
            pltpu.VMEM((total, part), bf16),
        ],
    )
    return out[:blocks], out[blocks], out[blocks + 1]


def attention_back(ids, queries, keys, values, grads, ot, lse):
    blocks = len(queries)
    tokens, part = queries[0].shape
    length = tokens // 2
    heads = part // HEAD_DIM
    total = blocks * length

    def body(ids_ref, *refs):
        ins, refs = refs[: 4 * blocks], refs[4 * blocks :]
        ot_ref, lse_ref, refs = refs[0], refs[1], refs[2:]
        out_refs, refs = refs[:blocks], refs[blocks:]
        q_all, k_all, v_all, g_all, kt_all, q_stack, g_stack, low, ds_low, dk, dv, dqt, dq = refs
        me = ids_ref[0]
        for j in range(blocks):
            rows = pl.ds(pl.multiple_of((me ^ j) * length, length), length)
            q_all[rows, :] = ins[j][...]
            k_all[rows, :] = ins[blocks + j][...]
            v_all[rows, :] = ins[2 * blocks + j][...]
            g_all[rows, :] = ins[3 * blocks + j][...]
            kt_all[:, rows] = jnp.transpose(ins[blocks + j][...].astype(f32)).astype(bf16)
        dk[...] = jnp.zeros_like(dk)
        dv[...] = jnp.zeros_like(dv)
        hidden = lax.broadcasted_iota(jnp.int32, (length, length), 0) > lax.broadcasted_iota(
            jnp.int32, (length, length), 1
        )
        for qa in range(blocks):
            here = slice(qa * length, (qa + 1) * length)
            q_block, g_block = q_all[here, :], g_all[here, :]
            for h in range(heads):
                lanes = slice(h * length, (h + 1) * length)
                q_stack[lanes, :] = head_lanes(q_block, h)
                g_stack[lanes, :] = head_lanes(g_block, h)
            product = jnp.transpose(g_block.astype(f32)) * ot_ref[0, :, here]
            totals = [
                jnp.sum(product[h * HEAD_DIM : (h + 1) * HEAD_DIM], axis=0, keepdims=True)
                for h in range(heads)
            ]
            for kb in range(qa + 1):
                there = slice(kb * length, (kb + 1) * length)
                for h in range(heads):
                    lanes = slice(h * length, (h + 1) * length)
                    found = dot(k_all[there, :], q_stack[lanes, :], NT)
                    if kb == qa:
                        found = jnp.where(hidden, -1e30, found)
                    probs = jnp.exp2(found * SCORE_SCALE - lse_ref[0, qa : qa + 1, lanes])
                    grad_probs = dot(v_all[there, :], g_stack[lanes, :], NT)
                    low[:, lanes] = probs.astype(bf16)
                    ds_low[:, lanes] = (probs * (grad_probs - totals[h])).astype(bf16)
                dv[there, :] += dot(low[...], g_stack[...])
                dk[there, :] += dot(ds_low[...], q_stack[...])
                for h in range(heads):
                    lanes = slice(h * length, (h + 1) * length)
                    rows = slice(h * HEAD_DIM, (h + 1) * HEAD_DIM)
                    piece = dot(kt_all[rows, there], ds_low[:, lanes])
                    if kb == 0:
                        dqt[rows, :] = piece
                    else:
                        dqt[rows, :] += piece
            dq[here, :] = (0.125 * jnp.transpose(dqt[...])).astype(bf16)
        for j in range(blocks):
            rows = pl.ds(pl.multiple_of((me ^ j) * length, length), length)
            out_refs[j][:, 0:part] = dq[rows, :]
            out_refs[j][:, part : 2 * part] = (0.125 * dk[rows, :]).astype(bf16)
            out_refs[j][:, 2 * part : 3 * part] = dv[rows, :].astype(bf16)

    spec = pl.BlockSpec((length, part), lambda i, d: (i, 0))
    return kernel_call(
        body,
        (2,),
        ids,
        [(a, spec) for a in (*queries, *keys, *values, *grads)]
        + [
            (ot, pl.BlockSpec((1, part, total), lambda i, d: (i, 0, 0))),
            (lse, pl.BlockSpec((1, blocks, heads * length), lambda i, d: (i, 0, 0))),
        ],
        [((tokens, 3 * part), bf16, pl.BlockSpec((length, 3 * part), lambda i, d: (i, 0)))]
        * blocks,
        [pltpu.VMEM((total, part), bf16)] * 4
        + [
            pltpu.VMEM((part, total), bf16),
            pltpu.VMEM((heads * length, part), bf16),
            pltpu.VMEM((heads * length, part), bf16),
            pltpu.VMEM((length, heads * length), bf16),
            pltpu.VMEM((length, heads * length), bf16),
            pltpu.VMEM((total, part), f32),
            pltpu.VMEM((total, part), f32),
            pltpu.VMEM((part, length), f32),
            pltpu.VMEM((total, part), bf16),
        ],
    )


def head_rows(weight, j):
    part = weight.shape[0] // lax.axis_size("seq")
    return (weight, pl.BlockSpec((part, weight.shape[1]), lambda i, d: (d[0] ^ j, 0)))


def attention_out(ids, rows, attended, weight, gain, slot, groups, capacity):
    tokens, width = rows.shape
    slots = groups * capacity
    blocks = len(attended)

    def body(ids_ref, x_ref, gain_ref, slot_ref, *refs):
        att, weights, (h_ref, send_ref) = refs[:blocks], refs[blocks : 2 * blocks], refs[2 * blocks :]
        hidden = x_ref[...].astype(f32)
        for j in range(blocks):
            hidden += dot(att[j][...], weights[j][...])
        h_ref[...] = hidden
        normed = (hidden * norm_scale(hidden) * gain_ref[...]).astype(bf16)
        pick = lax.broadcasted_iota(jnp.int32, (slots, tokens), 0) == slot_ref[...]
        laid = dot(jnp.where(pick, 1.0, 0.0).astype(bf16), normed)
        send_ref[...] = laid.astype(bf16)

    return kernel_call(
        body,
        (1,),
        ids,
        [(rows, None), (gain, None), (slot, None)]
        + [(a, None) for a in attended]
        + [head_rows(weight, j) for j in range(blocks)],
        [((tokens, width), f32, None), ((slots, width), bf16, None)],
    )


def normal_parts(values):
    below = 0.5 + 0.5 * lax.erf(values * 0.7071067811865476)
    fall = jnp.exp2(values * values * -0.7213475204444817)
    return below, values * fall * 0.3989422804014327


def unit_specs(weights, step):
    starts = [0]
    for w in weights:
        starts.append(starts[-1] + w.shape[0] // step)

    def spec(j):
        last = starts[j + 1] - starts[j] - 1
        return pl.BlockSpec(
            (step, weights[j].shape[1]), lambda i, d: (jnp.clip(i - starts[j], 0, last), 0)
        )

    return starts, [(w, spec(j)) for j, w in enumerate(weights)]


def take_units(refs, starts, held):
    here = pl.program_id(0)
    for j, ref in enumerate(refs):

        @pl.when((here >= starts[j]) & (here < starts[j + 1]))
        def _():
            held[...] = ref[...]


def expert_grad_act(ids, grads, weights):
    slots, width = grads.shape
    step = 512
    starts, units = unit_specs(weights, step)
    hidden = starts[-1] * step

    def body(ids_ref, g_ref, *refs):
        w_refs, (out_ref, held) = refs[:-2], refs[-2:]
        take_units(w_refs, starts, held)
        out_ref[...] = dot(g_ref[...], held[...], NT)

    return kernel_call(
        body,
        (hidden // step,),
        ids,
        [(grads, None)] + units,
        [((slots, hidden), f32, pl.BlockSpec((slots, step), lambda i, d: (0, i)))],
        [pltpu.VMEM((step, width), bf16)],
    )[0]


def expert_main(ids, rows_in, grad_act, weights):
    slots, width = rows_in.shape
    step, chunk = 512, 256
    starts, units = unit_specs(weights, step)
    hidden = starts[-1] * step

    def body(ids_ref, x_ref, ga_ref, *refs):
        w_refs, (act_ref, gp_ref, out_ref, total, held) = refs[:-5], refs[-5:]
        here = pl.program_id(0)
        take_units(w_refs, starts, held)

        @pl.when(here == 0)
        def _():
            total[...] = jnp.zeros_like(total)

        parts = [slice(r * chunk, (r + 1) * chunk) for r in range(slots // chunk)]
        pre, last = dot(x_ref[parts[0], :], held[...], NT), None
        for r, part in enumerate(parts):
            later = None
            if r + 1 < len(parts):
                later = dot(x_ref[parts[r + 1], :], held[...], NT)
            below, dense = normal_parts(pre)
            act_ref[part, :] = (pre * below).astype(bf16)
            grad_pre = (ga_ref[part, :] * (below + dense)).astype(bf16)
            gp_ref[part, :] = grad_pre
            if last is not None:
                total[parts[r - 1], :] += dot(last, held[...])
            pre, last = later, grad_pre
        total[parts[-1], :] += dot(last, held[...])

        @pl.when(here == pl.num_programs(0) - 1)
        def _():
            out_ref[...] = total[...].astype(bf16)

    wide = pl.BlockSpec((slots, step), lambda i, d: (0, i))
    return kernel_call(
        body,
        (hidden // step,),
        ids,
        [(rows_in, None), (grad_act, wide)] + units,
        [((slots, hidden), bf16, wide)] * 2 + [((slots, width), bf16, None)],
        [pltpu.VMEM((slots, width), f32), pltpu.VMEM((step, width), bf16)],
    )


def expert_out(ids, activated, weights):
    slots = activated.shape[0]
    width = weights[0].shape[1]
    step = 512
    starts, units = unit_specs(weights, step)

    def body(ids_ref, act_ref, *refs):
        w_refs, (out_ref, total, held) = refs[:-3], refs[-3:]
        here = pl.program_id(0)
        take_units(w_refs, starts, held)

        @pl.when(here == 0)
        def _():
            total[...] = jnp.zeros_like(total)

        total[...] += dot(act_ref[...], held[...])

        @pl.when(here == pl.num_programs(0) - 1)
        def _():
            out_ref[...] = total[...].astype(bf16)

    return kernel_call(
        body,
        (starts[-1],),
        ids,
        [(activated, pl.BlockSpec((slots, step), lambda i, d: (0, i)))] + units,
        [((slots, width), bf16, None)],
        [pltpu.VMEM((slots, width), f32), pltpu.VMEM((step, width), bf16)],
    )[0]


def unit_grads(ids, lefts, rights, j, adds, kind, cuts=None):
    slots, width = rights[0].shape
    units = lefts[0].shape[1] // lax.axis_size("seq")
    step = 256
    steps = units // step
    pairs = len(lefts)
    block = pl.BlockSpec((step, width), lambda i, d: (i, 0))
    upto = lambda c: pl.BlockSpec((step, width), lambda i, d: (jnp.minimum(i, c - 1), 0))
    beyond = lambda c: pl.BlockSpec((step, width), lambda i, d: (jnp.maximum(i - c, 0), 0))
    add_ins, splits = [], []
    for pair in adds:
        for a in pair:
            if isinstance(a, tuple):
                c = a[0].shape[0] // step
                add_ins += [(a[0], upto(c)), (a[1], beyond(c))]
                splits.append(c)
            else:
                add_ins.append((a, block))
                splits.append(0)
    more = len(adds[0])

    def body(ids_ref, *refs):
        l_refs, r_refs, refs = refs[:pairs], refs[pairs : 2 * pairs], refs[2 * pairs :]
        add_refs, out_refs = list(refs[: len(add_ins)]), refs[len(add_ins) :]
        here = pl.program_id(0)
        for p in range(pairs):
            total = dot(l_refs[p][...], r_refs[p][...], TN)
            for c in splits[p * more : (p + 1) * more]:
                if c:
                    one, two = add_refs.pop(0), add_refs.pop(0)
                    total += jnp.where(here < c, one[...], two[...]).astype(f32)
                else:
                    total += add_refs.pop(0)[...].astype(f32)
            if not cuts:
                out_refs[p][...] = total.astype(kind)
                continue

            @pl.when(here < cuts[p])
            def _():
                out_refs[2 * p][...] = total.astype(kind)

            @pl.when(here >= cuts[p])
            def _():
                out_refs[2 * p + 1][...] = total.astype(kind)

    outs = [((units, width), kind, block)] * pairs
    if cuts:
        outs = []
        for c in cuts:
            outs += [((c * step, width), kind, upto(c)), ((units - c * step, width), kind, beyond(c))]
    return kernel_call(
        body,
        (steps,),
        ids,
        [(left, pl.BlockSpec((slots, step), lambda i, d: (0, j * steps + i))) for left in lefts]
        + [(right, None) for right in rights]
        + add_ins,
        outs,
    )


def block_result(ids, hidden, returned, column):
    tokens, width = hidden.shape
    slots = returned.shape[0]

    def body(ids_ref, h_ref, c_ref, back_ref, out_ref):
        pick = one_hot_columns(c_ref[...], slots)
        out_ref[...] = (h_ref[...] + dot(pick, back_ref[...])).astype(bf16)

    return kernel_call(
        body,
        (1,),
        ids,
        [(hidden, None), (column, None), (returned, None)],
        [((tokens, width), bf16, None)],
    )[0]


def norm_back(values, gain, grads):
    scale = norm_scale(values)
    scaled = grads * gain
    along = jnp.mean(values * scaled, axis=-1, keepdims=True)
    through = scale * scaled - values * (scale * scale * scale * along)
    return through, jnp.sum(grads * (values * scale), axis=0, keepdims=True)


def hidden_back(ids, hidden, cotangent, gain, returned, column, weight, attended):
    tokens, width = hidden.shape
    slots = returned.shape[0]
    blocks = lax.axis_size("seq")
    part = width // blocks
    kinds = [f32 if j % 2 == 0 else bf16 for j in range(blocks)]

    def body(ids_ref, h_ref, c_ref, gain_ref, col_ref, back_ref, *refs):
        weights, att, refs = refs[:blocks], refs[blocks : 2 * blocks], refs[2 * blocks :]
        (gh_ref, gain_out), att_refs, grad_refs = refs[:2], refs[2 : 2 + blocks], refs[2 + blocks :]
        pick = one_hot_columns(col_ref[...], slots)
        grads = dot(pick, back_ref[...])
        through, gain_grad = norm_back(h_ref[...], gain_ref[...], grads)
        grad_hidden = c_ref[...].astype(f32) + through
        gh_ref[...] = grad_hidden
        low = grad_hidden.astype(bf16)
        gain_out[...] = gain_grad
        for j in range(blocks):
            att_refs[j][...] = dot(low, weights[j][...], NT).astype(bf16)
        for j in range(blocks):
            grad_refs[j][...] = dot(att[j][...], low, TN).astype(kinds[j])

    out = kernel_call(
        body,
        (1,),
        ids,
        [(hidden, None), (cotangent, None), (gain, None), (column, None), (returned, None)]
        + [head_rows(weight, j) for j in range(blocks)]
        + [(a, None) for a in attended],
        [((tokens, width), f32, None), ((1, width), f32, None)]
        + [((tokens, part), bf16, None)] * blocks
        + [((part, width), kind, None) for kind in kinds],
    )
    return out[0], out[1], out[2 : 2 + blocks], out[2 + blocks :]


def projection_back(ids, grads, weight):
    blocks = len(grads)
    tokens = grads[0].shape[0]
    width = weight.shape[0]
    part = grads[0].shape[1] // 3
    heads = width // part
    kinds = [f32 if j % 2 == 0 else bf16 for j in range(blocks)]

    def body(ids_ref, *refs):
        g_refs, w_refs, out_refs = refs[:blocks], refs[blocks : blocks + 3], refs[blocks + 3 :]
        for j in (1, 3, 2, 0):
            total = None
            for w in range(3):
                piece = dot(g_refs[j][:, w * part : (w + 1) * part], w_refs[w][...], NT)
                total = piece if total is None else total + piece
            out_refs[j][...] = total.astype(kinds[j])

    column = lambda which: pl.BlockSpec((width, part), lambda i, d: (0, d[0] + which * heads))
    return kernel_call(
        body,
        (1,),
        ids,
        [(g, None) for g in grads] + [(weight, column(w)) for w in range(3)],
        [((tokens, width), kind, None) for kind in kinds],
    )


def projection_grad(ids, normed, grads, groups):
    blocks = len(normed)
    tokens, columns = grads[0].shape
    width = normed[0].shape[1]
    step, height = 256, width // groups
    pairs = step // height // 2

    def body(ids_ref, *refs):
        n_refs, g_refs = refs[:blocks], refs[blocks : 2 * blocks]
        kept_ref, sent_ref, held = refs[2 * blocks :]
        total = dot(n_refs[0][...], g_refs[0][...], TN)
        for j in range(1, blocks):
            total += dot(n_refs[j][...], g_refs[j][...], TN)
        held[...] = total
        odd = ids_ref[1] % 2
        for b in range(pairs):
            kept = pl.multiple_of(2 * b * height + odd * height, 8)
            sent = pl.multiple_of((2 * b + 1) * height - odd * height, 8)
            kept_ref[b] = held[pl.ds(kept, height), :]
            sent_ref[b] = held[pl.ds(sent, height), :].astype(bf16)

    block = pl.BlockSpec((pairs, height, columns), lambda i, d: (i, 0, 0))
    return kernel_call(
        body,
        (width // step,),
        ids,
        [(n, pl.BlockSpec((tokens, step), lambda i, d: (0, i))) for n in normed]
        + [(g, None) for g in grads],
        [((groups // 2, height, columns), f32, block), ((groups // 2, height, columns), bf16, block)],
        [pltpu.VMEM((step, columns), f32)],
    )


def sum_groups(ids, pieces, times, first):
    groups, rows, width = pieces.shape
    widths = [first, width - first] if first < width else [width]

    def body(ids_ref, in_ref, *out_refs):
        total = in_ref[0].astype(f32)
        for k in range(1, groups):
            total += in_ref[k].astype(f32)
        low = total.astype(bf16)
        for k in range(times):
            out_refs[0][k] = low[:, :first]
            if first < width:
                out_refs[1][k] = low[:, first:]

    return kernel_call(
        body,
        (1,),
        ids,
        [(pieces, None)],
        [((times, rows, w), bf16, None) for w in widths],
    )


def across(value, alike=False):
    size = lax.axis_size("expert")
    sets = [list(range(p, size, 2)) for p in range(2)] if alike else None
    return lax.all_to_all(
        value, "expert", split_axis=0, concat_axis=0, tiled=True, axis_index_groups=sets
    )


def after(value, *earlier):
    return lax.optimization_barrier((value, *earlier))[0]


def after_all(values, *earlier):
    return lax.optimization_barrier((*values, *earlier))[: len(values)]


def spread_over_seq(value):
    far = swap(value, "seq", 2)
    return [value, swap(value, "seq", 1), far, swap(far, "seq", 1)]


def widen_columns(ids, pieces, first, total, out=None):
    blocks = len(pieces)
    rows, columns = pieces[0].shape
    part = total // 3 // blocks
    count = columns // part
    step = 256

    def body(ids_ref, *refs):
        me = ids_ref[0]
        for j in range(blocks):
            at = pl.multiple_of((me ^ j) * part, part)
            refs[-1][:, pl.ds(at, part)] = refs[j][...].astype(f32)

    spec = pl.BlockSpec((step, part * blocks), lambda i, w, d: (i, first + w))
    ins = [(p, pl.BlockSpec((step, part), lambda i, w, d: (i, w))) for p in pieces]
    aliases = {}
    if out is not None:
        ins.append((out, pl.BlockSpec(memory_space=pl.ANY)))
        aliases = {len(ins): 0}
    return kernel_call(
        body,
        (rows // step, count),
        ids,
        ins,
        [((rows, total), f32, spec)],
        aliases=aliases,
    )[0]


def widen_rows(ids, pieces):
    blocks = len(pieces)
    rows, columns = pieces[0].shape

    def body(ids_ref, *refs):
        me = ids_ref[0]
        for j in range(blocks):
            at = pl.multiple_of((me ^ j) * rows, rows)
            refs[blocks][pl.ds(at, rows), :] = refs[j][...].astype(f32)

    return kernel_call(
        body,
        (1,),
        ids,
        [(p, None) for p in pieces],
        [((rows * blocks, columns), f32, None)],
    )[0]


def input_back(ids, rows, gain, grad_hidden, pieces):
    tokens, width = rows.shape

    def body(ids_ref, x_ref, gain_ref, gh_ref, a_ref, b_ref, c_ref, out_ref, gain_out):
        grads = a_ref[...] + b_ref[...].astype(f32) + c_ref[...].astype(f32)
        through, gain_grad = norm_back(x_ref[...].astype(f32), gain_ref[...], grads)
        out_ref[...] = gh_ref[...] + through
        gain_out[...] = gain_grad

    return kernel_call(
        body,
        (1,),
        ids,
        [(rows, None), (gain, None), (grad_hidden, None)] + [(a, None) for a in pieces],
        [((tokens, width), f32, None), ((1, width), f32, None)],
    )


def sum_along(value, axis):
    step = 1
    while step < lax.axis_size(axis):
        value = value + swap(value, axis, step)
        step *= 2
    return value


def shards(
    inputs,
    query_key_value_weight,
    output_weight,
    gain_attn,
    gain_ffn,
    w_up,
    w_down,
    expert_of,
    cotangent,
):
    groups = lax.axis_size("expert")
    blocks = lax.axis_size("seq")
    seq_count, local_len, width = inputs.shape
    tokens = seq_count * local_len
    capacity = max(2, 2 * tokens // groups)
    ids = jnp.stack([lax.axis_index("seq"), lax.axis_index("expert")]).astype(jnp.int32)
    gain_a, gain_f = gain_attn.reshape(1, width), gain_ffn.reshape(1, width)
    rows = inputs.reshape(tokens, width)
    cot = cotangent.reshape(tokens, width)

    down, up = w_down[0], w_up[0]
    rows_1 = swap(rows, "seq", 1)
    split = 5 * tokens // 8
    far_0, far_1 = swap(rows[:split], "seq", 2), swap(rows[split:], "seq", 2)
    down_near, up_near = swap(down, "seq", 1), swap(up, "seq", 1)
    first = project(ids, (rows, rows_1), gain_a, query_key_value_weight)
    slot, column, send = route(
        ids, expert_of.reshape(1, tokens), after(cot, first[0][0]), groups, capacity
    )
    send = after(send, far_0, down_near, up_near)
    rows_2 = after(jnp.concatenate([far_0, far_1], axis=0), send)
    grads_in = to_groups(send)
    rows_3 = swap(rows_2, "seq", 1)

    cut = up.shape[0] // 2
    up_far = swap(after(up[:cut], rows_2), "seq", 2)
    second = project(ids, (rows_2, rows_3), gain_a, query_key_value_weight)
    normed, queries, keys, values = (list(p) for p in zip(*first, *second))
    out, ot, lse = attention(ids, queries, keys, values)
    out = lax.optimization_barrier((*out, up_far))[:blocks]
    attended = [out[0]] + [swap(out[j], "seq", j) for j in range(1, blocks)]
    down_far = swap(after(down, *attended), "seq", 2)
    up_more = swap(after(up[cut:], *attended), "seq", 2)
    hidden, send = attention_out(
        ids, rows, attended, output_weight, gain_f, slot, groups, capacity
    )
    up_near_far = swap(after(up_far, send), "seq", 1)
    down_all = [down, down_near, down_far, swap(down_far, "seq", 1)]

    rows_in = to_groups(after(send, grads_in))
    grad_act = expert_grad_act(ids, grads_in, down_all)
    up_more = after(up_more, grad_act)
    up_all = [up, up_near, up_far, up_more, up_near_far, swap(up_more, "seq", 1)]
    activated, grad_pre, back = expert_main(ids, rows_in, grad_act, up_all)
    returned_grad = to_groups(back)
    left, right = (grad_pre, activated), (rows_in, grads_in)
    none = ((), ())
    near_3 = [swap(p, "seq", 1) for p in unit_grads(ids, left, right, 3, none, bf16)]
    near_1 = [swap(p, "seq", 1) for p in unit_grads(ids, left, right, 1, none, bf16)]
    up_0, up_1, down_0, down_1 = unit_grads(
        ids, left, right, 2, [(p,) for p in near_3], bf16, (1, 2)
    )
    up_0 = swap(up_0, "seq", 2)
    result = expert_out(ids, after(activated, down_0), down_all)

    returned_grad = after(returned_grad, result, up_0, *near_1)
    returned = to_groups(after(result, returned_grad))
    grad_hidden, ffn_gain_part, grad_att, out_parts = hidden_back(
        ids, hidden, cot, gain_f, returned_grad, column, output_weight, attended
    )
    grad_att = [grad_att[0]] + [swap(grad_att[j], "seq", j) for j in range(1, blocks)]
    near_out = [swap(after(out_parts[j], grad_att[1]), "seq", 1) for j in (1, 3)]
    far_out = (out_parts[2] + near_out[1].astype(f32)).astype(bf16)
    far_out = swap(after(far_out, *grad_att), "seq", 2)
    up_1 = swap(after(up_1, *grad_att), "seq", 2)
    down_0 = swap(after(down_0, *grad_att), "seq", 2)
    grad_proj = attention_back(ids, queries, keys, values, grad_att, ot, lse)
    grad_proj = after_all(grad_proj, far_out)

    kept, sent = projection_grad(ids, normed, grad_proj, groups)
    other = swap(sent, "expert", 1)
    out_part = (out_parts[0] + near_out[0].astype(f32) + far_out.astype(f32)).astype(bf16)
    height = out_part.shape[0] // groups
    out_own = across(after(out_part, returned, sent).reshape(groups, height, width))
    pieces = projection_back(ids, after_all(grad_proj, sent), query_key_value_weight)
    near = [swap(pieces[j], "seq", 1) for j in (1, 3)]
    far_rows = (pieces[2] + near[1].astype(f32)).astype(bf16)
    block_out = block_result(ids, hidden, after(returned, far_rows), column)
    out_own = after(out_own, up_1, far_rows, block_out)
    summed = across(after((kept + other.astype(f32)).astype(bf16), out_own), alike=True)
    far_arrived = swap(far_rows, "seq", 2)
    down_1 = swap(after(down_1, far_rows, down_0), "seq", 2)
    up_left = after(grad_pre, out_own)
    up_grad = unit_grads(ids, [up_left], [rows_in], 0, [(near_1[0], (up_0, up_1))], f32)[0]
    out_own = sum_groups(ids, out_own, groups, width)[0]
    summed = after(summed, out_own, up_grad)
    part = width // blocks
    first, rest = sum_groups(ids, summed, groups, part)
    rest_own = across(after(rest, far_arrived)).reshape(width, 2 * part)

    input_grad, attn_gain_part = input_back(
        ids, rows, gain_a, grad_hidden, (pieces[0], near[0], far_arrived)
    )
    gains = sum_along(jnp.concatenate([attn_gain_part, ffn_gain_part], axis=0), "seq")
    rest_own = after(rest_own, input_grad, gains)
    first_own = across(after(first, rest_own)).reshape(width, part)
    rest_all = spread_over_seq(rest_own)
    down_left = after(activated, rest)
    down_grad = unit_grads(ids, [down_left], [grads_in], 0, [(near_1[1], (down_0, down_1))], f32)[0]
    gains = gains + swap(after(gains, rest_own), "expert", 1)
    first_own = after(first_own, gains)
    first_all = spread_over_seq(first_own)
    qkv_grad = widen_columns(ids, rest_all, 1, 3 * width)
    out_own = across(after(out_own, first_own)).reshape(out_part.shape)
    out_own = after(out_own, qkv_grad, down_grad)
    step = groups // 2
    while step > 1:
        gains = gains + swap(gains, "expert", step)
        step //= 2
    out_all = spread_over_seq(out_own)
    qkv_grad = widen_columns(ids, first_all, 0, 3 * width, qkv_grad)
    out_grad = widen_rows(ids, after_all(out_all, qkv_grad))

    return (
        block_out.reshape(inputs.shape),
        input_grad.reshape(inputs.shape),
        qkv_grad,
        out_grad,
        gains[0],
        gains[1],
        up_grad[None],
        down_grad[None],
    )


def solution(mesh):
    tokens = P("expert", "seq", None)
    units = P("expert", "seq", None)
    in_specs = (tokens, P(), P(), P(), P(), units, units, P("expert", "seq"), tokens)
    out_specs = (tokens, tokens, P(), P(), P(), P(), units, units)
    return jax.shard_map(shards, mesh=mesh, in_specs=in_specs, out_specs=out_specs, check_vma=False)
```

```python
import jax
import jax.numpy as jnp
from jax import lax
from jax.experimental import pallas as pl
from jax.experimental.pallas import tpu as pltpu
from jax.sharding import PartitionSpec as P

HEAD_DIM = 64
EPSILON = 1e-06
SCORE_SCALE = 0.125 * 1.4426950408889634
bf16, f32 = jnp.bfloat16, jnp.float32

NN = (((1,), (0,)), ((), ()))
NT = (((1,), (1,)), ((), ()))
TN = (((0,), (0,)), ((), ()))


def dot(left, right, dims=NN):
    return lax.dot_general(left, right, dims, preferred_element_type=f32)


def sds(shape, dtype):
    return jax.ShapeDtypeStruct(shape, dtype)


def whole(shape):
    return pl.BlockSpec(shape, lambda *_: (0,) * len(shape))


def kernel_call(body, grid, ids, ins, outs, scratch=(), vmem=60, aliases=None):
    in_specs = [whole(a.shape) if sp is None else sp for a, sp in ins]
    out_specs = [whole(sh) if sp is None else sp for sh, _, sp in outs]
    return pl.pallas_call(
        body,
        grid_spec=pltpu.PrefetchScalarGridSpec(
            num_scalar_prefetch=1,
            grid=grid,
            in_specs=in_specs,
            out_specs=out_specs,
            scratch_shapes=list(scratch),
        ),
        out_shape=[sds(sh, dt) for sh, dt, _ in outs],
        input_output_aliases=aliases or {},
        compiler_params=pltpu.CompilerParams(
            vmem_limit_bytes=vmem << 20, dimension_semantics=("arbitrary",) * len(grid)
        ),
        cost_estimate=pl.CostEstimate(flops=1, bytes_accessed=1, transcendentals=0),
    )(ids, *[a for a, _ in ins])


def swap(value, axis, step):
    size = lax.axis_size(axis)
    return lax.ppermute(value, axis, [(i, i ^ step) for i in range(size)])


def norm_scale(values):
    return lax.rsqrt(jnp.mean(values * values, axis=-1, keepdims=True) + EPSILON)


def route(ids, routes, rows, groups, capacity):
    tokens, width = rows.shape
    slots = groups * capacity

    def body(ids_ref, routes_ref, rows_ref, slot_ref, column_ref, send_ref):
        route_row = routes_ref[...]
        named = lax.broadcasted_iota(jnp.int32, (groups, tokens), 0) == route_row
        ones = jnp.where(named, 1.0, 0.0)
        earlier = lax.broadcasted_iota(jnp.int32, (tokens, tokens), 0)
        later = lax.broadcasted_iota(jnp.int32, (tokens, tokens), 1)
        upto = jnp.where(earlier <= later, 1.0, 0.0)
        count = dot(ones, upto)
        place = jnp.sum(count * ones, axis=0, keepdims=True) - 1.0
        slot = route_row * capacity + place.astype(jnp.int32)
        slot_ref[...] = slot
        column_ref[...] = jnp.transpose(jnp.broadcast_to(slot.astype(f32), (128, tokens)))
        pick = lax.broadcasted_iota(jnp.int32, (slots, tokens), 0) == slot
        laid = dot(jnp.where(pick, 1.0, 0.0).astype(bf16), rows_ref[...])
        send_ref[...] = laid.astype(bf16)

    return kernel_call(
        body,
        (1,),
        ids,
        [(routes, None), (rows, None)],
        [
            ((1, tokens), jnp.int32, None),
            ((tokens, 128), f32, None),
            ((slots, width), bf16, None),
        ],
    )


def to_groups(rows):
    groups = lax.axis_size("expert")
    cut = rows.reshape(groups, rows.shape[0] // groups, rows.shape[1])
    return lax.all_to_all(cut, "expert", split_axis=0, concat_axis=0, tiled=True).reshape(rows.shape)


def one_hot_columns(column, slots):
    wide = jnp.concatenate([column] * (slots // 128), axis=1)
    lanes = lax.broadcasted_iota(jnp.int32, wide.shape, 1).astype(f32)
    return jnp.where(wide == lanes, 1.0, 0.0).astype(bf16)


def project(ids, rows, gain, weight):
    tokens, width = rows[0].shape
    part = width // lax.axis_size("seq")
    heads = width // part
    count = len(rows)

    def body(ids_ref, gain_ref, wq_ref, wk_ref, wv_ref, *refs):
        x_refs, refs = refs[:count], refs[count:]
        for x_ref, outs in zip(x_refs, (refs[4 * r : 4 * r + 4] for r in range(count))):
            values = x_ref[...].astype(f32)
            normed = (values * norm_scale(values) * gain_ref[...]).astype(bf16)
            outs[0][...] = normed
            for w_ref, out in zip((wq_ref, wk_ref, wv_ref), outs[1:]):
                out[...] = dot(normed, w_ref[...]).astype(bf16)

    half = tokens // 2
    column = lambda which: pl.BlockSpec((width, part), lambda i, d: (0, d[0] + which * heads))
    row_spec = lambda n: pl.BlockSpec((half, n), lambda i, d: (i, 0))
    out = kernel_call(
        body,
        (2,),
        ids,
        [(gain, None)] + [(weight, column(w)) for w in range(3)] + [(r, row_spec(width)) for r in rows],
        (
            [((tokens, width), bf16, row_spec(width))]
            + [((tokens, part), bf16, row_spec(part))] * 3
        )
        * count,
    )
    return [out[4 * r : 4 * r + 4] for r in range(count)]


def head_lanes(block, head):
    lanes = lax.broadcasted_iota(jnp.int32, block.shape, 1)
    inside = (lanes >= head * HEAD_DIM) & (lanes < (head + 1) * HEAD_DIM)
    return jnp.where(inside, block, jnp.zeros_like(block))


def fold_rows(values, how):
    return how(values.reshape(values.shape[0] // 8, 8, values.shape[1]), axis=0)


def attention(ids, queries, keys, values):
    blocks = len(queries)
    tokens, part = queries[0].shape
    length = tokens // 2
    heads = part // HEAD_DIM
    total = blocks * length

    def body(ids_ref, *refs):
        ins, refs = refs[: 3 * blocks], refs[3 * blocks :]
        out_refs, refs = refs[:blocks], refs[blocks:]
        ot_ref, lse_ref, q_all, k_all, vt_all, stacked, scores, result = refs
        me = ids_ref[0]
        for j in range(blocks):
            rows = pl.ds(pl.multiple_of((me ^ j) * length, length), length)
            q_all[rows, :] = ins[j][...]
            k_all[rows, :] = ins[blocks + j][...]
            vt_all[:, rows] = jnp.transpose(ins[2 * blocks + j][...].astype(f32)).astype(bf16)
        hidden = lax.broadcasted_iota(jnp.int32, (length, length), 0) > lax.broadcasted_iota(
            jnp.int32, (length, length), 1
        )
        for qa in range(blocks):
            here = slice(qa * length, (qa + 1) * length)
            q_block = q_all[here, :]
            for h in range(heads):
                stacked[h * length : (h + 1) * length, :] = head_lanes(q_block, h)
            for h in range(heads):
                lanes = slice(h * length, (h + 1) * length)
                most = None
                for kb in range(qa + 1):
                    there = slice(kb * length, (kb + 1) * length)
                    found = dot(k_all[there, :], stacked[lanes, :], NT)
                    if kb == qa:
                        found = jnp.where(hidden, -1e30, found)
                    scores[there, lanes] = found
                    top = fold_rows(found, jnp.max)
                    most = top if most is None else jnp.maximum(most, top)
                peak = jnp.max(most, axis=0, keepdims=True) * SCORE_SCALE
                summed, gathered = None, None
                for kb in range(qa + 1):
                    there = slice(kb * length, (kb + 1) * length)
                    raised = jnp.exp2(scores[there, lanes] * SCORE_SCALE - peak)
                    part_sum = fold_rows(raised, jnp.sum)
                    summed = part_sum if summed is None else summed + part_sum
                    piece = dot(
                        vt_all[h * HEAD_DIM : (h + 1) * HEAD_DIM, there], raised.astype(bf16)
                    )
                    gathered = piece if gathered is None else gathered + piece
                weight = jnp.sum(summed, axis=0, keepdims=True)
                ot_ref[0, h * HEAD_DIM : (h + 1) * HEAD_DIM, here] = gathered * (1.0 / weight)
                lse_ref[0, qa : qa + 1, lanes] = peak + jnp.log2(weight)
            result[here, :] = jnp.transpose(ot_ref[0, :, here]).astype(bf16)
        for j in range(blocks):
            rows = pl.ds(pl.multiple_of((me ^ j) * length, length), length)
            out_refs[j][...] = result[rows, :]

    spec = pl.BlockSpec((length, part), lambda i, d: (i, 0))
    out = kernel_call(
        body,
        (2,),
        ids,
        [(a, spec) for a in (*queries, *keys, *values)],
        [((tokens, part), bf16, spec)] * blocks
        + [
            ((2, part, total), f32, pl.BlockSpec((1, part, total), lambda i, d: (i, 0, 0))),
            (
                (2, blocks, heads * length),
                f32,
                pl.BlockSpec((1, blocks, heads * length), lambda i, d: (i, 0, 0)),
            ),
        ],
        [
            pltpu.VMEM((total, part), bf16),
            pltpu.VMEM((total, part), bf16),
            pltpu.VMEM((part, total), bf16),
            pltpu.VMEM((heads * length, part), bf16),
            pltpu.VMEM((total, heads * length), f32),
            pltpu.VMEM((total, part), bf16),
        ],
    )
    return out[:blocks], out[blocks], out[blocks + 1]


def attention_back(ids, queries, keys, values, grads, ot, lse):
    blocks = len(queries)
    tokens, part = queries[0].shape
    length = tokens // 2
    heads = part // HEAD_DIM
    total = blocks * length

    def body(ids_ref, *refs):
        ins, refs = refs[: 4 * blocks], refs[4 * blocks :]
        ot_ref, lse_ref, refs = refs[0], refs[1], refs[2:]
        out_refs, refs = refs[:blocks], refs[blocks:]
        q_all, k_all, v_all, g_all, kt_all, q_stack, g_stack, low, ds_low, dk, dv, dqt, dq = refs
        me = ids_ref[0]
        for j in range(blocks):
            rows = pl.ds(pl.multiple_of((me ^ j) * length, length), length)
            q_all[rows, :] = ins[j][...]
            k_all[rows, :] = ins[blocks + j][...]
            v_all[rows, :] = ins[2 * blocks + j][...]
            g_all[rows, :] = ins[3 * blocks + j][...]
            kt_all[:, rows] = jnp.transpose(ins[blocks + j][...].astype(f32)).astype(bf16)
        dk[...] = jnp.zeros_like(dk)
        dv[...] = jnp.zeros_like(dv)
        hidden = lax.broadcasted_iota(jnp.int32, (length, length), 0) > lax.broadcasted_iota(
            jnp.int32, (length, length), 1
        )
        for qa in range(blocks):
            here = slice(qa * length, (qa + 1) * length)
            q_block, g_block = q_all[here, :], g_all[here, :]
            for h in range(heads):
                lanes = slice(h * length, (h + 1) * length)
                q_stack[lanes, :] = head_lanes(q_block, h)
                g_stack[lanes, :] = head_lanes(g_block, h)
            product = jnp.transpose(g_block.astype(f32)) * ot_ref[0, :, here]
            totals = [
                jnp.sum(product[h * HEAD_DIM : (h + 1) * HEAD_DIM], axis=0, keepdims=True)
                for h in range(heads)
            ]
            for kb in range(qa + 1):
                there = slice(kb * length, (kb + 1) * length)
                for h in range(heads):
                    lanes = slice(h * length, (h + 1) * length)
                    found = dot(k_all[there, :], q_stack[lanes, :], NT)
                    if kb == qa:
                        found = jnp.where(hidden, -1e30, found)
                    probs = jnp.exp2(found * SCORE_SCALE - lse_ref[0, qa : qa + 1, lanes])
                    grad_probs = dot(v_all[there, :], g_stack[lanes, :], NT)
                    low[:, lanes] = probs.astype(bf16)
                    ds_low[:, lanes] = (probs * (grad_probs - totals[h])).astype(bf16)
                dv[there, :] += dot(low[...], g_stack[...])
                dk[there, :] += dot(ds_low[...], q_stack[...])
                for h in range(heads):
                    lanes = slice(h * length, (h + 1) * length)
                    rows = slice(h * HEAD_DIM, (h + 1) * HEAD_DIM)
                    piece = dot(kt_all[rows, there], ds_low[:, lanes])
                    if kb == 0:
                        dqt[rows, :] = piece
                    else:
                        dqt[rows, :] += piece
            dq[here, :] = (0.125 * jnp.transpose(dqt[...])).astype(bf16)
        for j in range(blocks):
            rows = pl.ds(pl.multiple_of((me ^ j) * length, length), length)
            out_refs[j][:, 0:part] = dq[rows, :]
            out_refs[j][:, part : 2 * part] = (0.125 * dk[rows, :]).astype(bf16)
            out_refs[j][:, 2 * part : 3 * part] = dv[rows, :].astype(bf16)

    spec = pl.BlockSpec((length, part), lambda i, d: (i, 0))
    return kernel_call(
        body,
        (2,),
        ids,
        [(a, spec) for a in (*queries, *keys, *values, *grads)]
        + [
            (ot, pl.BlockSpec((1, part, total), lambda i, d: (i, 0, 0))),
            (lse, pl.BlockSpec((1, blocks, heads * length), lambda i, d: (i, 0, 0))),
        ],
        [((tokens, 3 * part), bf16, pl.BlockSpec((length, 3 * part), lambda i, d: (i, 0)))]
        * blocks,
        [pltpu.VMEM((total, part), bf16)] * 4
        + [
            pltpu.VMEM((part, total), bf16),
            pltpu.VMEM((heads * length, part), bf16),
            pltpu.VMEM((heads * length, part), bf16),
            pltpu.VMEM((length, heads * length), bf16),
            pltpu.VMEM((length, heads * length), bf16),
            pltpu.VMEM((total, part), f32),
            pltpu.VMEM((total, part), f32),
            pltpu.VMEM((part, length), f32),
            pltpu.VMEM((total, part), bf16),
        ],
    )


def head_rows(weight, j):
    part = weight.shape[0] // lax.axis_size("seq")
    return (weight, pl.BlockSpec((part, weight.shape[1]), lambda i, d: (d[0] ^ j, 0)))


def attention_out(ids, rows, attended, weight, gain, slot, groups, capacity):
    tokens, width = rows.shape
    slots = groups * capacity
    blocks = len(attended)

    def body(ids_ref, x_ref, gain_ref, slot_ref, *refs):
        att, weights, (h_ref, send_ref) = refs[:blocks], refs[blocks : 2 * blocks], refs[2 * blocks :]
        hidden = x_ref[...].astype(f32)
        for j in range(blocks):
            hidden += dot(att[j][...], weights[j][...])
        h_ref[...] = hidden
        normed = (hidden * norm_scale(hidden) * gain_ref[...]).astype(bf16)
        pick = lax.broadcasted_iota(jnp.int32, (slots, tokens), 0) == slot_ref[...]
        laid = dot(jnp.where(pick, 1.0, 0.0).astype(bf16), normed)
        send_ref[...] = laid.astype(bf16)

    return kernel_call(
        body,
        (1,),
        ids,
        [(rows, None), (gain, None), (slot, None)]
        + [(a, None) for a in attended]
        + [head_rows(weight, j) for j in range(blocks)],
        [((tokens, width), f32, None), ((slots, width), bf16, None)],
    )


def normal_parts(values):
    below = 0.5 + 0.5 * lax.erf(values * 0.7071067811865476)
    fall = jnp.exp2(values * values * -0.7213475204444817)
    return below, values * fall * 0.3989422804014327


def unit_specs(weights, step):
    starts = [0]
    for w in weights:
        starts.append(starts[-1] + w.shape[0] // step)

    def spec(j):
        last = starts[j + 1] - starts[j] - 1
        return pl.BlockSpec(
            (step, weights[j].shape[1]), lambda i, d: (jnp.clip(i - starts[j], 0, last), 0)
        )

    return starts, [(w, spec(j)) for j, w in enumerate(weights)]


def take_units(refs, starts, held):
    here = pl.program_id(0)
    for j, ref in enumerate(refs):

        @pl.when((here >= starts[j]) & (here < starts[j + 1]))
        def _():
            held[...] = ref[...]


def expert_grad_act(ids, grads, weights):
    slots, width = grads.shape
    step = 512
    starts, units = unit_specs(weights, step)
    hidden = starts[-1] * step

    def body(ids_ref, g_ref, *refs):
        w_refs, (out_ref, held) = refs[:-2], refs[-2:]
        take_units(w_refs, starts, held)
        out_ref[...] = dot(g_ref[...], held[...], NT)

    return kernel_call(
        body,
        (hidden // step,),
        ids,
        [(grads, None)] + units,
        [((slots, hidden), f32, pl.BlockSpec((slots, step), lambda i, d: (0, i)))],
        [pltpu.VMEM((step, width), bf16)],
    )[0]


def expert_main(ids, rows_in, grad_act, weights):
    slots, width = rows_in.shape
    step, chunk = 512, 256
    starts, units = unit_specs(weights, step)
    hidden = starts[-1] * step

    def body(ids_ref, x_ref, ga_ref, *refs):
        w_refs, (act_ref, gp_ref, out_ref, total, held) = refs[:-5], refs[-5:]
        here = pl.program_id(0)
        take_units(w_refs, starts, held)

        @pl.when(here == 0)
        def _():
            total[...] = jnp.zeros_like(total)

        parts = [slice(r * chunk, (r + 1) * chunk) for r in range(slots // chunk)]
        pre, last = dot(x_ref[parts[0], :], held[...], NT), None
        for r, part in enumerate(parts):
            later = None
            if r + 1 < len(parts):
                later = dot(x_ref[parts[r + 1], :], held[...], NT)
            below, dense = normal_parts(pre)
            act_ref[part, :] = (pre * below).astype(bf16)
            grad_pre = (ga_ref[part, :] * (below + dense)).astype(bf16)
            gp_ref[part, :] = grad_pre
            if last is not None:
                total[parts[r - 1], :] += dot(last, held[...])
            pre, last = later, grad_pre
        total[parts[-1], :] += dot(last, held[...])

        @pl.when(here == pl.num_programs(0) - 1)
        def _():
            out_ref[...] = total[...].astype(bf16)

    wide = pl.BlockSpec((slots, step), lambda i, d: (0, i))
    return kernel_call(
        body,
        (hidden // step,),
        ids,
        [(rows_in, None), (grad_act, wide)] + units,
        [((slots, hidden), bf16, wide)] * 2 + [((slots, width), bf16, None)],
        [pltpu.VMEM((slots, width), f32), pltpu.VMEM((step, width), bf16)],
    )


def expert_out(ids, activated, weights):
    slots = activated.shape[0]
    width = weights[0].shape[1]
    step = 512
    starts, units = unit_specs(weights, step)

    def body(ids_ref, act_ref, *refs):
        w_refs, (out_ref, total, held) = refs[:-3], refs[-3:]
        here = pl.program_id(0)
        take_units(w_refs, starts, held)

        @pl.when(here == 0)
        def _():
            total[...] = jnp.zeros_like(total)

        total[...] += dot(act_ref[...], held[...])

        @pl.when(here == pl.num_programs(0) - 1)
        def _():
            out_ref[...] = total[...].astype(bf16)

    return kernel_call(
        body,
        (starts[-1],),
        ids,
        [(activated, pl.BlockSpec((slots, step), lambda i, d: (0, i)))] + units,
        [((slots, width), bf16, None)],
        [pltpu.VMEM((slots, width), f32), pltpu.VMEM((step, width), bf16)],
    )[0]


def unit_grads(ids, lefts, rights, j, adds, kind, cuts=None):
    slots, width = rights[0].shape
    units = lefts[0].shape[1] // lax.axis_size("seq")
    step = 256
    steps = units // step
    pairs = len(lefts)
    block = pl.BlockSpec((step, width), lambda i, d: (i, 0))
    upto = lambda c: pl.BlockSpec((step, width), lambda i, d: (jnp.minimum(i, c - 1), 0))
    beyond = lambda c: pl.BlockSpec((step, width), lambda i, d: (jnp.maximum(i - c, 0), 0))
    add_ins, splits = [], []
    for pair in adds:
        for a in pair:
            if isinstance(a, tuple):
                c = a[0].shape[0] // step
                add_ins += [(a[0], upto(c)), (a[1], beyond(c))]
                splits.append(c)
            else:
                add_ins.append((a, block))
                splits.append(0)
    more = len(adds[0])

    def body(ids_ref, *refs):
        l_refs, r_refs, refs = refs[:pairs], refs[pairs : 2 * pairs], refs[2 * pairs :]
        add_refs, out_refs = list(refs[: len(add_ins)]), refs[len(add_ins) :]
        here = pl.program_id(0)
        for p in range(pairs):
            total = dot(l_refs[p][...], r_refs[p][...], TN)
            for c in splits[p * more : (p + 1) * more]:
                if c:
                    one, two = add_refs.pop(0), add_refs.pop(0)
                    total += jnp.where(here < c, one[...], two[...]).astype(f32)
                else:
                    total += add_refs.pop(0)[...].astype(f32)
            if not cuts:
                out_refs[p][...] = total.astype(kind)
                continue

            @pl.when(here < cuts[p])
            def _():
                out_refs[2 * p][...] = total.astype(kind)

            @pl.when(here >= cuts[p])
            def _():
                out_refs[2 * p + 1][...] = total.astype(kind)

    outs = [((units, width), kind, block)] * pairs
    if cuts:
        outs = []
        for c in cuts:
            outs += [((c * step, width), kind, upto(c)), ((units - c * step, width), kind, beyond(c))]
    return kernel_call(
        body,
        (steps,),
        ids,
        [(left, pl.BlockSpec((slots, step), lambda i, d: (0, j * steps + i))) for left in lefts]
        + [(right, None) for right in rights]
        + add_ins,
        outs,
    )


def block_result(ids, hidden, returned, column):
    tokens, width = hidden.shape
    slots = returned.shape[0]

    def body(ids_ref, h_ref, c_ref, back_ref, out_ref):
        pick = one_hot_columns(c_ref[...], slots)
        out_ref[...] = (h_ref[...] + dot(pick, back_ref[...])).astype(bf16)

    return kernel_call(
        body,
        (1,),
        ids,
        [(hidden, None), (column, None), (returned, None)],
        [((tokens, width), bf16, None)],
    )[0]


def norm_back(values, gain, grads):
    scale = norm_scale(values)
    scaled = grads * gain
    along = jnp.mean(values * scaled, axis=-1, keepdims=True)
    through = scale * scaled - values * (scale * scale * scale * along)
    return through, jnp.sum(grads * (values * scale), axis=0, keepdims=True)


def hidden_back(ids, hidden, cotangent, gain, returned, column, weight, attended):
    tokens, width = hidden.shape
    slots = returned.shape[0]
    blocks = lax.axis_size("seq")
    part = width // blocks
    kinds = [f32 if j % 2 == 0 else bf16 for j in range(blocks)]

    def body(ids_ref, h_ref, c_ref, gain_ref, col_ref, back_ref, *refs):
        weights, att, refs = refs[:blocks], refs[blocks : 2 * blocks], refs[2 * blocks :]
        (gh_ref, gain_out), att_refs, grad_refs = refs[:2], refs[2 : 2 + blocks], refs[2 + blocks :]
        pick = one_hot_columns(col_ref[...], slots)
        grads = dot(pick, back_ref[...])
        through, gain_grad = norm_back(h_ref[...], gain_ref[...], grads)
        grad_hidden = c_ref[...].astype(f32) + through
        gh_ref[...] = grad_hidden
        low = grad_hidden.astype(bf16)
        gain_out[...] = gain_grad
        for j in range(blocks):
            att_refs[j][...] = dot(low, weights[j][...], NT).astype(bf16)
        for j in range(blocks):
            grad_refs[j][...] = dot(att[j][...], low, TN).astype(kinds[j])

    out = kernel_call(
        body,
        (1,),
        ids,
        [(hidden, None), (cotangent, None), (gain, None), (column, None), (returned, None)]
        + [head_rows(weight, j) for j in range(blocks)]
        + [(a, None) for a in attended],
        [((tokens, width), f32, None), ((1, width), f32, None)]
        + [((tokens, part), bf16, None)] * blocks
        + [((part, width), kind, None) for kind in kinds],
    )
    return out[0], out[1], out[2 : 2 + blocks], out[2 + blocks :]


def projection_back(ids, grads, weight):
    blocks = len(grads)
    tokens = grads[0].shape[0]
    width = weight.shape[0]
    part = grads[0].shape[1] // 3
    heads = width // part
    kinds = [f32 if j % 2 == 0 else bf16 for j in range(blocks)]

    def body(ids_ref, *refs):
        g_refs, w_refs, out_refs = refs[:blocks], refs[blocks : blocks + 3], refs[blocks + 3 :]
        for j in (1, 3, 2, 0):
            total = None
            for w in range(3):
                piece = dot(g_refs[j][:, w * part : (w + 1) * part], w_refs[w][...], NT)
                total = piece if total is None else total + piece
            out_refs[j][...] = total.astype(kinds[j])

    column = lambda which: pl.BlockSpec((width, part), lambda i, d: (0, d[0] + which * heads))
    return kernel_call(
        body,
        (1,),
        ids,
        [(g, None) for g in grads] + [(weight, column(w)) for w in range(3)],
        [((tokens, width), kind, None) for kind in kinds],
    )


def projection_grad(ids, normed, grads, groups):
    blocks = len(normed)
    tokens, columns = grads[0].shape
    width = normed[0].shape[1]
    step, height = 256, width // groups
    pairs = step // height // 2

    def body(ids_ref, *refs):
        n_refs, g_refs = refs[:blocks], refs[blocks : 2 * blocks]
        kept_ref, sent_ref, held = refs[2 * blocks :]
        total = dot(n_refs[0][...], g_refs[0][...], TN)
        for j in range(1, blocks):
            total += dot(n_refs[j][...], g_refs[j][...], TN)
        held[...] = total
        odd = ids_ref[1] % 2
        for b in range(pairs):
            kept = pl.multiple_of(2 * b * height + odd * height, 8)
            sent = pl.multiple_of((2 * b + 1) * height - odd * height, 8)
            kept_ref[b] = held[pl.ds(kept, height), :]
            sent_ref[b] = held[pl.ds(sent, height), :].astype(bf16)

    block = pl.BlockSpec((pairs, height, columns), lambda i, d: (i, 0, 0))
    return kernel_call(
        body,
        (width // step,),
        ids,
        [(n, pl.BlockSpec((tokens, step), lambda i, d: (0, i))) for n in normed]
        + [(g, None) for g in grads],
        [((groups // 2, height, columns), f32, block), ((groups // 2, height, columns), bf16, block)],
        [pltpu.VMEM((step, columns), f32)],
    )


def sum_groups(ids, pieces, times, first):
    groups, rows, width = pieces.shape
    widths = [first, width - first] if first < width else [width]

    def body(ids_ref, in_ref, *out_refs):
        total = in_ref[0].astype(f32)
        for k in range(1, groups):
            total += in_ref[k].astype(f32)
        low = total.astype(bf16)
        for k in range(times):
            out_refs[0][k] = low[:, :first]
            if first < width:
                out_refs[1][k] = low[:, first:]

    return kernel_call(
        body,
        (1,),
        ids,
        [(pieces, None)],
        [((times, rows, w), bf16, None) for w in widths],
    )


def across(value, alike=False):
    size = lax.axis_size("expert")
    sets = [list(range(p, size, 2)) for p in range(2)] if alike else None
    return lax.all_to_all(
        value, "expert", split_axis=0, concat_axis=0, tiled=True, axis_index_groups=sets
    )


def after(value, *earlier):
    return lax.optimization_barrier((value, *earlier))[0]


def after_all(values, *earlier):
    return lax.optimization_barrier((*values, *earlier))[: len(values)]


def spread_over_seq(value, *earlier):
    far = after(swap(value, "seq", 2), *earlier)
    return [value, swap(value, "seq", 1), far, swap(far, "seq", 1)]


def widen_columns(ids, pieces, first, count, total, out=None):
    blocks = len(pieces)
    rows, columns = pieces[0].shape
    part = columns // count
    step = 256

    def body(ids_ref, *refs):
        me = ids_ref[0]
        for j in range(blocks):
            at = pl.multiple_of((me ^ j) * part, part)
            refs[-1][:, pl.ds(at, part)] = refs[j][...].astype(f32)

    spec = pl.BlockSpec((step, part * blocks), lambda i, w, d: (i, first + w))
    ins = [(p, pl.BlockSpec((step, part), lambda i, w, d: (i, w))) for p in pieces]
    aliases = {}
    if out is not None:
        ins.append((out, pl.BlockSpec(memory_space=pl.ANY)))
        aliases = {len(ins): 0}
    return kernel_call(
        body,
        (rows // step, count),
        ids,
        ins,
        [((rows, total), f32, spec)],
        aliases=aliases,
    )[0]


def widen_rows(ids, pieces):
    blocks = len(pieces)
    rows, columns = pieces[0].shape

    def body(ids_ref, *refs):
        me = ids_ref[0]
        for j in range(blocks):
            at = pl.multiple_of((me ^ j) * rows, rows)
            refs[blocks][pl.ds(at, rows), :] = refs[j][...].astype(f32)

    return kernel_call(
        body,
        (1,),
        ids,
        [(p, None) for p in pieces],
        [((rows * blocks, columns), f32, None)],
    )[0]


def input_back(ids, rows, gain, grad_hidden, pieces):
    tokens, width = rows.shape

    def body(ids_ref, x_ref, gain_ref, gh_ref, a_ref, b_ref, c_ref, out_ref, gain_out):
        grads = a_ref[...] + b_ref[...].astype(f32) + c_ref[...].astype(f32)
        through, gain_grad = norm_back(x_ref[...].astype(f32), gain_ref[...], grads)
        out_ref[...] = gh_ref[...] + through
        gain_out[...] = gain_grad

    return kernel_call(
        body,
        (1,),
        ids,
        [(rows, None), (gain, None), (grad_hidden, None)] + [(a, None) for a in pieces],
        [((tokens, width), f32, None), ((1, width), f32, None)],
    )


def sum_along(value, axis):
    step = 1
    while step < lax.axis_size(axis):
        value = value + swap(value, axis, step)
        step *= 2
    return value


def shards(
    inputs,
    query_key_value_weight,
    output_weight,
    gain_attn,
    gain_ffn,
    w_up,
    w_down,
    expert_of,
    cotangent,
):
    groups = lax.axis_size("expert")
    blocks = lax.axis_size("seq")
    seq_count, local_len, width = inputs.shape
    tokens = seq_count * local_len
    capacity = max(2, 2 * tokens // groups)
    ids = jnp.stack([lax.axis_index("seq"), lax.axis_index("expert")]).astype(jnp.int32)
    gain_a, gain_f = gain_attn.reshape(1, width), gain_ffn.reshape(1, width)
    rows = inputs.reshape(tokens, width)
    cot = cotangent.reshape(tokens, width)

    down, up = w_down[0], w_up[0]
    rows_1 = swap(rows, "seq", 1)
    split = 5 * tokens // 8
    far_0, far_1 = swap(rows[:split], "seq", 2), swap(rows[split:], "seq", 2)
    down_near, up_near = swap(down, "seq", 1), swap(up, "seq", 1)
    first = project(ids, (rows, rows_1), gain_a, query_key_value_weight)
    slot, column, send = route(
        ids, expert_of.reshape(1, tokens), after(cot, first[0][0]), groups, capacity
    )
    send = after(send, far_0, down_near, up_near)
    rows_2 = after(jnp.concatenate([far_0, far_1], axis=0), send)
    grads_in = to_groups(send)
    rows_3 = swap(rows_2, "seq", 1)

    cut = up.shape[0] // 2
    up_far = swap(after(up[:cut], rows_2), "seq", 2)
    second = project(ids, (rows_2, rows_3), gain_a, query_key_value_weight)
    normed, queries, keys, values = (list(p) for p in zip(*first, *second))
    out, ot, lse = attention(ids, queries, keys, values)
    out = lax.optimization_barrier((*out, up_far))[:blocks]
    attended = [out[0]] + [swap(out[j], "seq", j) for j in range(1, blocks)]
    down_far = swap(after(down, *attended), "seq", 2)
    up_more = swap(after(up[cut:], *attended), "seq", 2)
    hidden, send = attention_out(
        ids, rows, attended, output_weight, gain_f, slot, groups, capacity
    )
    up_near_far = swap(after(up_far, send), "seq", 1)
    down_all = [down, down_near, down_far, swap(down_far, "seq", 1)]

    rows_in = to_groups(after(send, grads_in))
    grad_act = expert_grad_act(ids, grads_in, down_all)
    up_more = after(up_more, grad_act)
    up_all = [up, up_near, up_far, up_more, up_near_far, swap(up_more, "seq", 1)]
    activated, grad_pre, back = expert_main(ids, rows_in, grad_act, up_all)
    returned_grad = to_groups(back)
    left, right = (grad_pre, activated), (rows_in, grads_in)
    none = ((), ())
    near_3 = [swap(p, "seq", 1) for p in unit_grads(ids, left, right, 3, none, bf16)]
    near_1 = [swap(p, "seq", 1) for p in unit_grads(ids, left, right, 1, none, bf16)]
    up_0, up_1, down_0, down_1 = unit_grads(
        ids, left, right, 2, [(p,) for p in near_3], bf16, (1, 3)
    )
    up_0 = swap(up_0, "seq", 2)
    result = expert_out(ids, after(activated, down_0), down_all)

    returned_grad = after(returned_grad, result, up_0, *near_1)
    returned = to_groups(after(result, returned_grad))
    grad_hidden, ffn_gain_part, grad_att, out_parts = hidden_back(
        ids, hidden, cot, gain_f, returned_grad, column, output_weight, attended
    )
    grad_att = [grad_att[0]] + [swap(grad_att[j], "seq", j) for j in range(1, blocks)]
    near_out = [swap(after(out_parts[j], grad_att[1]), "seq", 1) for j in (1, 3)]
    far_out = (out_parts[2] + near_out[1].astype(f32)).astype(bf16)
    far_out = swap(after(far_out, *grad_att), "seq", 2)
    up_1 = swap(after(up_1, *grad_att), "seq", 2)
    down_0 = swap(after(down_0, *grad_att), "seq", 2)
    grad_proj = attention_back(ids, queries, keys, values, grad_att, ot, lse)
    grad_proj = after_all(grad_proj, far_out)

    kept, sent = projection_grad(ids, normed, grad_proj, groups)
    other = swap(sent, "expert", 1)
    out_part = (out_parts[0] + near_out[0].astype(f32) + far_out.astype(f32)).astype(bf16)
    height = out_part.shape[0] // groups
    out_own = across(after(out_part, returned, sent).reshape(groups, height, width))
    pieces = projection_back(ids, after_all(grad_proj, sent), query_key_value_weight)
    near = [swap(pieces[j], "seq", 1) for j in (1, 3)]
    far_rows = (pieces[2] + near[1].astype(f32)).astype(bf16)
    out_own = after(out_own, up_1, pieces[0])
    summed = across(after((kept + other.astype(f32)).astype(bf16), out_own), alike=True)
    far_arrived = swap(far_rows, "seq", 2)
    down_1 = swap(after(down_1, far_rows, down_0), "seq", 2)
    up_left = after(grad_pre, out_own)
    up_grad = unit_grads(ids, [up_left], [rows_in], 0, [(near_1[0], (up_0, up_1))], f32)[0]
    out_own = sum_groups(ids, out_own, groups, width)[0]
    block_out = block_result(ids, hidden, after(returned, far_rows), column)
    summed = after(summed, out_own, up_grad, down_0, block_out)
    part = width // blocks
    first, rest = sum_groups(ids, summed, groups, part)
    first_own = across(first).reshape(width, part)

    input_grad, attn_gain_part = input_back(
        ids, rows, gain_a, grad_hidden, (pieces[0], near[0], far_arrived)
    )
    first_own = after(first_own, input_grad)
    rest_own = across(after(rest, first_own)).reshape(width, 2 * part)
    first_all = spread_over_seq(first_own)
    gains = jnp.concatenate([attn_gain_part, ffn_gain_part], axis=0)
    gains = after(gains, first_own)
    gains = gains + swap(gains, "seq", 1)
    qkv_grad = widen_columns(ids, first_all, 0, 1, 3 * width)
    rest_own = after(rest_own, gains, qkv_grad, down_1)
    down_left = after(activated, rest_own)
    down_grad = unit_grads(ids, [down_left], [grads_in], 0, [(near_1[1], (down_0, down_1))], f32)[0]
    gains = sum_along(after(gains, rest_own), "expert")
    gains = gains + swap(gains, "seq", 2)
    rest_all = spread_over_seq(rest_own, gains, down_grad)
    out_own = across(after(out_own, rest_own)).reshape(out_part.shape)
    qkv_grad = widen_columns(ids, rest_all, 1, 2, 3 * width, qkv_grad)
    out_all = spread_over_seq(out_own, qkv_grad)
    out_grad = widen_rows(ids, after_all(out_all, qkv_grad))

    return (
        block_out.reshape(inputs.shape),
        input_grad.reshape(inputs.shape),
        qkv_grad,
        out_grad,
        gains[0],
        gains[1],
        up_grad[None],
        down_grad[None],
    )


def solution(mesh):
    tokens = P("expert", "seq", None)
    units = P("expert", "seq", None)
    in_specs = (tokens, P(), P(), P(), P(), units, units, P("expert", "seq"), tokens)
    out_specs = (tokens, tokens, P(), P(), P(), P(), units, units)
    return jax.shard_map(shards, mesh=mesh, in_specs=in_specs, out_specs=out_specs, check_vma=False)
```

```python
import jax
import jax.numpy as jnp
from jax import lax
from jax.experimental import pallas as pl
from jax.experimental.pallas import tpu as pltpu
from jax.sharding import PartitionSpec as P

HEAD_DIM = 64
EPSILON = 1e-06
SCORE_SCALE = 0.125 * 1.4426950408889634
bf16, f32 = jnp.bfloat16, jnp.float32

NN = (((1,), (0,)), ((), ()))
NT = (((1,), (1,)), ((), ()))
TN = (((0,), (0,)), ((), ()))


def dot(left, right, dims=NN):
    return lax.dot_general(left, right, dims, preferred_element_type=f32)


def sds(shape, dtype):
    return jax.ShapeDtypeStruct(shape, dtype)


def whole(shape):
    return pl.BlockSpec(shape, lambda *_: (0,) * len(shape))


def kernel_call(body, grid, ids, ins, outs, scratch=(), vmem=60, aliases=None):
    in_specs = [whole(a.shape) if sp is None else sp for a, sp in ins]
    out_specs = [whole(sh) if sp is None else sp for sh, _, sp in outs]
    return pl.pallas_call(
        body,
        grid_spec=pltpu.PrefetchScalarGridSpec(
            num_scalar_prefetch=1,
            grid=grid,
            in_specs=in_specs,
            out_specs=out_specs,
            scratch_shapes=list(scratch),
        ),
        out_shape=[sds(sh, dt) for sh, dt, _ in outs],
        input_output_aliases=aliases or {},
        compiler_params=pltpu.CompilerParams(
            vmem_limit_bytes=vmem << 20, dimension_semantics=("arbitrary",) * len(grid)
        ),
        cost_estimate=pl.CostEstimate(flops=1, bytes_accessed=1, transcendentals=0),
    )(ids, *[a for a, _ in ins])


def swap(value, axis, step):
    size = lax.axis_size(axis)
    return lax.ppermute(value, axis, [(i, i ^ step) for i in range(size)])


def norm_scale(values):
    return lax.rsqrt(jnp.mean(values * values, axis=-1, keepdims=True) + EPSILON)


def route(ids, routes, rows, groups, capacity):
    tokens, width = rows.shape
    slots = groups * capacity

    def body(ids_ref, routes_ref, rows_ref, slot_ref, column_ref, send_ref):
        route_row = routes_ref[...]
        named = lax.broadcasted_iota(jnp.int32, (groups, tokens), 0) == route_row
        ones = jnp.where(named, 1.0, 0.0)
        earlier = lax.broadcasted_iota(jnp.int32, (tokens, tokens), 0)
        later = lax.broadcasted_iota(jnp.int32, (tokens, tokens), 1)
        upto = jnp.where(earlier <= later, 1.0, 0.0)
        count = dot(ones, upto)
        place = jnp.sum(count * ones, axis=0, keepdims=True) - 1.0
        slot = route_row * capacity + place.astype(jnp.int32)
        slot_ref[...] = slot
        column_ref[...] = jnp.transpose(jnp.broadcast_to(slot.astype(f32), (128, tokens)))
        pick = lax.broadcasted_iota(jnp.int32, (slots, tokens), 0) == slot
        laid = dot(jnp.where(pick, 1.0, 0.0).astype(bf16), rows_ref[...])
        send_ref[...] = laid.astype(bf16)

    return kernel_call(
        body,
        (1,),
        ids,
        [(routes, None), (rows, None)],
        [
            ((1, tokens), jnp.int32, None),
            ((tokens, 128), f32, None),
            ((slots, width), bf16, None),
        ],
    )


def to_groups(rows):
    groups = lax.axis_size("expert")
    cut = rows.reshape(groups, rows.shape[0] // groups, rows.shape[1])
    return lax.all_to_all(cut, "expert", split_axis=0, concat_axis=0, tiled=True).reshape(rows.shape)


def one_hot_columns(column, slots):
    wide = jnp.concatenate([column] * (slots // 128), axis=1)
    lanes = lax.broadcasted_iota(jnp.int32, wide.shape, 1).astype(f32)
    return jnp.where(wide == lanes, 1.0, 0.0).astype(bf16)


def project(ids, rows, gain, weight):
    tokens, width = rows[0].shape
    part = width // lax.axis_size("seq")
    heads = width // part
    count = len(rows)

    def body(ids_ref, gain_ref, wq_ref, wk_ref, wv_ref, *refs):
        x_refs, refs = refs[:count], refs[count:]
        for x_ref, outs in zip(x_refs, (refs[4 * r : 4 * r + 4] for r in range(count))):
            values = x_ref[...].astype(f32)
            normed = (values * norm_scale(values) * gain_ref[...]).astype(bf16)
            outs[0][...] = normed
            for w_ref, out in zip((wq_ref, wk_ref, wv_ref), outs[1:]):
                out[...] = dot(normed, w_ref[...]).astype(bf16)

    half = tokens // 2
    column = lambda which: pl.BlockSpec((width, part), lambda i, d: (0, d[0] + which * heads))
    row_spec = lambda n: pl.BlockSpec((half, n), lambda i, d: (i, 0))
    out = kernel_call(
        body,
        (2,),
        ids,
        [(gain, None)] + [(weight, column(w)) for w in range(3)] + [(r, row_spec(width)) for r in rows],
        (
            [((tokens, width), bf16, row_spec(width))]
            + [((tokens, part), bf16, row_spec(part))] * 3
        )
        * count,
    )
    return [out[4 * r : 4 * r + 4] for r in range(count)]


def head_lanes(block, head):
    lanes = lax.broadcasted_iota(jnp.int32, block.shape, 1)
    inside = (lanes >= head * HEAD_DIM) & (lanes < (head + 1) * HEAD_DIM)
    return jnp.where(inside, block, jnp.zeros_like(block))


def fold_rows(values, how):
    return how(values.reshape(values.shape[0] // 8, 8, values.shape[1]), axis=0)


def attention(ids, queries, keys, values):
    blocks = len(queries)
    tokens, part = queries[0].shape
    length = tokens // 2
    heads = part // HEAD_DIM
    total = blocks * length

    def body(ids_ref, *refs):
        ins, refs = refs[: 3 * blocks], refs[3 * blocks :]
        out_refs, refs = refs[:blocks], refs[blocks:]
        ot_ref, lse_ref, q_all, k_all, vt_all, stacked, scores, result = refs
        me = ids_ref[0]
        for j in range(blocks):
            rows = pl.ds(pl.multiple_of((me ^ j) * length, length), length)
            q_all[rows, :] = ins[j][...]
            k_all[rows, :] = ins[blocks + j][...]
            vt_all[:, rows] = jnp.transpose(ins[2 * blocks + j][...].astype(f32)).astype(bf16)
        hidden = lax.broadcasted_iota(jnp.int32, (length, length), 0) > lax.broadcasted_iota(
            jnp.int32, (length, length), 1
        )
        for qa in range(blocks):
            here = slice(qa * length, (qa + 1) * length)
            q_block = q_all[here, :]
            for h in range(heads):
                stacked[h * length : (h + 1) * length, :] = head_lanes(q_block, h)
            for h in range(heads):
                lanes = slice(h * length, (h + 1) * length)
                most = None
                for kb in range(qa + 1):
                    there = slice(kb * length, (kb + 1) * length)
                    found = dot(k_all[there, :], stacked[lanes, :], NT)
                    if kb == qa:
                        found = jnp.where(hidden, -1e30, found)
                    scores[there, lanes] = found
                    top = fold_rows(found, jnp.max)
                    most = top if most is None else jnp.maximum(most, top)
                peak = jnp.max(most, axis=0, keepdims=True) * SCORE_SCALE
                summed, gathered = None, None
                for kb in range(qa + 1):
                    there = slice(kb * length, (kb + 1) * length)
                    raised = jnp.exp2(scores[there, lanes] * SCORE_SCALE - peak)
                    part_sum = fold_rows(raised, jnp.sum)
                    summed = part_sum if summed is None else summed + part_sum
                    piece = dot(
                        vt_all[h * HEAD_DIM : (h + 1) * HEAD_DIM, there], raised.astype(bf16)
                    )
                    gathered = piece if gathered is None else gathered + piece
                weight = jnp.sum(summed, axis=0, keepdims=True)
                ot_ref[0, h * HEAD_DIM : (h + 1) * HEAD_DIM, here] = gathered * (1.0 / weight)
                lse_ref[0, qa : qa + 1, lanes] = peak + jnp.log2(weight)
            result[here, :] = jnp.transpose(ot_ref[0, :, here]).astype(bf16)
        for j in range(blocks):
            rows = pl.ds(pl.multiple_of((me ^ j) * length, length), length)
            out_refs[j][...] = result[rows, :]

    spec = pl.BlockSpec((length, part), lambda i, d: (i, 0))
    out = kernel_call(
        body,
        (2,),
        ids,
        [(a, spec) for a in (*queries, *keys, *values)],
        [((tokens, part), bf16, spec)] * blocks
        + [
            ((2, part, total), f32, pl.BlockSpec((1, part, total), lambda i, d: (i, 0, 0))),
            (
                (2, blocks, heads * length),
                f32,
                pl.BlockSpec((1, blocks, heads * length), lambda i, d: (i, 0, 0)),
            ),
        ],
        [
            pltpu.VMEM((total, part), bf16),
            pltpu.VMEM((total, part), bf16),
            pltpu.VMEM((part, total), bf16),
            pltpu.VMEM((heads * length, part), bf16),
            pltpu.VMEM((total, heads * length), f32),
            pltpu.VMEM((total, part), bf16),
        ],
    )
    return out[:blocks], out[blocks], out[blocks + 1]


def attention_back(ids, queries, keys, values, grads, ot, lse):
    blocks = len(queries)
    tokens, part = queries[0].shape
    length = tokens // 2
    heads = part // HEAD_DIM
    total = blocks * length

    def body(ids_ref, *refs):
        ins, refs = refs[: 4 * blocks], refs[4 * blocks :]
        ot_ref, lse_ref, refs = refs[0], refs[1], refs[2:]
        out_refs, refs = refs[:blocks], refs[blocks:]
        q_all, k_all, v_all, g_all, kt_all, q_stack, g_stack, low, ds_low, dk, dv, dqt, dq = refs
        me = ids_ref[0]
        for j in range(blocks):
            rows = pl.ds(pl.multiple_of((me ^ j) * length, length), length)
            q_all[rows, :] = ins[j][...]
            k_all[rows, :] = ins[blocks + j][...]
            v_all[rows, :] = ins[2 * blocks + j][...]
            g_all[rows, :] = ins[3 * blocks + j][...]
            kt_all[:, rows] = jnp.transpose(ins[blocks + j][...].astype(f32)).astype(bf16)
        dk[...] = jnp.zeros_like(dk)
        dv[...] = jnp.zeros_like(dv)
        hidden = lax.broadcasted_iota(jnp.int32, (length, length), 0) > lax.broadcasted_iota(
            jnp.int32, (length, length), 1
        )
        for qa in range(blocks):
            here = slice(qa * length, (qa + 1) * length)
            q_block, g_block = q_all[here, :], g_all[here, :]
            for h in range(heads):
                lanes = slice(h * length, (h + 1) * length)
                q_stack[lanes, :] = head_lanes(q_block, h)
                g_stack[lanes, :] = head_lanes(g_block, h)
            product = jnp.transpose(g_block.astype(f32)) * ot_ref[0, :, here]
            totals = [
                jnp.sum(product[h * HEAD_DIM : (h + 1) * HEAD_DIM], axis=0, keepdims=True)
                for h in range(heads)
            ]
            for kb in range(qa + 1):
                there = slice(kb * length, (kb + 1) * length)
                for h in range(heads):
                    lanes = slice(h * length, (h + 1) * length)
                    found = dot(k_all[there, :], q_stack[lanes, :], NT)
                    if kb == qa:
                        found = jnp.where(hidden, -1e30, found)
                    probs = jnp.exp2(found * SCORE_SCALE - lse_ref[0, qa : qa + 1, lanes])
                    grad_probs = dot(v_all[there, :], g_stack[lanes, :], NT)
                    low[:, lanes] = probs.astype(bf16)
                    ds_low[:, lanes] = (probs * (grad_probs - totals[h])).astype(bf16)
                dv[there, :] += dot(low[...], g_stack[...])
                dk[there, :] += dot(ds_low[...], q_stack[...])
                for h in range(heads):
                    lanes = slice(h * length, (h + 1) * length)
                    rows = slice(h * HEAD_DIM, (h + 1) * HEAD_DIM)
                    piece = dot(kt_all[rows, there], ds_low[:, lanes])
                    if kb == 0:
                        dqt[rows, :] = piece
                    else:
                        dqt[rows, :] += piece
            dq[here, :] = (0.125 * jnp.transpose(dqt[...])).astype(bf16)
        for j in range(blocks):
            rows = pl.ds(pl.multiple_of((me ^ j) * length, length), length)
            out_refs[j][:, 0:part] = dq[rows, :]
            out_refs[j][:, part : 2 * part] = (0.125 * dk[rows, :]).astype(bf16)
            out_refs[j][:, 2 * part : 3 * part] = dv[rows, :].astype(bf16)

    spec = pl.BlockSpec((length, part), lambda i, d: (i, 0))
    return kernel_call(
        body,
        (2,),
        ids,
        [(a, spec) for a in (*queries, *keys, *values, *grads)]
        + [
            (ot, pl.BlockSpec((1, part, total), lambda i, d: (i, 0, 0))),
            (lse, pl.BlockSpec((1, blocks, heads * length), lambda i, d: (i, 0, 0))),
        ],
        [((tokens, 3 * part), bf16, pl.BlockSpec((length, 3 * part), lambda i, d: (i, 0)))]
        * blocks,
        [pltpu.VMEM((total, part), bf16)] * 4
        + [
            pltpu.VMEM((part, total), bf16),
            pltpu.VMEM((heads * length, part), bf16),
            pltpu.VMEM((heads * length, part), bf16),
            pltpu.VMEM((length, heads * length), bf16),
            pltpu.VMEM((length, heads * length), bf16),
            pltpu.VMEM((total, part), f32),
            pltpu.VMEM((total, part), f32),
            pltpu.VMEM((part, length), f32),
            pltpu.VMEM((total, part), bf16),
        ],
    )


def head_rows(weight, j):
    part = weight.shape[0] // lax.axis_size("seq")
    return (weight, pl.BlockSpec((part, weight.shape[1]), lambda i, d: (d[0] ^ j, 0)))


def attention_out(ids, rows, attended, weight, gain, slot, groups, capacity):
    tokens, width = rows.shape
    slots = groups * capacity
    blocks = len(attended)

    def body(ids_ref, x_ref, gain_ref, slot_ref, *refs):
        att, weights, (h_ref, send_ref) = refs[:blocks], refs[blocks : 2 * blocks], refs[2 * blocks :]
        hidden = x_ref[...].astype(f32)
        for j in range(blocks):
            hidden += dot(att[j][...], weights[j][...])
        h_ref[...] = hidden
        normed = (hidden * norm_scale(hidden) * gain_ref[...]).astype(bf16)
        pick = lax.broadcasted_iota(jnp.int32, (slots, tokens), 0) == slot_ref[...]
        laid = dot(jnp.where(pick, 1.0, 0.0).astype(bf16), normed)
        send_ref[...] = laid.astype(bf16)

    return kernel_call(
        body,
        (1,),
        ids,
        [(rows, None), (gain, None), (slot, None)]
        + [(a, None) for a in attended]
        + [head_rows(weight, j) for j in range(blocks)],
        [((tokens, width), f32, None), ((slots, width), bf16, None)],
    )


def normal_parts(values):
    below = 0.5 + 0.5 * lax.erf(values * 0.7071067811865476)
    fall = jnp.exp2(values * values * -0.7213475204444817)
    return below, values * fall * 0.3989422804014327


def unit_specs(weights, step):
    starts = [0]
    for w in weights:
        starts.append(starts[-1] + w.shape[0] // step)

    def spec(j):
        last = starts[j + 1] - starts[j] - 1
        return pl.BlockSpec(
            (step, weights[j].shape[1]), lambda i, d: (jnp.clip(i - starts[j], 0, last), 0)
        )

    return starts, [(w, spec(j)) for j, w in enumerate(weights)]


def take_units(refs, starts, held):
    here = pl.program_id(0)
    for j, ref in enumerate(refs):

        @pl.when((here >= starts[j]) & (here < starts[j + 1]))
        def _():
            held[...] = ref[...]


def expert_grad_act(ids, grads, weights):
    slots, width = grads.shape
    step = 512
    starts, units = unit_specs(weights, step)
    hidden = starts[-1] * step

    def body(ids_ref, g_ref, *refs):
        w_refs, (out_ref, held) = refs[:-2], refs[-2:]
        take_units(w_refs, starts, held)
        out_ref[...] = dot(g_ref[...], held[...], NT)

    return kernel_call(
        body,
        (hidden // step,),
        ids,
        [(grads, None)] + units,
        [((slots, hidden), f32, pl.BlockSpec((slots, step), lambda i, d: (0, i)))],
        [pltpu.VMEM((step, width), bf16)],
    )[0]


def expert_main(ids, rows_in, grad_act, weights):
    slots, width = rows_in.shape
    step, chunk = 512, 256
    starts, units = unit_specs(weights, step)
    hidden = starts[-1] * step

    def body(ids_ref, x_ref, ga_ref, *refs):
        w_refs, (act_ref, gp_ref, out_ref, total, held) = refs[:-5], refs[-5:]
        here = pl.program_id(0)
        take_units(w_refs, starts, held)

        @pl.when(here == 0)
        def _():
            total[...] = jnp.zeros_like(total)

        parts = [slice(r * chunk, (r + 1) * chunk) for r in range(slots // chunk)]
        pre, last = dot(x_ref[parts[0], :], held[...], NT), None
        for r, part in enumerate(parts):
            later = None
            if r + 1 < len(parts):
                later = dot(x_ref[parts[r + 1], :], held[...], NT)
            below, dense = normal_parts(pre)
            act_ref[part, :] = (pre * below).astype(bf16)
            grad_pre = (ga_ref[part, :] * (below + dense)).astype(bf16)
            gp_ref[part, :] = grad_pre
            if last is not None:
                total[parts[r - 1], :] += dot(last, held[...])
            pre, last = later, grad_pre
        total[parts[-1], :] += dot(last, held[...])

        @pl.when(here == pl.num_programs(0) - 1)
        def _():
            out_ref[...] = total[...].astype(bf16)

    wide = pl.BlockSpec((slots, step), lambda i, d: (0, i))
    return kernel_call(
        body,
        (hidden // step,),
        ids,
        [(rows_in, None), (grad_act, wide)] + units,
        [((slots, hidden), bf16, wide)] * 2 + [((slots, width), bf16, None)],
        [pltpu.VMEM((slots, width), f32), pltpu.VMEM((step, width), bf16)],
    )


def expert_out(ids, activated, weights):
    slots = activated.shape[0]
    width = weights[0].shape[1]
    step = 512
    starts, units = unit_specs(weights, step)

    def body(ids_ref, act_ref, *refs):
        w_refs, (out_ref, total, held) = refs[:-3], refs[-3:]
        here = pl.program_id(0)
        take_units(w_refs, starts, held)

        @pl.when(here == 0)
        def _():
            total[...] = jnp.zeros_like(total)

        total[...] += dot(act_ref[...], held[...])

        @pl.when(here == pl.num_programs(0) - 1)
        def _():
            out_ref[...] = total[...].astype(bf16)

    return kernel_call(
        body,
        (starts[-1],),
        ids,
        [(activated, pl.BlockSpec((slots, step), lambda i, d: (0, i)))] + units,
        [((slots, width), bf16, None)],
        [pltpu.VMEM((slots, width), f32), pltpu.VMEM((step, width), bf16)],
    )[0]


def unit_grads(ids, lefts, rights, j, adds, kind, cuts=None):
    slots, width = rights[0].shape
    units = lefts[0].shape[1] // lax.axis_size("seq")
    step = 256
    steps = units // step
    pairs = len(lefts)
    block = pl.BlockSpec((step, width), lambda i, d: (i, 0))
    upto = lambda c: pl.BlockSpec((step, width), lambda i, d: (jnp.minimum(i, c - 1), 0))
    beyond = lambda c: pl.BlockSpec((step, width), lambda i, d: (jnp.maximum(i - c, 0), 0))
    add_ins, splits = [], []
    for pair in adds:
        for a in pair:
            if isinstance(a, tuple):
                c = a[0].shape[0] // step
                add_ins += [(a[0], upto(c)), (a[1], beyond(c))]
                splits.append(c)
            else:
                add_ins.append((a, block))
                splits.append(0)
    more = len(adds[0])

    def body(ids_ref, *refs):
        l_refs, r_refs, refs = refs[:pairs], refs[pairs : 2 * pairs], refs[2 * pairs :]
        add_refs, out_refs = list(refs[: len(add_ins)]), refs[len(add_ins) :]
        here = pl.program_id(0)
        for p in range(pairs):
            total = dot(l_refs[p][...], r_refs[p][...], TN)
            for c in splits[p * more : (p + 1) * more]:
                if c:
                    one, two = add_refs.pop(0), add_refs.pop(0)
                    total += jnp.where(here < c, one[...], two[...]).astype(f32)
                else:
                    total += add_refs.pop(0)[...].astype(f32)
            if not cuts:
                out_refs[p][...] = total.astype(kind)
                continue

            @pl.when(here < cuts[p])
            def _():
                out_refs[2 * p][...] = total.astype(kind)

            @pl.when(here >= cuts[p])
            def _():
                out_refs[2 * p + 1][...] = total.astype(kind)

    outs = [((units, width), kind, block)] * pairs
    if cuts:
        outs = []
        for c in cuts:
            outs += [((c * step, width), kind, upto(c)), ((units - c * step, width), kind, beyond(c))]
    return kernel_call(
        body,
        (steps,),
        ids,
        [(left, pl.BlockSpec((slots, step), lambda i, d: (0, j * steps + i))) for left in lefts]
        + [(right, None) for right in rights]
        + add_ins,
        outs,
    )


def block_result(ids, hidden, returned, column):
    tokens, width = hidden.shape
    slots = returned.shape[0]

    def body(ids_ref, h_ref, c_ref, back_ref, out_ref):
        pick = one_hot_columns(c_ref[...], slots)
        out_ref[...] = (h_ref[...] + dot(pick, back_ref[...])).astype(bf16)

    return kernel_call(
        body,
        (1,),
        ids,
        [(hidden, None), (column, None), (returned, None)],
        [((tokens, width), bf16, None)],
    )[0]


def norm_back(values, gain, grads):
    scale = norm_scale(values)
    scaled = grads * gain
    along = jnp.mean(values * scaled, axis=-1, keepdims=True)
    through = scale * scaled - values * (scale * scale * scale * along)
    return through, jnp.sum(grads * (values * scale), axis=0, keepdims=True)


def hidden_back(ids, hidden, cotangent, gain, returned, column, weight, attended):
    tokens, width = hidden.shape
    slots = returned.shape[0]
    blocks = lax.axis_size("seq")
    part = width // blocks
    kinds = [f32 if j % 2 == 0 else bf16 for j in range(blocks)]

    def body(ids_ref, h_ref, c_ref, gain_ref, col_ref, back_ref, *refs):
        weights, att, refs = refs[:blocks], refs[blocks : 2 * blocks], refs[2 * blocks :]
        (gh_ref, gain_out), att_refs, grad_refs = refs[:2], refs[2 : 2 + blocks], refs[2 + blocks :]
        pick = one_hot_columns(col_ref[...], slots)
        grads = dot(pick, back_ref[...])
        through, gain_grad = norm_back(h_ref[...], gain_ref[...], grads)
        grad_hidden = c_ref[...].astype(f32) + through
        gh_ref[...] = grad_hidden
        low = grad_hidden.astype(bf16)
        gain_out[...] = gain_grad
        for j in range(blocks):
            att_refs[j][...] = dot(low, weights[j][...], NT).astype(bf16)
        for j in range(blocks):
            grad_refs[j][...] = dot(att[j][...], low, TN).astype(kinds[j])

    out = kernel_call(
        body,
        (1,),
        ids,
        [(hidden, None), (cotangent, None), (gain, None), (column, None), (returned, None)]
        + [head_rows(weight, j) for j in range(blocks)]
        + [(a, None) for a in attended],
        [((tokens, width), f32, None), ((1, width), f32, None)]
        + [((tokens, part), bf16, None)] * blocks
        + [((part, width), kind, None) for kind in kinds],
    )
    return out[0], out[1], out[2 : 2 + blocks], out[2 + blocks :]


def projection_back(ids, grads, weight):
    blocks = len(grads)
    tokens = grads[0].shape[0]
    width = weight.shape[0]
    part = grads[0].shape[1] // 3
    heads = width // part
    kinds = [f32 if j % 2 == 0 else bf16 for j in range(blocks)]

    def body(ids_ref, *refs):
        g_refs, w_refs, out_refs = refs[:blocks], refs[blocks : blocks + 3], refs[blocks + 3 :]
        for j in (1, 3, 2, 0):
            total = None
            for w in range(3):
                piece = dot(g_refs[j][:, w * part : (w + 1) * part], w_refs[w][...], NT)
                total = piece if total is None else total + piece
            out_refs[j][...] = total.astype(kinds[j])

    column = lambda which: pl.BlockSpec((width, part), lambda i, d: (0, d[0] + which * heads))
    return kernel_call(
        body,
        (1,),
        ids,
        [(g, None) for g in grads] + [(weight, column(w)) for w in range(3)],
        [((tokens, width), kind, None) for kind in kinds],
    )


def projection_grad(ids, normed, grads, groups):
    blocks = len(normed)
    tokens, columns = grads[0].shape
    width = normed[0].shape[1]
    step, height = 256, width // groups
    pairs = step // height // 2

    def body(ids_ref, *refs):
        n_refs, g_refs = refs[:blocks], refs[blocks : 2 * blocks]
        kept_ref, sent_ref, held = refs[2 * blocks :]
        total = dot(n_refs[0][...], g_refs[0][...], TN)
        for j in range(1, blocks):
            total += dot(n_refs[j][...], g_refs[j][...], TN)
        held[...] = total
        odd = ids_ref[1] % 2
        for b in range(pairs):
            kept = pl.multiple_of(2 * b * height + odd * height, 8)
            sent = pl.multiple_of((2 * b + 1) * height - odd * height, 8)
            kept_ref[b] = held[pl.ds(kept, height), :]
            sent_ref[b] = held[pl.ds(sent, height), :].astype(bf16)

    block = pl.BlockSpec((pairs, height, columns), lambda i, d: (i, 0, 0))
    return kernel_call(
        body,
        (width // step,),
        ids,
        [(n, pl.BlockSpec((tokens, step), lambda i, d: (0, i))) for n in normed]
        + [(g, None) for g in grads],
        [((groups // 2, height, columns), f32, block), ((groups // 2, height, columns), bf16, block)],
        [pltpu.VMEM((step, columns), f32)],
    )


def sum_groups(ids, pieces, out_pieces, part):
    rows, width = pieces.shape[1:]
    groups, height, total = out_pieces.shape

    def body(ids_ref, in_ref, out_in_ref, mixed_ref, rest_ref):
        low = sum(in_ref[k].astype(f32) for k in range(pieces.shape[0])).astype(bf16)
        out = sum(out_in_ref[k].astype(f32) for k in range(groups))
        tall = [out[:, c * part : (c + 1) * part] for c in range(total // part)]
        tall = jnp.concatenate(tall, axis=0).astype(bf16)
        for k in range(groups):
            mixed_ref[k, :, :part] = low[:, :part]
            mixed_ref[k, :, part:] = tall
            rest_ref[k] = low[:, part:]

    return kernel_call(
        body,
        (1,),
        ids,
        [(pieces, None), (out_pieces, None)],
        [((groups, rows, 2 * part), bf16, None), ((groups, rows, width - part), bf16, None)],
        vmem=28,
    )


def across(value, alike=False):
    size = lax.axis_size("expert")
    sets = [list(range(p, size, 2)) for p in range(2)] if alike else None
    return lax.all_to_all(
        value, "expert", split_axis=0, concat_axis=0, tiled=True, axis_index_groups=sets
    )


def after(value, *earlier):
    return lax.optimization_barrier((value, *earlier))[0]


def after_all(values, *earlier):
    return lax.optimization_barrier((*values, *earlier))[: len(values)]


def spread_over_seq(value, *earlier):
    far = after(swap(value, "seq", 2), *earlier)
    return [value, swap(value, "seq", 1), far, swap(far, "seq", 1)]


def widen_columns(ids, pieces, first, count, total, out=None):
    blocks = len(pieces)
    rows, columns = pieces[0].shape
    part = total // 3 // blocks
    step = 256

    def body(ids_ref, *refs):
        me = ids_ref[0]
        for j in range(blocks):
            at = pl.multiple_of((me ^ j) * part, part)
            refs[-1][:, pl.ds(at, part)] = refs[j][...].astype(f32)

    spec = pl.BlockSpec((step, part * blocks), lambda i, w, d: (i, first + w))
    ins = [(p, pl.BlockSpec((step, part), lambda i, w, d: (i, w))) for p in pieces]
    aliases = {}
    if out is not None:
        ins.append((out, pl.BlockSpec(memory_space=pl.ANY)))
        aliases = {len(ins): 0}
    return kernel_call(
        body,
        (rows // step, count),
        ids,
        ins,
        [((rows, total), f32, spec)],
        aliases=aliases,
        vmem=28,
    )[0]


def widen_rows(ids, pieces, groups):
    blocks = len(pieces)
    width = pieces[0].shape[0]
    part = pieces[0].shape[1] // 2
    height, tall = part // groups, width // groups

    def body(ids_ref, *refs):
        me = ids_ref[0]
        for j in range(blocks):
            for e in range(groups):
                cut = refs[j][e * tall : (e + 1) * tall, :].astype(f32)
                at = pl.multiple_of((me ^ j) * part, part) + e * height
                for c in range(blocks):
                    refs[blocks][pl.ds(pl.multiple_of(at, 8), height), c * part : (c + 1) * part] = cut[
                        c * height : (c + 1) * height
                    ]

    return kernel_call(
        body,
        (1,),
        ids,
        [(p, pl.BlockSpec((width, part), lambda i, d: (0, 1))) for p in pieces],
        [((width, part * blocks), f32, None)],
        vmem=28,
    )[0]


def input_back(ids, rows, gain, grad_hidden, pieces):
    tokens, width = rows.shape

    def body(ids_ref, x_ref, gain_ref, gh_ref, a_ref, b_ref, c_ref, out_ref, gain_out):
        grads = a_ref[...] + b_ref[...].astype(f32) + c_ref[...].astype(f32)
        through, gain_grad = norm_back(x_ref[...].astype(f32), gain_ref[...], grads)
        out_ref[...] = gh_ref[...] + through
        gain_out[...] = gain_grad

    return kernel_call(
        body,
        (1,),
        ids,
        [(rows, None), (gain, None), (grad_hidden, None)] + [(a, None) for a in pieces],
        [((tokens, width), f32, None), ((1, width), f32, None)],
    )


def sum_along(value, axis):
    step = 1
    while step < lax.axis_size(axis):
        value = value + swap(value, axis, step)
        step *= 2
    return value


def shards(
    inputs,
    query_key_value_weight,
    output_weight,
    gain_attn,
    gain_ffn,
    w_up,
    w_down,
    expert_of,
    cotangent,
):
    groups = lax.axis_size("expert")
    blocks = lax.axis_size("seq")
    seq_count, local_len, width = inputs.shape
    tokens = seq_count * local_len
    capacity = max(2, 2 * tokens // groups)
    ids = jnp.stack([lax.axis_index("seq"), lax.axis_index("expert")]).astype(jnp.int32)
    gain_a, gain_f = gain_attn.reshape(1, width), gain_ffn.reshape(1, width)
    rows = inputs.reshape(tokens, width)
    cot = cotangent.reshape(tokens, width)

    down, up = w_down[0], w_up[0]
    rows_1 = swap(rows, "seq", 1)
    split = 5 * tokens // 8
    far_0, far_1 = swap(rows[:split], "seq", 2), swap(rows[split:], "seq", 2)
    down_near, up_near = swap(down, "seq", 1), swap(up, "seq", 1)
    first = project(ids, (rows, rows_1), gain_a, query_key_value_weight)
    slot, column, send = route(
        ids, expert_of.reshape(1, tokens), after(cot, first[0][0]), groups, capacity
    )
    send = after(send, far_0, down_near, up_near)
    rows_2 = after(jnp.concatenate([far_0, far_1], axis=0), send)
    grads_in = to_groups(send)
    rows_3 = swap(rows_2, "seq", 1)

    cut = up.shape[0] // 2
    up_far = swap(after(up[:cut], rows_2), "seq", 2)
    second = project(ids, (rows_2, rows_3), gain_a, query_key_value_weight)
    normed, queries, keys, values = (list(p) for p in zip(*first, *second))
    out, ot, lse = attention(ids, queries, keys, values)
    out = lax.optimization_barrier((*out, up_far))[:blocks]
    attended = [out[0]] + [swap(out[j], "seq", j) for j in range(1, blocks)]
    down_far = swap(after(down, *attended), "seq", 2)
    up_more = swap(after(up[cut:], *attended), "seq", 2)
    hidden, send = attention_out(
        ids, rows, attended, output_weight, gain_f, slot, groups, capacity
    )
    up_near_far = swap(after(up_far, send), "seq", 1)
    down_all = [down, down_near, down_far, swap(down_far, "seq", 1)]

    rows_in = to_groups(after(send, grads_in))
    grad_act = expert_grad_act(ids, grads_in, down_all)
    up_more = after(up_more, grad_act)
    up_all = [up, up_near, up_far, up_more, up_near_far, swap(up_more, "seq", 1)]
    activated, grad_pre, back = expert_main(ids, rows_in, grad_act, up_all)
    returned_grad = to_groups(back)
    left, right = (grad_pre, activated), (rows_in, grads_in)
    none = ((), ())
    near_3 = [swap(p, "seq", 1) for p in unit_grads(ids, left, right, 3, none, bf16)]
    near_1 = [swap(p, "seq", 1) for p in unit_grads(ids, left, right, 1, none, bf16)]
    up_0, up_1, down_0, down_1 = unit_grads(
        ids, left, right, 2, [(p,) for p in near_3], bf16, (1, 1)
    )
    up_0 = swap(up_0, "seq", 2)
    down_0 = swap(after(down_0, up_0), "seq", 2)
    result = expert_out(ids, after(activated, down_1), down_all)

    returned_grad = after(returned_grad, result, up_0, *near_1)
    returned = to_groups(after(result, returned_grad))
    grad_hidden, ffn_gain_part, grad_att, out_parts = hidden_back(
        ids, hidden, cot, gain_f, returned_grad, column, output_weight, attended
    )
    grad_att = after_all(grad_att, down_0)
    grad_att = [grad_att[0]] + [swap(grad_att[j], "seq", j) for j in range(1, blocks)]
    near_out = [swap(after(out_parts[j], grad_att[1]), "seq", 1) for j in (1, 3)]
    far_out = (out_parts[2] + near_out[1].astype(f32)).astype(bf16)
    far_out = swap(after(far_out, *grad_att), "seq", 2)
    up_1 = swap(after(up_1, *grad_att), "seq", 2)
    down_1 = swap(after(down_1, *grad_att), "seq", 2)
    grad_proj = attention_back(ids, queries, keys, values, grad_att, ot, lse)
    grad_proj = after_all(grad_proj, far_out)

    kept, sent = projection_grad(ids, normed, grad_proj, groups)
    other = swap(sent, "expert", 1)
    out_part = (out_parts[0] + near_out[0].astype(f32) + far_out.astype(f32)).astype(bf16)
    height = out_part.shape[0] // groups
    out_own = across(after(out_part, returned, sent).reshape(groups, height, width))
    pieces = projection_back(ids, after_all(grad_proj, sent), query_key_value_weight)
    near = [swap(pieces[j], "seq", 1) for j in (1, 3)]
    far_rows = (pieces[2] + near[1].astype(f32)).astype(bf16)
    out_own = after(out_own, up_1, pieces[0])
    summed = across(after((kept + other.astype(f32)).astype(bf16), out_own), alike=True)
    far_arrived = swap(far_rows, "seq", 2)
    up_left = after(grad_pre, out_own)
    up_grad = unit_grads(ids, [up_left], [rows_in], 0, [(near_1[0], (up_0, up_1))], f32)[0]
    summed = after(summed, up_grad, down_1, far_rows)
    part = width // blocks
    mixed, rest = sum_groups(ids, summed, out_own, part)
    mixed_own = across(mixed).reshape(width, 2 * part)
    block_out = block_result(ids, hidden, after(returned, rest), column)
    mixed_own = after(mixed_own, block_out, far_arrived)

    rest_own = across(after(rest, mixed_own)).reshape(width, 2 * part)
    input_grad, attn_gain_part = input_back(
        ids, rows, gain_a, grad_hidden, (pieces[0], near[0], after(far_arrived, mixed_own))
    )
    gains = jnp.concatenate([attn_gain_part, ffn_gain_part], axis=0)
    gains = sum_along(gains + swap(gains, "seq", 1), "expert")
    mixed_all = spread_over_seq(mixed_own, gains)
    qkv_grad = widen_columns(ids, mixed_all, 0, 1, 3 * width)
    out_grad = widen_rows(ids, after_all(mixed_all, qkv_grad), groups)
    rest_own = after(rest_own, out_grad)
    down_left = after(activated, rest_own)
    down_grad = unit_grads(ids, [down_left], [grads_in], 0, [(near_1[1], (down_0, down_1))], f32)[0]
    gains = gains + swap(after(gains, rest_own), "seq", 2)
    rest_all = spread_over_seq(rest_own, gains, down_grad)
    qkv_grad = widen_columns(ids, rest_all, 1, 2, 3 * width, qkv_grad)

    return (
        block_out.reshape(inputs.shape),
        input_grad.reshape(inputs.shape),
        qkv_grad,
        out_grad,
        gains[0],
        gains[1],
        up_grad[None],
        down_grad[None],
    )


def solution(mesh):
    tokens = P("expert", "seq", None)
    units = P("expert", "seq", None)
    in_specs = (tokens, P(), P(), P(), P(), units, units, P("expert", "seq"), tokens)
    out_specs = (tokens, tokens, P(), P(), P(), P(), units, units)
    return jax.shard_map(shards, mesh=mesh, in_specs=in_specs, out_specs=out_specs, check_vma=False)
```

```python
import jax
import jax.numpy as jnp
from jax import lax
from jax.experimental import pallas as pl
from jax.experimental.pallas import tpu as pltpu
from jax.sharding import PartitionSpec as P

HEAD_DIM = 64
EPSILON = 1e-06
SCORE_SCALE = 0.125 * 1.4426950408889634
bf16, f32 = jnp.bfloat16, jnp.float32

NN = (((1,), (0,)), ((), ()))
NT = (((1,), (1,)), ((), ()))
TN = (((0,), (0,)), ((), ()))


def dot(left, right, dims=NN):
    return lax.dot_general(left, right, dims, preferred_element_type=f32)


def sds(shape, dtype):
    return jax.ShapeDtypeStruct(shape, dtype)


def whole(shape):
    return pl.BlockSpec(shape, lambda *_: (0,) * len(shape))


def kernel_call(body, grid, ids, ins, outs, scratch=(), vmem=60, aliases=None):
    in_specs = [whole(a.shape) if sp is None else sp for a, sp in ins]
    out_specs = [whole(sh) if sp is None else sp for sh, _, sp in outs]
    return pl.pallas_call(
        body,
        grid_spec=pltpu.PrefetchScalarGridSpec(
            num_scalar_prefetch=1,
            grid=grid,
            in_specs=in_specs,
            out_specs=out_specs,
            scratch_shapes=list(scratch),
        ),
        out_shape=[sds(sh, dt) for sh, dt, _ in outs],
        input_output_aliases=aliases or {},
        compiler_params=pltpu.CompilerParams(
            vmem_limit_bytes=vmem << 20, dimension_semantics=("arbitrary",) * len(grid)
        ),
        cost_estimate=pl.CostEstimate(flops=1, bytes_accessed=1, transcendentals=0),
    )(ids, *[a for a, _ in ins])


def swap(value, axis, step):
    size = lax.axis_size(axis)
    return lax.ppermute(value, axis, [(i, i ^ step) for i in range(size)])


def norm_scale(values):
    return lax.rsqrt(jnp.mean(values * values, axis=-1, keepdims=True) + EPSILON)


def route(ids, routes, rows, groups, capacity):
    tokens, width = rows.shape
    slots = groups * capacity

    def body(ids_ref, routes_ref, rows_ref, slot_ref, column_ref, send_ref):
        route_row = routes_ref[...]
        named = lax.broadcasted_iota(jnp.int32, (groups, tokens), 0) == route_row
        ones = jnp.where(named, 1.0, 0.0)
        earlier = lax.broadcasted_iota(jnp.int32, (tokens, tokens), 0)
        later = lax.broadcasted_iota(jnp.int32, (tokens, tokens), 1)
        upto = jnp.where(earlier <= later, 1.0, 0.0)
        count = dot(ones, upto)
        place = jnp.sum(count * ones, axis=0, keepdims=True) - 1.0
        slot = route_row * capacity + place.astype(jnp.int32)
        slot_ref[...] = slot
        column_ref[...] = jnp.transpose(jnp.broadcast_to(slot.astype(f32), (128, tokens)))
        pick = lax.broadcasted_iota(jnp.int32, (slots, tokens), 0) == slot
        laid = dot(jnp.where(pick, 1.0, 0.0).astype(bf16), rows_ref[...])
        send_ref[...] = laid.astype(bf16)

    return kernel_call(
        body,
        (1,),
        ids,
        [(routes, None), (rows, None)],
        [
            ((1, tokens), jnp.int32, None),
            ((tokens, 128), f32, None),
            ((slots, width), bf16, None),
        ],
    )


def to_groups(rows):
    groups = lax.axis_size("expert")
    cut = rows.reshape(groups, rows.shape[0] // groups, rows.shape[1])
    return lax.all_to_all(cut, "expert", split_axis=0, concat_axis=0, tiled=True).reshape(rows.shape)


def one_hot_columns(column, slots):
    wide = jnp.concatenate([column] * (slots // 128), axis=1)
    lanes = lax.broadcasted_iota(jnp.int32, wide.shape, 1).astype(f32)
    return jnp.where(wide == lanes, 1.0, 0.0).astype(bf16)


def project(ids, rows, gain, weight):
    tokens, width = rows[0].shape
    part = width // lax.axis_size("seq")
    heads = width // part
    count = len(rows)

    def body(ids_ref, gain_ref, wq_ref, wk_ref, wv_ref, *refs):
        x_refs, refs = refs[:count], refs[count:]
        for x_ref, outs in zip(x_refs, (refs[4 * r : 4 * r + 4] for r in range(count))):
            values = x_ref[...].astype(f32)
            normed = (values * norm_scale(values) * gain_ref[...]).astype(bf16)
            outs[0][...] = normed
            for w_ref, out in zip((wq_ref, wk_ref, wv_ref), outs[1:]):
                out[...] = dot(normed, w_ref[...]).astype(bf16)

    half = tokens // 2
    column = lambda which: pl.BlockSpec((width, part), lambda i, d: (0, d[0] + which * heads))
    row_spec = lambda n: pl.BlockSpec((half, n), lambda i, d: (i, 0))
    out = kernel_call(
        body,
        (2,),
        ids,
        [(gain, None)] + [(weight, column(w)) for w in range(3)] + [(r, row_spec(width)) for r in rows],
        (
            [((tokens, width), bf16, row_spec(width))]
            + [((tokens, part), bf16, row_spec(part))] * 3
        )
        * count,
    )
    return [out[4 * r : 4 * r + 4] for r in range(count)]


def head_lanes(block, head):
    lanes = lax.broadcasted_iota(jnp.int32, block.shape, 1)
    inside = (lanes >= head * HEAD_DIM) & (lanes < (head + 1) * HEAD_DIM)
    return jnp.where(inside, block, jnp.zeros_like(block))


def fold_rows(values, how):
    return how(values.reshape(values.shape[0] // 8, 8, values.shape[1]), axis=0)


def attention(ids, queries, keys, values):
    blocks = len(queries)
    tokens, part = queries[0].shape
    length = tokens // 2
    heads = part // HEAD_DIM
    total = blocks * length

    def body(ids_ref, *refs):
        ins, refs = refs[: 3 * blocks], refs[3 * blocks :]
        out_refs, refs = refs[:blocks], refs[blocks:]
        ot_ref, lse_ref, q_all, k_all, vt_all, stacked, scores, result = refs
        me = ids_ref[0]
        for j in range(blocks):
            rows = pl.ds(pl.multiple_of((me ^ j) * length, length), length)
            q_all[rows, :] = ins[j][...]
            k_all[rows, :] = ins[blocks + j][...]
            vt_all[:, rows] = jnp.transpose(ins[2 * blocks + j][...].astype(f32)).astype(bf16)
        hidden = lax.broadcasted_iota(jnp.int32, (length, length), 0) > lax.broadcasted_iota(
            jnp.int32, (length, length), 1
        )
        for qa in range(blocks):
            here = slice(qa * length, (qa + 1) * length)
            q_block = q_all[here, :]
            for h in range(heads):
                stacked[h * length : (h + 1) * length, :] = head_lanes(q_block, h)
            for h in range(heads):
                lanes = slice(h * length, (h + 1) * length)
                most = None
                for kb in range(qa + 1):
                    there = slice(kb * length, (kb + 1) * length)
                    found = dot(k_all[there, :], stacked[lanes, :], NT)
                    if kb == qa:
                        found = jnp.where(hidden, -1e30, found)
                    scores[there, lanes] = found
                    top = fold_rows(found, jnp.max)
                    most = top if most is None else jnp.maximum(most, top)
                peak = jnp.max(most, axis=0, keepdims=True) * SCORE_SCALE
                summed, gathered = None, None
                for kb in range(qa + 1):
                    there = slice(kb * length, (kb + 1) * length)
                    raised = jnp.exp2(scores[there, lanes] * SCORE_SCALE - peak)
                    part_sum = fold_rows(raised, jnp.sum)
                    summed = part_sum if summed is None else summed + part_sum
                    piece = dot(
                        vt_all[h * HEAD_DIM : (h + 1) * HEAD_DIM, there], raised.astype(bf16)
                    )
                    gathered = piece if gathered is None else gathered + piece
                weight = jnp.sum(summed, axis=0, keepdims=True)
                ot_ref[0, h * HEAD_DIM : (h + 1) * HEAD_DIM, here] = gathered * (1.0 / weight)
                lse_ref[0, qa : qa + 1, lanes] = peak + jnp.log2(weight)
            result[here, :] = jnp.transpose(ot_ref[0, :, here]).astype(bf16)
        for j in range(blocks):
            rows = pl.ds(pl.multiple_of((me ^ j) * length, length), length)
            out_refs[j][...] = result[rows, :]

    spec = pl.BlockSpec((length, part), lambda i, d: (i, 0))
    out = kernel_call(
        body,
        (2,),
        ids,
        [(a, spec) for a in (*queries, *keys, *values)],
        [((tokens, part), bf16, spec)] * blocks
        + [
            ((2, part, total), f32, pl.BlockSpec((1, part, total), lambda i, d: (i, 0, 0))),
            (
                (2, blocks, heads * length),
                f32,
                pl.BlockSpec((1, blocks, heads * length), lambda i, d: (i, 0, 0)),
            ),
        ],
        [
            pltpu.VMEM((total, part), bf16),
            pltpu.VMEM((total, part), bf16),
            pltpu.VMEM((part, total), bf16),
            pltpu.VMEM((heads * length, part), bf16),
            pltpu.VMEM((total, heads * length), f32),
            pltpu.VMEM((total, part), bf16),
        ],
    )
    return out[:blocks], out[blocks], out[blocks + 1]


def attention_back(ids, queries, keys, values, grads, ot, lse):
    blocks = len(queries)
    tokens, part = queries[0].shape
    length = tokens // 2
    heads = part // HEAD_DIM
    total = blocks * length

    def body(ids_ref, *refs):
        ins, refs = refs[: 4 * blocks], refs[4 * blocks :]
        ot_ref, lse_ref, refs = refs[0], refs[1], refs[2:]
        out_refs, refs = refs[:blocks], refs[blocks:]
        q_all, k_all, v_all, g_all, kt_all, q_stack, g_stack, low, ds_low, dk, dv, dqt, dq = refs
        me = ids_ref[0]
        for j in range(blocks):
            rows = pl.ds(pl.multiple_of((me ^ j) * length, length), length)
            q_all[rows, :] = ins[j][...]
            k_all[rows, :] = ins[blocks + j][...]
            v_all[rows, :] = ins[2 * blocks + j][...]
            g_all[rows, :] = ins[3 * blocks + j][...]
            kt_all[:, rows] = jnp.transpose(ins[blocks + j][...].astype(f32)).astype(bf16)
        dk[...] = jnp.zeros_like(dk)
        dv[...] = jnp.zeros_like(dv)
        hidden = lax.broadcasted_iota(jnp.int32, (length, length), 0) > lax.broadcasted_iota(
            jnp.int32, (length, length), 1
        )
        for qa in range(blocks):
            here = slice(qa * length, (qa + 1) * length)
            q_block, g_block = q_all[here, :], g_all[here, :]
            for h in range(heads):
                lanes = slice(h * length, (h + 1) * length)
                q_stack[lanes, :] = head_lanes(q_block, h)
                g_stack[lanes, :] = head_lanes(g_block, h)
            product = jnp.transpose(g_block.astype(f32)) * ot_ref[0, :, here]
            totals = [
                jnp.sum(product[h * HEAD_DIM : (h + 1) * HEAD_DIM], axis=0, keepdims=True)
                for h in range(heads)
            ]
            for kb in range(qa + 1):
                there = slice(kb * length, (kb + 1) * length)
                for h in range(heads):
                    lanes = slice(h * length, (h + 1) * length)
                    found = dot(k_all[there, :], q_stack[lanes, :], NT)
                    if kb == qa:
                        found = jnp.where(hidden, -1e30, found)
                    probs = jnp.exp2(found * SCORE_SCALE - lse_ref[0, qa : qa + 1, lanes])
                    grad_probs = dot(v_all[there, :], g_stack[lanes, :], NT)
                    low[:, lanes] = probs.astype(bf16)
                    ds_low[:, lanes] = (probs * (grad_probs - totals[h])).astype(bf16)
                dv[there, :] += dot(low[...], g_stack[...])
                dk[there, :] += dot(ds_low[...], q_stack[...])
                for h in range(heads):
                    lanes = slice(h * length, (h + 1) * length)
                    rows = slice(h * HEAD_DIM, (h + 1) * HEAD_DIM)
                    piece = dot(kt_all[rows, there], ds_low[:, lanes])
                    if kb == 0:
                        dqt[rows, :] = piece
                    else:
                        dqt[rows, :] += piece
            dq[here, :] = (0.125 * jnp.transpose(dqt[...])).astype(bf16)
        for j in range(blocks):
            rows = pl.ds(pl.multiple_of((me ^ j) * length, length), length)
            out_refs[j][:, 0:part] = dq[rows, :]
            out_refs[j][:, part : 2 * part] = (0.125 * dk[rows, :]).astype(bf16)
            out_refs[j][:, 2 * part : 3 * part] = dv[rows, :].astype(bf16)

    spec = pl.BlockSpec((length, part), lambda i, d: (i, 0))
    return kernel_call(
        body,
        (2,),
        ids,
        [(a, spec) for a in (*queries, *keys, *values, *grads)]
        + [
            (ot, pl.BlockSpec((1, part, total), lambda i, d: (i, 0, 0))),
            (lse, pl.BlockSpec((1, blocks, heads * length), lambda i, d: (i, 0, 0))),
        ],
        [((tokens, 3 * part), bf16, pl.BlockSpec((length, 3 * part), lambda i, d: (i, 0)))]
        * blocks,
        [pltpu.VMEM((total, part), bf16)] * 4
        + [
            pltpu.VMEM((part, total), bf16),
            pltpu.VMEM((heads * length, part), bf16),
            pltpu.VMEM((heads * length, part), bf16),
            pltpu.VMEM((length, heads * length), bf16),
            pltpu.VMEM((length, heads * length), bf16),
            pltpu.VMEM((total, part), f32),
            pltpu.VMEM((total, part), f32),
            pltpu.VMEM((part, length), f32),
            pltpu.VMEM((total, part), bf16),
        ],
    )


def head_rows(weight, j):
    part = weight.shape[0] // lax.axis_size("seq")
    return (weight, pl.BlockSpec((part, weight.shape[1]), lambda i, d: (d[0] ^ j, 0)))


def attention_out(ids, rows, attended, weight, gain, slot, groups, capacity):
    tokens, width = rows.shape
    slots = groups * capacity
    blocks = len(attended)

    def body(ids_ref, x_ref, gain_ref, slot_ref, *refs):
        att, weights, (h_ref, send_ref) = refs[:blocks], refs[blocks : 2 * blocks], refs[2 * blocks :]
        hidden = x_ref[...].astype(f32)
        for j in range(blocks):
            hidden += dot(att[j][...], weights[j][...])
        h_ref[...] = hidden
        normed = (hidden * norm_scale(hidden) * gain_ref[...]).astype(bf16)
        pick = lax.broadcasted_iota(jnp.int32, (slots, tokens), 0) == slot_ref[...]
        laid = dot(jnp.where(pick, 1.0, 0.0).astype(bf16), normed)
        send_ref[...] = laid.astype(bf16)

    return kernel_call(
        body,
        (1,),
        ids,
        [(rows, None), (gain, None), (slot, None)]
        + [(a, None) for a in attended]
        + [head_rows(weight, j) for j in range(blocks)],
        [((tokens, width), f32, None), ((slots, width), bf16, None)],
    )


def normal_parts(values):
    below = 0.5 + 0.5 * lax.erf(values * 0.7071067811865476)
    fall = jnp.exp2(values * values * -0.7213475204444817)
    return below, values * fall * 0.3989422804014327


def unit_specs(weights, step):
    starts = [0]
    for w in weights:
        starts.append(starts[-1] + w.shape[0] // step)

    def spec(j):
        last = starts[j + 1] - starts[j] - 1
        return pl.BlockSpec(
            (step, weights[j].shape[1]), lambda i, d: (jnp.clip(i - starts[j], 0, last), 0)
        )

    return starts, [(w, spec(j)) for j, w in enumerate(weights)]


def take_units(refs, starts, held):
    here = pl.program_id(0)
    for j, ref in enumerate(refs):

        @pl.when((here >= starts[j]) & (here < starts[j + 1]))
        def _():
            held[...] = ref[...]


def expert_grad_act(ids, grads, weights):
    slots, width = grads.shape
    step = 512
    starts, units = unit_specs(weights, step)
    hidden = starts[-1] * step

    def body(ids_ref, g_ref, *refs):
        w_refs, (out_ref, held) = refs[:-2], refs[-2:]
        take_units(w_refs, starts, held)
        out_ref[...] = dot(g_ref[...], held[...], NT)

    return kernel_call(
        body,
        (hidden // step,),
        ids,
        [(grads, None)] + units,
        [((slots, hidden), f32, pl.BlockSpec((slots, step), lambda i, d: (0, i)))],
        [pltpu.VMEM((step, width), bf16)],
    )[0]


def expert_main(ids, rows_in, grad_act, weights):
    slots, width = rows_in.shape
    step, rows = 512, 256
    units = [(j, first) for j, w in enumerate(weights) for first in range(0, w.shape[0], step)]
    hidden = len(units) * step

    def body(ids_ref, x_ref, ga_ref, *refs):
        w_refs, (act_ref, gp_ref, out_ref) = refs[:-3], refs[-3:]

        def held(c):
            j, first = units[c]
            return w_refs[j][first : first + step, :]

        pre, late, total = dot(x_ref[...], held(0), NT), None, None
        for c in range(len(units)):
            later = dot(x_ref[...], held(c + 1), NT) if c + 1 < len(units) else None
            part = slice(c * step, (c + 1) * step)
            below, dense = normal_parts(pre)
            act_ref[:, part] = (pre * below).astype(bf16)
            grad_pre = (ga_ref[:, part] * (below + dense)).astype(bf16)
            gp_ref[:, part] = grad_pre
            if late is not None:
                piece = dot(late, held(c - 1))
                total = piece if total is None else total + piece
            pre, late = later, grad_pre
        out_ref[...] = (total + dot(late, held(len(units) - 1))).astype(bf16)

    block = lambda n: pl.BlockSpec((rows, n), lambda i, d: (i, 0))
    return kernel_call(
        body,
        (slots // rows,),
        ids,
        [(rows_in, block(width)), (grad_act, block(hidden))] + [(w, None) for w in weights],
        [((slots, hidden), bf16, block(hidden))] * 2 + [((slots, width), bf16, block(width))],
    )


def expert_out(ids, activated, weights):
    slots, hidden = activated.shape
    width = weights[0].shape[1]
    rows = 256

    def body(ids_ref, act_ref, *refs):
        total, first = None, 0
        for ref in refs[:-1]:
            piece = dot(act_ref[:, first : first + ref.shape[0]], ref[...])
            total = piece if total is None else total + piece
            first += ref.shape[0]
        refs[-1][...] = total.astype(bf16)

    block = lambda n: pl.BlockSpec((rows, n), lambda i, d: (i, 0))
    return kernel_call(
        body,
        (slots // rows,),
        ids,
        [(activated, block(hidden))] + [(w, None) for w in weights],
        [((slots, width), bf16, block(width))],
    )[0]


def unit_grads(ids, lefts, rights, j, adds, kind, cuts=None):
    slots, width = rights[0].shape
    units = lefts[0].shape[1] // lax.axis_size("seq")
    step = 256
    steps = units // step
    pairs = len(lefts)
    block = pl.BlockSpec((step, width), lambda i, d: (i, 0))
    upto = lambda c: pl.BlockSpec((step, width), lambda i, d: (jnp.minimum(i, c - 1), 0))
    beyond = lambda c: pl.BlockSpec((step, width), lambda i, d: (jnp.maximum(i - c, 0), 0))
    add_ins, splits = [], []
    for pair in adds:
        for a in pair:
            if isinstance(a, tuple):
                c = a[0].shape[0] // step
                add_ins += [(a[0], upto(c)), (a[1], beyond(c))]
                splits.append(c)
            else:
                add_ins.append((a, block))
                splits.append(0)
    more = len(adds[0])

    def body(ids_ref, *refs):
        l_refs, r_refs, refs = refs[:pairs], refs[pairs : 2 * pairs], refs[2 * pairs :]
        add_refs, out_refs = list(refs[: len(add_ins)]), refs[len(add_ins) :]
        here = pl.program_id(0)
        for p in range(pairs):
            total = dot(l_refs[p][...], r_refs[p][...], TN)
            for c in splits[p * more : (p + 1) * more]:
                if c:
                    one, two = add_refs.pop(0), add_refs.pop(0)
                    total += jnp.where(here < c, one[...], two[...]).astype(f32)
                else:
                    total += add_refs.pop(0)[...].astype(f32)
            if not cuts:
                out_refs[p][...] = total.astype(kind)
                continue

            @pl.when(here < cuts[p])
            def _():
                out_refs[2 * p][...] = total.astype(kind)

            @pl.when(here >= cuts[p])
            def _():
                out_refs[2 * p + 1][...] = total.astype(kind)

    outs = [((units, width), kind, block)] * pairs
    if cuts:
        outs = []
        for c in cuts:
            outs += [((c * step, width), kind, upto(c)), ((units - c * step, width), kind, beyond(c))]
    return kernel_call(
        body,
        (steps,),
        ids,
        [(left, pl.BlockSpec((slots, step), lambda i, d: (0, j * steps + i))) for left in lefts]
        + [(right, None) for right in rights]
        + add_ins,
        outs,
    )


def block_result(ids, hidden, returned, column):
    tokens, width = hidden.shape
    slots = returned.shape[0]

    def body(ids_ref, h_ref, c_ref, back_ref, out_ref):
        pick = one_hot_columns(c_ref[...], slots)
        out_ref[...] = (h_ref[...] + dot(pick, back_ref[...])).astype(bf16)

    return kernel_call(
        body,
        (1,),
        ids,
        [(hidden, None), (column, None), (returned, None)],
        [((tokens, width), bf16, None)],
    )[0]


def norm_back(values, gain, grads):
    scale = norm_scale(values)
    scaled = grads * gain
    along = jnp.mean(values * scaled, axis=-1, keepdims=True)
    through = scale * scaled - values * (scale * scale * scale * along)
    return through, jnp.sum(grads * (values * scale), axis=0, keepdims=True)


def hidden_back(ids, hidden, cotangent, gain, returned, column, weight, attended):
    tokens, width = hidden.shape
    slots = returned.shape[0]
    blocks = lax.axis_size("seq")
    part = width // blocks
    kinds = [f32 if j % 2 == 0 else bf16 for j in range(blocks)]

    def body(ids_ref, h_ref, c_ref, gain_ref, col_ref, back_ref, *refs):
        weights, att, refs = refs[:blocks], refs[blocks : 2 * blocks], refs[2 * blocks :]
        (gh_ref, gain_out), att_refs, grad_refs = refs[:2], refs[2 : 2 + blocks], refs[2 + blocks :]
        pick = one_hot_columns(col_ref[...], slots)
        grads = dot(pick, back_ref[...])
        through, gain_grad = norm_back(h_ref[...], gain_ref[...], grads)
        grad_hidden = c_ref[...].astype(f32) + through
        gh_ref[...] = grad_hidden
        low = grad_hidden.astype(bf16)
        gain_out[...] = gain_grad
        for j in range(blocks):
            att_refs[j][...] = dot(low, weights[j][...], NT).astype(bf16)
        for j in range(blocks):
            grad_refs[j][...] = dot(att[j][...], low, TN).astype(kinds[j])

    out = kernel_call(
        body,
        (1,),
        ids,
        [(hidden, None), (cotangent, None), (gain, None), (column, None), (returned, None)]
        + [head_rows(weight, j) for j in range(blocks)]
        + [(a, None) for a in attended],
        [((tokens, width), f32, None), ((1, width), f32, None)]
        + [((tokens, part), bf16, None)] * blocks
        + [((part, width), kind, None) for kind in kinds],
    )
    return out[0], out[1], out[2 : 2 + blocks], out[2 + blocks :]


def projection_back(ids, grads, weight):
    blocks = len(grads)
    tokens = grads[0].shape[0]
    width = weight.shape[0]
    part = grads[0].shape[1] // 3
    heads = width // part
    kinds = [f32 if j % 2 == 0 else bf16 for j in range(blocks)]

    def body(ids_ref, *refs):
        g_refs, w_refs, out_refs = refs[:blocks], refs[blocks : blocks + 3], refs[blocks + 3 :]
        for j in (1, 3, 2, 0):
            total = None
            for w in range(3):
                piece = dot(g_refs[j][:, w * part : (w + 1) * part], w_refs[w][...], NT)
                total = piece if total is None else total + piece
            out_refs[j][...] = total.astype(kinds[j])

    column = lambda which: pl.BlockSpec((width, part), lambda i, d: (0, d[0] + which * heads))
    return kernel_call(
        body,
        (1,),
        ids,
        [(g, None) for g in grads] + [(weight, column(w)) for w in range(3)],
        [((tokens, width), kind, None) for kind in kinds],
    )


def projection_grad(ids, normed, grads, groups):
    blocks = len(normed)
    tokens, columns = grads[0].shape
    width = normed[0].shape[1]
    step, height = 256, width // groups
    pairs = step // height // 2

    def body(ids_ref, *refs):
        n_refs, g_refs = refs[:blocks], refs[blocks : 2 * blocks]
        kept_ref, sent_ref, held = refs[2 * blocks :]
        total = dot(n_refs[0][...], g_refs[0][...], TN)
        for j in range(1, blocks):
            total += dot(n_refs[j][...], g_refs[j][...], TN)
        held[...] = total
        odd = ids_ref[1] % 2
        for b in range(pairs):
            kept = pl.multiple_of(2 * b * height + odd * height, 8)
            sent = pl.multiple_of((2 * b + 1) * height - odd * height, 8)
            kept_ref[b] = held[pl.ds(kept, height), :]
            sent_ref[b] = held[pl.ds(sent, height), :].astype(bf16)

    block = pl.BlockSpec((pairs, height, columns), lambda i, d: (i, 0, 0))
    return kernel_call(
        body,
        (width // step,),
        ids,
        [(n, pl.BlockSpec((tokens, step), lambda i, d: (0, i))) for n in normed]
        + [(g, None) for g in grads],
        [((groups // 2, height, columns), f32, block), ((groups // 2, height, columns), bf16, block)],
        [pltpu.VMEM((step, columns), f32)],
    )


def sum_groups(ids, pieces, out_pieces, part):
    rows, width = pieces.shape[1:]
    groups, height, total = out_pieces.shape

    def body(ids_ref, in_ref, out_in_ref, mixed_ref, rest_ref):
        low = sum(in_ref[k].astype(f32) for k in range(pieces.shape[0])).astype(bf16)
        out = sum(out_in_ref[k].astype(f32) for k in range(groups))
        tall = [out[:, c * part : (c + 1) * part] for c in range(total // part)]
        tall = jnp.concatenate(tall, axis=0).astype(bf16)
        for k in range(groups):
            mixed_ref[k, :, :part] = low[:, :part]
            mixed_ref[k, :, part:] = tall
            rest_ref[k] = low[:, part:]

    return kernel_call(
        body,
        (1,),
        ids,
        [(pieces, None), (out_pieces, None)],
        [((groups, rows, 2 * part), bf16, None), ((groups, rows, width - part), bf16, None)],
        vmem=28,
    )


def across(value, alike=False):
    size = lax.axis_size("expert")
    sets = [list(range(p, size, 2)) for p in range(2)] if alike else None
    return lax.all_to_all(
        value, "expert", split_axis=0, concat_axis=0, tiled=True, axis_index_groups=sets
    )


def after(value, *earlier):
    return lax.optimization_barrier((value, *earlier))[0]


def after_all(values, *earlier):
    return lax.optimization_barrier((*values, *earlier))[: len(values)]


def spread_over_seq(value, *earlier):
    far = after(swap(value, "seq", 2), *earlier)
    return [value, swap(value, "seq", 1), far, swap(far, "seq", 1)]


def widen_columns(ids, pieces, first, count, total, out=None):
    blocks = len(pieces)
    rows, columns = pieces[0].shape
    part = total // 3 // blocks
    step = 256

    def body(ids_ref, *refs):
        me = ids_ref[0]
        for j in range(blocks):
            at = pl.multiple_of((me ^ j) * part, part)
            refs[-1][:, pl.ds(at, part)] = refs[j][...].astype(f32)

    spec = pl.BlockSpec((step, part * blocks), lambda i, w, d: (i, first + w))
    ins = [(p, pl.BlockSpec((step, part), lambda i, w, d: (i, w))) for p in pieces]
    aliases = {}
    if out is not None:
        ins.append((out, pl.BlockSpec(memory_space=pl.ANY)))
        aliases = {len(ins): 0}
    return kernel_call(
        body,
        (rows // step, count),
        ids,
        ins,
        [((rows, total), f32, spec)],
        aliases=aliases,
        vmem=28,
    )[0]


def widen_rows(ids, pieces, groups):
    blocks = len(pieces)
    width = pieces[0].shape[0]
    part = pieces[0].shape[1] // 2
    height, tall = part // groups, width // groups

    def body(ids_ref, *refs):
        me = ids_ref[0]
        for j in range(blocks):
            for e in range(groups):
                cut = refs[j][e * tall : (e + 1) * tall, :].astype(f32)
                at = pl.multiple_of((me ^ j) * part, part) + e * height
                for c in range(blocks):
                    refs[blocks][pl.ds(pl.multiple_of(at, 8), height), c * part : (c + 1) * part] = cut[
                        c * height : (c + 1) * height
                    ]

    return kernel_call(
        body,
        (1,),
        ids,
        [(p, pl.BlockSpec((width, part), lambda i, d: (0, 1))) for p in pieces],
        [((width, part * blocks), f32, None)],
        vmem=28,
    )[0]


def input_back(ids, rows, gain, grad_hidden, pieces):
    tokens, width = rows.shape

    def body(ids_ref, x_ref, gain_ref, gh_ref, a_ref, b_ref, c_ref, out_ref, gain_out):
        grads = a_ref[...] + b_ref[...].astype(f32) + c_ref[...].astype(f32)
        through, gain_grad = norm_back(x_ref[...].astype(f32), gain_ref[...], grads)
        out_ref[...] = gh_ref[...] + through
        gain_out[...] = gain_grad

    return kernel_call(
        body,
        (1,),
        ids,
        [(rows, None), (gain, None), (grad_hidden, None)] + [(a, None) for a in pieces],
        [((tokens, width), f32, None), ((1, width), f32, None)],
    )


def sum_along(value, axis):
    step = 1
    while step < lax.axis_size(axis):
        value = value + swap(value, axis, step)
        step *= 2
    return value


def shards(
    inputs,
    query_key_value_weight,
    output_weight,
    gain_attn,
    gain_ffn,
    w_up,
    w_down,
    expert_of,
    cotangent,
):
    groups = lax.axis_size("expert")
    blocks = lax.axis_size("seq")
    seq_count, local_len, width = inputs.shape
    tokens = seq_count * local_len
    capacity = max(2, 2 * tokens // groups)
    ids = jnp.stack([lax.axis_index("seq"), lax.axis_index("expert")]).astype(jnp.int32)
    gain_a, gain_f = gain_attn.reshape(1, width), gain_ffn.reshape(1, width)
    rows = inputs.reshape(tokens, width)
    cot = cotangent.reshape(tokens, width)

    down, up = w_down[0], w_up[0]
    rows_1 = swap(rows, "seq", 1)
    split = 5 * tokens // 8
    far_0, far_1 = swap(rows[:split], "seq", 2), swap(rows[split:], "seq", 2)
    down_near, up_near = swap(down, "seq", 1), swap(up, "seq", 1)
    first = project(ids, (rows, rows_1), gain_a, query_key_value_weight)
    slot, column, send = route(
        ids, expert_of.reshape(1, tokens), after(cot, first[0][0]), groups, capacity
    )
    send = after(send, far_0, down_near, up_near)
    rows_2 = after(jnp.concatenate([far_0, far_1], axis=0), send)
    grads_in = to_groups(send)
    rows_3 = swap(rows_2, "seq", 1)

    cut = up.shape[0] // 2
    up_far = swap(after(up[:cut], rows_2), "seq", 2)
    second = project(ids, (rows_2, rows_3), gain_a, query_key_value_weight)
    normed, queries, keys, values = (list(p) for p in zip(*first, *second))
    out, ot, lse = attention(ids, queries, keys, values)
    out = lax.optimization_barrier((*out, up_far))[:blocks]
    attended = [out[0]] + [swap(out[j], "seq", j) for j in range(1, blocks)]
    down_far = swap(after(down, *attended), "seq", 2)
    up_more = swap(after(up[cut:], *attended), "seq", 2)
    hidden, send = attention_out(
        ids, rows, attended, output_weight, gain_f, slot, groups, capacity
    )
    up_near_far = swap(after(up_far, send), "seq", 1)
    down_all = [down, down_near, down_far, swap(down_far, "seq", 1)]

    rows_in = to_groups(after(send, grads_in))
    grad_act = expert_grad_act(ids, grads_in, down_all)
    up_more = after(up_more, grad_act)
    up_all = [up, up_near, up_far, up_more, up_near_far, swap(up_more, "seq", 1)]
    activated, grad_pre, back = expert_main(ids, rows_in, grad_act, up_all)
    returned_grad = to_groups(back)
    left, right = (grad_pre, activated), (rows_in, grads_in)
    none = ((), ())
    near_3 = [swap(p, "seq", 1) for p in unit_grads(ids, left, right, 3, none, bf16)]
    near_1 = [swap(p, "seq", 1) for p in unit_grads(ids, left, right, 1, none, bf16)]
    up_0, up_1, down_0, down_1 = unit_grads(
        ids, left, right, 2, [(p,) for p in near_3], bf16, (1, 1)
    )
    up_0 = swap(up_0, "seq", 2)
    down_0 = swap(after(down_0, up_0), "seq", 2)
    result = expert_out(ids, after(activated, down_1), down_all)

    returned_grad = after(returned_grad, result, up_0, *near_1)
    returned = to_groups(after(result, returned_grad))
    grad_hidden, ffn_gain_part, grad_att, out_parts = hidden_back(
        ids, hidden, cot, gain_f, returned_grad, column, output_weight, attended
    )
    grad_att = after_all(grad_att, down_0)
    grad_att = [grad_att[0]] + [swap(grad_att[j], "seq", j) for j in range(1, blocks)]
    near_out = [swap(after(out_parts[j], grad_att[1]), "seq", 1) for j in (1, 3)]
    far_out = (out_parts[2] + near_out[1].astype(f32)).astype(bf16)
    far_out = swap(after(far_out, *grad_att), "seq", 2)
    up_1 = swap(after(up_1, *grad_att), "seq", 2)
    down_1 = swap(after(down_1, *grad_att), "seq", 2)
    grad_proj = attention_back(ids, queries, keys, values, grad_att, ot, lse)
    grad_proj = after_all(grad_proj, far_out)

    kept, sent = projection_grad(ids, normed, grad_proj, groups)
    other = swap(sent, "expert", 1)
    out_part = (out_parts[0] + near_out[0].astype(f32) + far_out.astype(f32)).astype(bf16)
    height = out_part.shape[0] // groups
    out_own = across(after(out_part, returned, sent).reshape(groups, height, width))
    pieces = projection_back(ids, after_all(grad_proj, sent), query_key_value_weight)
    near = [swap(pieces[j], "seq", 1) for j in (1, 3)]
    far_rows = (pieces[2] + near[1].astype(f32)).astype(bf16)
    out_own = after(out_own, up_1, pieces[0])
    summed = across(after((kept + other.astype(f32)).astype(bf16), out_own), alike=True)
    far_arrived = swap(far_rows, "seq", 2)
    up_left = after(grad_pre, out_own)
    up_grad = unit_grads(ids, [up_left], [rows_in], 0, [(near_1[0], (up_0, up_1))], f32)[0]
    summed = after(summed, up_grad, down_1, far_rows)
    part = width // blocks
    mixed, rest = sum_groups(ids, summed, out_own, part)
    mixed_own = across(mixed).reshape(width, 2 * part)
    block_out = block_result(ids, hidden, after(returned, rest), column)
    mixed_own = after(mixed_own, block_out, far_arrived)

    rest_own = across(after(rest, mixed_own)).reshape(width, 2 * part)
    input_grad, attn_gain_part = input_back(
        ids, rows, gain_a, grad_hidden, (pieces[0], near[0], after(far_arrived, mixed_own))
    )
    gains = jnp.concatenate([attn_gain_part, ffn_gain_part], axis=0)
    gains = sum_along(gains + swap(gains, "seq", 1), "expert")
    mixed_all = spread_over_seq(mixed_own, gains)
    qkv_grad = widen_columns(ids, mixed_all, 0, 1, 3 * width)
    out_grad = widen_rows(ids, after_all(mixed_all, qkv_grad), groups)
    rest_own = after(rest_own, out_grad)
    down_left = after(activated, rest_own)
    down_grad = unit_grads(ids, [down_left], [grads_in], 0, [(near_1[1], (down_0, down_1))], f32)[0]
    gains = gains + swap(after(gains, rest_own), "seq", 2)
    rest_all = spread_over_seq(rest_own, gains, down_grad)
    qkv_grad = widen_columns(ids, rest_all, 1, 2, 3 * width, qkv_grad)

    return (
        block_out.reshape(inputs.shape),
        input_grad.reshape(inputs.shape),
        qkv_grad,
        out_grad,
        gains[0],
        gains[1],
        up_grad[None],
        down_grad[None],
    )


def solution(mesh):
    tokens = P("expert", "seq", None)
    units = P("expert", "seq", None)
    in_specs = (tokens, P(), P(), P(), P(), units, units, P("expert", "seq"), tokens)
    out_specs = (tokens, tokens, P(), P(), P(), P(), units, units)
    return jax.shard_map(shards, mesh=mesh, in_specs=in_specs, out_specs=out_specs, check_vma=False)
```

```python
import jax
import jax.numpy as jnp
from jax import lax
from jax.experimental import pallas as pl
from jax.experimental.pallas import tpu as pltpu
from jax.sharding import PartitionSpec as P

HEAD_DIM = 64
EPSILON = 1e-06
SCORE_SCALE = 0.125 * 1.4426950408889634
bf16, f32 = jnp.bfloat16, jnp.float32

NN = (((1,), (0,)), ((), ()))
NT = (((1,), (1,)), ((), ()))
TN = (((0,), (0,)), ((), ()))


def dot(left, right, dims=NN):
    return lax.dot_general(left, right, dims, preferred_element_type=f32)


def sds(shape, dtype):
    return jax.ShapeDtypeStruct(shape, dtype)


def whole(shape):
    return pl.BlockSpec(shape, lambda *_: (0,) * len(shape))


def kernel_call(body, grid, ids, ins, outs, scratch=(), vmem=60, aliases=None):
    in_specs = [whole(a.shape) if sp is None else sp for a, sp in ins]
    out_specs = [whole(sh) if sp is None else sp for sh, _, sp in outs]
    return pl.pallas_call(
        body,
        grid_spec=pltpu.PrefetchScalarGridSpec(
            num_scalar_prefetch=1,
            grid=grid,
            in_specs=in_specs,
            out_specs=out_specs,
            scratch_shapes=list(scratch),
        ),
        out_shape=[sds(sh, dt) for sh, dt, _ in outs],
        input_output_aliases=aliases or {},
        compiler_params=pltpu.CompilerParams(
            vmem_limit_bytes=vmem << 20, dimension_semantics=("arbitrary",) * len(grid)
        ),
        cost_estimate=pl.CostEstimate(flops=1, bytes_accessed=1, transcendentals=0),
    )(ids, *[a for a, _ in ins])


def swap(value, axis, step):
    size = lax.axis_size(axis)
    return lax.ppermute(value, axis, [(i, i ^ step) for i in range(size)])


def norm_scale(values):
    return lax.rsqrt(jnp.mean(values * values, axis=-1, keepdims=True) + EPSILON)


def route(ids, routes, rows, groups, capacity):
    tokens, width = rows.shape
    slots = groups * capacity

    def body(ids_ref, routes_ref, rows_ref, slot_ref, column_ref, send_ref):
        route_row = routes_ref[...]
        named = lax.broadcasted_iota(jnp.int32, (groups, tokens), 0) == route_row
        ones = jnp.where(named, 1.0, 0.0)
        earlier = lax.broadcasted_iota(jnp.int32, (tokens, tokens), 0)
        later = lax.broadcasted_iota(jnp.int32, (tokens, tokens), 1)
        upto = jnp.where(earlier <= later, 1.0, 0.0)
        count = dot(ones, upto)
        place = jnp.sum(count * ones, axis=0, keepdims=True) - 1.0
        slot = route_row * capacity + place.astype(jnp.int32)
        slot_ref[...] = slot
        column_ref[...] = jnp.transpose(jnp.broadcast_to(slot.astype(f32), (128, tokens)))
        pick = lax.broadcasted_iota(jnp.int32, (slots, tokens), 0) == slot
        laid = dot(jnp.where(pick, 1.0, 0.0).astype(bf16), rows_ref[...])
        send_ref[...] = laid.astype(bf16)

    return kernel_call(
        body,
        (1,),
        ids,
        [(routes, None), (rows, None)],
        [
            ((1, tokens), jnp.int32, None),
            ((tokens, 128), f32, None),
            ((slots, width), bf16, None),
        ],
    )


def to_groups(rows):
    groups = lax.axis_size("expert")
    cut = rows.reshape(groups, rows.shape[0] // groups, rows.shape[1])
    return lax.all_to_all(cut, "expert", split_axis=0, concat_axis=0, tiled=True).reshape(rows.shape)


def one_hot_columns(column, slots):
    wide = jnp.concatenate([column] * (slots // 128), axis=1)
    lanes = lax.broadcasted_iota(jnp.int32, wide.shape, 1).astype(f32)
    return jnp.where(wide == lanes, 1.0, 0.0).astype(bf16)


def project(ids, rows, gain, weight):
    tokens, width = rows[0].shape
    part = width // lax.axis_size("seq")
    heads = width // part
    count = len(rows)

    def body(ids_ref, gain_ref, wq_ref, wk_ref, wv_ref, *refs):
        x_refs, refs = refs[:count], refs[count:]
        for x_ref, outs in zip(x_refs, (refs[4 * r : 4 * r + 4] for r in range(count))):
            values = x_ref[...].astype(f32)
            normed = (values * norm_scale(values) * gain_ref[...]).astype(bf16)
            outs[0][...] = normed
            for w_ref, out in zip((wq_ref, wk_ref, wv_ref), outs[1:]):
                out[...] = dot(normed, w_ref[...]).astype(bf16)

    half = tokens // 2
    column = lambda which: pl.BlockSpec((width, part), lambda i, d: (0, d[0] + which * heads))
    row_spec = lambda n: pl.BlockSpec((half, n), lambda i, d: (i, 0))
    out = kernel_call(
        body,
        (2,),
        ids,
        [(gain, None)] + [(weight, column(w)) for w in range(3)] + [(r, row_spec(width)) for r in rows],
        (
            [((tokens, width), bf16, row_spec(width))]
            + [((tokens, part), bf16, row_spec(part))] * 3
        )
        * count,
    )
    return [out[4 * r : 4 * r + 4] for r in range(count)]


def head_lanes(block, head):
    lanes = lax.broadcasted_iota(jnp.int32, block.shape, 1)
    inside = (lanes >= head * HEAD_DIM) & (lanes < (head + 1) * HEAD_DIM)
    return jnp.where(inside, block, jnp.zeros_like(block))


def fold_rows(values, how):
    return how(values.reshape(values.shape[0] // 8, 8, values.shape[1]), axis=0)


def attention(ids, queries, keys, values):
    blocks = len(queries)
    tokens, part = queries[0].shape
    length = tokens // 2
    heads = part // HEAD_DIM
    total = blocks * length

    def body(ids_ref, *refs):
        ins, refs = refs[: 3 * blocks], refs[3 * blocks :]
        out_refs, refs = refs[:blocks], refs[blocks:]
        ot_ref, lse_ref, q_all, k_all, vt_all, stacked, scores, result = refs
        me = ids_ref[0]
        for j in range(blocks):
            rows = pl.ds(pl.multiple_of((me ^ j) * length, length), length)
            q_all[rows, :] = ins[j][...]
            k_all[rows, :] = ins[blocks + j][...]
            vt_all[:, rows] = jnp.transpose(ins[2 * blocks + j][...].astype(f32)).astype(bf16)
        hidden = lax.broadcasted_iota(jnp.int32, (length, length), 0) > lax.broadcasted_iota(
            jnp.int32, (length, length), 1
        )
        for qa in range(blocks):
            here = slice(qa * length, (qa + 1) * length)
            q_block = q_all[here, :]
            for h in range(heads):
                stacked[h * length : (h + 1) * length, :] = head_lanes(q_block, h)
            for h in range(heads):
                lanes = slice(h * length, (h + 1) * length)
                most = None
                for kb in range(qa + 1):
                    there = slice(kb * length, (kb + 1) * length)
                    found = dot(k_all[there, :], stacked[lanes, :], NT)
                    if kb == qa:
                        found = jnp.where(hidden, -1e30, found)
                    scores[there, lanes] = found
                    top = fold_rows(found, jnp.max)
                    most = top if most is None else jnp.maximum(most, top)
                peak = jnp.max(most, axis=0, keepdims=True) * SCORE_SCALE
                summed, gathered = None, None
                for kb in range(qa + 1):
                    there = slice(kb * length, (kb + 1) * length)
                    raised = jnp.exp2(scores[there, lanes] * SCORE_SCALE - peak)
                    part_sum = fold_rows(raised, jnp.sum)
                    summed = part_sum if summed is None else summed + part_sum
                    piece = dot(
                        vt_all[h * HEAD_DIM : (h + 1) * HEAD_DIM, there], raised.astype(bf16)
                    )
                    gathered = piece if gathered is None else gathered + piece
                weight = jnp.sum(summed, axis=0, keepdims=True)
                ot_ref[0, h * HEAD_DIM : (h + 1) * HEAD_DIM, here] = gathered * (1.0 / weight)
                lse_ref[0, qa : qa + 1, lanes] = peak + jnp.log2(weight)
            result[here, :] = jnp.transpose(ot_ref[0, :, here]).astype(bf16)
        for j in range(blocks):
            rows = pl.ds(pl.multiple_of((me ^ j) * length, length), length)
            out_refs[j][...] = result[rows, :]

    spec = pl.BlockSpec((length, part), lambda i, d: (i, 0))
    out = kernel_call(
        body,
        (2,),
        ids,
        [(a, spec) for a in (*queries, *keys, *values)],
        [((tokens, part), bf16, spec)] * blocks
        + [
            ((2, part, total), f32, pl.BlockSpec((1, part, total), lambda i, d: (i, 0, 0))),
            (
                (2, blocks, heads * length),
                f32,
                pl.BlockSpec((1, blocks, heads * length), lambda i, d: (i, 0, 0)),
            ),
        ],
        [
            pltpu.VMEM((total, part), bf16),
            pltpu.VMEM((total, part), bf16),
            pltpu.VMEM((part, total), bf16),
            pltpu.VMEM((heads * length, part), bf16),
            pltpu.VMEM((total, heads * length), f32),
            pltpu.VMEM((total, part), bf16),
        ],
    )
    return out[:blocks], out[blocks], out[blocks + 1]


def attention_back(ids, queries, keys, values, grads, ot, lse):
    blocks = len(queries)
    tokens, part = queries[0].shape
    length = tokens // 2
    heads = part // HEAD_DIM
    total = blocks * length

    def body(ids_ref, *refs):
        ins, refs = refs[: 4 * blocks], refs[4 * blocks :]
        ot_ref, lse_ref, refs = refs[0], refs[1], refs[2:]
        out_refs, refs = refs[:blocks], refs[blocks:]
        q_all, k_all, v_all, g_all, kt_all, q_stack, g_stack, low, ds_low, dk, dv, dqt, dq = refs
        me = ids_ref[0]
        for j in range(blocks):
            rows = pl.ds(pl.multiple_of((me ^ j) * length, length), length)
            q_all[rows, :] = ins[j][...]
            k_all[rows, :] = ins[blocks + j][...]
            v_all[rows, :] = ins[2 * blocks + j][...]
            g_all[rows, :] = ins[3 * blocks + j][...]
            kt_all[:, rows] = jnp.transpose(ins[blocks + j][...].astype(f32)).astype(bf16)
        dk[...] = jnp.zeros_like(dk)
        dv[...] = jnp.zeros_like(dv)
        hidden = lax.broadcasted_iota(jnp.int32, (length, length), 0) > lax.broadcasted_iota(
            jnp.int32, (length, length), 1
        )
        for qa in range(blocks):
            here = slice(qa * length, (qa + 1) * length)
            q_block, g_block = q_all[here, :], g_all[here, :]
            for h in range(heads):
                lanes = slice(h * length, (h + 1) * length)
                q_stack[lanes, :] = head_lanes(q_block, h)
                g_stack[lanes, :] = head_lanes(g_block, h)
            product = jnp.transpose(g_block.astype(f32)) * ot_ref[0, :, here]
            totals = [
                jnp.sum(product[h * HEAD_DIM : (h + 1) * HEAD_DIM], axis=0, keepdims=True)
                for h in range(heads)
            ]
            for kb in range(qa + 1):
                there = slice(kb * length, (kb + 1) * length)
                for h in range(heads):
                    lanes = slice(h * length, (h + 1) * length)
                    found = dot(k_all[there, :], q_stack[lanes, :], NT)
                    if kb == qa:
                        found = jnp.where(hidden, -1e30, found)
                    probs = jnp.exp2(found * SCORE_SCALE - lse_ref[0, qa : qa + 1, lanes])
                    grad_probs = dot(v_all[there, :], g_stack[lanes, :], NT)
                    low[:, lanes] = probs.astype(bf16)
                    ds_low[:, lanes] = (probs * (grad_probs - totals[h])).astype(bf16)
                dv[there, :] += dot(low[...], g_stack[...])
                dk[there, :] += dot(ds_low[...], q_stack[...])
                for h in range(heads):
                    lanes = slice(h * length, (h + 1) * length)
                    rows = slice(h * HEAD_DIM, (h + 1) * HEAD_DIM)
                    piece = dot(kt_all[rows, there], ds_low[:, lanes])
                    if kb == 0:
                        dqt[rows, :] = piece
                    else:
                        dqt[rows, :] += piece
            dq[here, :] = (0.125 * jnp.transpose(dqt[...])).astype(bf16)
        for j in range(blocks):
            rows = pl.ds(pl.multiple_of((me ^ j) * length, length), length)
            out_refs[j][:, 0:part] = dq[rows, :]
            out_refs[j][:, part : 2 * part] = (0.125 * dk[rows, :]).astype(bf16)
            out_refs[j][:, 2 * part : 3 * part] = dv[rows, :].astype(bf16)

    spec = pl.BlockSpec((length, part), lambda i, d: (i, 0))
    return kernel_call(
        body,
        (2,),
        ids,
        [(a, spec) for a in (*queries, *keys, *values, *grads)]
        + [
            (ot, pl.BlockSpec((1, part, total), lambda i, d: (i, 0, 0))),
            (lse, pl.BlockSpec((1, blocks, heads * length), lambda i, d: (i, 0, 0))),
        ],
        [((tokens, 3 * part), bf16, pl.BlockSpec((length, 3 * part), lambda i, d: (i, 0)))]
        * blocks,
        [pltpu.VMEM((total, part), bf16)] * 4
        + [
            pltpu.VMEM((part, total), bf16),
            pltpu.VMEM((heads * length, part), bf16),
            pltpu.VMEM((heads * length, part), bf16),
            pltpu.VMEM((length, heads * length), bf16),
            pltpu.VMEM((length, heads * length), bf16),
            pltpu.VMEM((total, part), f32),
            pltpu.VMEM((total, part), f32),
            pltpu.VMEM((part, length), f32),
            pltpu.VMEM((total, part), bf16),
        ],
    )


def head_rows(weight, j):
    part = weight.shape[0] // lax.axis_size("seq")
    return (weight, pl.BlockSpec((part, weight.shape[1]), lambda i, d: (d[0] ^ j, 0)))


def attention_out(ids, rows, attended, weight, gain, slot, groups, capacity):
    tokens, width = rows.shape
    slots = groups * capacity
    blocks = len(attended)

    def body(ids_ref, x_ref, gain_ref, slot_ref, *refs):
        att, weights, (h_ref, send_ref) = refs[:blocks], refs[blocks : 2 * blocks], refs[2 * blocks :]
        hidden = x_ref[...].astype(f32)
        for j in range(blocks):
            hidden += dot(att[j][...], weights[j][...])
        h_ref[...] = hidden
        normed = (hidden * norm_scale(hidden) * gain_ref[...]).astype(bf16)
        pick = lax.broadcasted_iota(jnp.int32, (slots, tokens), 0) == slot_ref[...]
        laid = dot(jnp.where(pick, 1.0, 0.0).astype(bf16), normed)
        send_ref[...] = laid.astype(bf16)

    return kernel_call(
        body,
        (1,),
        ids,
        [(rows, None), (gain, None), (slot, None)]
        + [(a, None) for a in attended]
        + [head_rows(weight, j) for j in range(blocks)],
        [((tokens, width), f32, None), ((slots, width), bf16, None)],
    )


def normal_parts(values):
    below = 0.5 + 0.5 * lax.erf(values * 0.7071067811865476)
    fall = jnp.exp2(values * values * -0.7213475204444817)
    return below, values * fall * 0.3989422804014327


def unit_specs(weights, step):
    starts = [0]
    for w in weights:
        starts.append(starts[-1] + w.shape[0] // step)

    def spec(j):
        last = starts[j + 1] - starts[j] - 1
        return pl.BlockSpec(
            (step, weights[j].shape[1]), lambda i, d: (jnp.clip(i - starts[j], 0, last), 0)
        )

    return starts, [(w, spec(j)) for j, w in enumerate(weights)]


def take_units(refs, starts, held):
    here = pl.program_id(0)
    for j, ref in enumerate(refs):

        @pl.when((here >= starts[j]) & (here < starts[j + 1]))
        def _():
            held[...] = ref[...]


def expert_grad_act(ids, grads, weights):
    slots, width = grads.shape
    step = 512
    starts, units = unit_specs(weights, step)
    hidden = starts[-1] * step

    def body(ids_ref, g_ref, *refs):
        w_refs, (out_ref, held) = refs[:-2], refs[-2:]
        take_units(w_refs, starts, held)
        out_ref[...] = dot(g_ref[...], held[...], NT)

    return kernel_call(
        body,
        (hidden // step,),
        ids,
        [(grads, None)] + units,
        [((slots, hidden), f32, pl.BlockSpec((slots, step), lambda i, d: (0, i)))],
        [pltpu.VMEM((step, width), bf16)],
    )[0]


def expert_main(ids, rows_in, grad_act, weights):
    slots, width = rows_in.shape
    step, rows = 512, 256
    units = [(j, first) for j, w in enumerate(weights) for first in range(0, w.shape[0], step)]
    hidden = len(units) * step

    def body(ids_ref, x_ref, ga_ref, *refs):
        w_refs, (act_ref, gp_ref, out_ref) = refs[:-3], refs[-3:]

        def held(c):
            j, first = units[c]
            return w_refs[j][first : first + step, :]

        pre, late, total = dot(x_ref[...], held(0), NT), None, None
        for c in range(len(units)):
            later = dot(x_ref[...], held(c + 1), NT) if c + 1 < len(units) else None
            part = slice(c * step, (c + 1) * step)
            below, dense = normal_parts(pre)
            act_ref[:, part] = (pre * below).astype(bf16)
            grad_pre = (ga_ref[:, part] * (below + dense)).astype(bf16)
            gp_ref[:, part] = grad_pre
            if late is not None:
                piece = dot(late, held(c - 1))
                total = piece if total is None else total + piece
            pre, late = later, grad_pre
        out_ref[...] = (total + dot(late, held(len(units) - 1))).astype(bf16)

    block = lambda n: pl.BlockSpec((rows, n), lambda i, d: (i, 0))
    return kernel_call(
        body,
        (slots // rows,),
        ids,
        [(rows_in, block(width)), (grad_act, block(hidden))] + [(w, None) for w in weights],
        [((slots, hidden), bf16, block(hidden))] * 2 + [((slots, width), bf16, block(width))],
    )


def expert_out(ids, activated, weights):
    slots, hidden = activated.shape
    width = weights[0].shape[1]
    rows = 256

    def body(ids_ref, act_ref, *refs):
        total, first = None, 0
        for ref in refs[:-1]:
            piece = dot(act_ref[:, first : first + ref.shape[0]], ref[...])
            total = piece if total is None else total + piece
            first += ref.shape[0]
        refs[-1][...] = total.astype(bf16)

    block = lambda n: pl.BlockSpec((rows, n), lambda i, d: (i, 0))
    return kernel_call(
        body,
        (slots // rows,),
        ids,
        [(activated, block(hidden))] + [(w, None) for w in weights],
        [((slots, width), bf16, block(width))],
    )[0]


def unit_grads(ids, lefts, rights, j, adds, kind, cuts=None):
    slots, width = rights[0].shape
    units = lefts[0].shape[1] // lax.axis_size("seq")
    step = 256
    steps = units // step
    pairs = len(lefts)
    block = pl.BlockSpec((step, width), lambda i, d: (i, 0))
    upto = lambda c: pl.BlockSpec((step, width), lambda i, d: (jnp.minimum(i, c - 1), 0))
    beyond = lambda c: pl.BlockSpec((step, width), lambda i, d: (jnp.maximum(i - c, 0), 0))
    add_ins, splits = [], []
    for pair in adds:
        for a in pair:
            if isinstance(a, tuple):
                c = a[0].shape[0] // step
                add_ins += [(a[0], upto(c)), (a[1], beyond(c))]
                splits.append(c)
            else:
                add_ins.append((a, block))
                splits.append(0)
    more = len(adds[0])

    def body(ids_ref, *refs):
        l_refs, r_refs, refs = refs[:pairs], refs[pairs : 2 * pairs], refs[2 * pairs :]
        add_refs, out_refs = list(refs[: len(add_ins)]), refs[len(add_ins) :]
        here = pl.program_id(0)
        for p in range(pairs):
            total = dot(l_refs[p][...], r_refs[p][...], TN)
            for c in splits[p * more : (p + 1) * more]:
                if c:
                    one, two = add_refs.pop(0), add_refs.pop(0)
                    total += jnp.where(here < c, one[...], two[...]).astype(f32)
                else:
                    total += add_refs.pop(0)[...].astype(f32)
            if not cuts:
                out_refs[p][...] = total.astype(kind)
                continue

            @pl.when(here < cuts[p])
            def _():
                out_refs[2 * p][...] = total.astype(kind)

            @pl.when(here >= cuts[p])
            def _():
                out_refs[2 * p + 1][...] = total.astype(kind)

    outs = [((units, width), kind, block)] * pairs
    if cuts:
        outs = []
        for c in cuts:
            outs += [((c * step, width), kind, upto(c)), ((units - c * step, width), kind, beyond(c))]
    return kernel_call(
        body,
        (steps,),
        ids,
        [(left, pl.BlockSpec((slots, step), lambda i, d: (0, j * steps + i))) for left in lefts]
        + [(right, None) for right in rights]
        + add_ins,
        outs,
    )


def block_result(ids, hidden, returned, column):
    tokens, width = hidden.shape
    slots = returned.shape[0]

    def body(ids_ref, h_ref, c_ref, back_ref, out_ref):
        pick = one_hot_columns(c_ref[...], slots)
        out_ref[...] = (h_ref[...] + dot(pick, back_ref[...])).astype(bf16)

    return kernel_call(
        body,
        (1,),
        ids,
        [(hidden, None), (column, None), (returned, None)],
        [((tokens, width), bf16, None)],
    )[0]


def norm_back(values, gain, grads):
    scale = norm_scale(values)
    scaled = grads * gain
    along = jnp.mean(values * scaled, axis=-1, keepdims=True)
    through = scale * scaled - values * (scale * scale * scale * along)
    return through, jnp.sum(grads * (values * scale), axis=0, keepdims=True)


def hidden_back(ids, hidden, cotangent, gain, returned, column, weight, attended):
    tokens, width = hidden.shape
    slots = returned.shape[0]
    blocks = lax.axis_size("seq")
    part = width // blocks
    kinds = [f32 if j % 2 == 0 else bf16 for j in range(blocks)]

    def body(ids_ref, h_ref, c_ref, gain_ref, col_ref, back_ref, *refs):
        weights, att, refs = refs[:blocks], refs[blocks : 2 * blocks], refs[2 * blocks :]
        (gh_ref, gain_out), att_refs, grad_refs = refs[:2], refs[2 : 2 + blocks], refs[2 + blocks :]
        pick = one_hot_columns(col_ref[...], slots)
        grads = dot(pick, back_ref[...])
        through, gain_grad = norm_back(h_ref[...], gain_ref[...], grads)
        grad_hidden = c_ref[...].astype(f32) + through
        gh_ref[...] = grad_hidden
        low = grad_hidden.astype(bf16)
        gain_out[...] = gain_grad
        for j in range(blocks):
            att_refs[j][...] = dot(low, weights[j][...], NT).astype(bf16)
        for j in range(blocks):
            grad_refs[j][...] = dot(att[j][...], low, TN).astype(kinds[j])

    out = kernel_call(
        body,
        (1,),
        ids,
        [(hidden, None), (cotangent, None), (gain, None), (column, None), (returned, None)]
        + [head_rows(weight, j) for j in range(blocks)]
        + [(a, None) for a in attended],
        [((tokens, width), f32, None), ((1, width), f32, None)]
        + [((tokens, part), bf16, None)] * blocks
        + [((part, width), kind, None) for kind in kinds],
    )
    return out[0], out[1], out[2 : 2 + blocks], out[2 + blocks :]


def projection_back(ids, grads, weight):
    blocks = len(grads)
    tokens = grads[0].shape[0]
    width = weight.shape[0]
    part = grads[0].shape[1] // 3
    heads = width // part
    kinds = [f32 if j % 2 == 0 else bf16 for j in range(blocks)]

    def body(ids_ref, *refs):
        g_refs, w_refs, out_refs = refs[:blocks], refs[blocks : blocks + 3], refs[blocks + 3 :]
        for j in (1, 3, 2, 0):
            total = None
            for w in range(3):
                piece = dot(g_refs[j][:, w * part : (w + 1) * part], w_refs[w][...], NT)
                total = piece if total is None else total + piece
            out_refs[j][...] = total.astype(kinds[j])

    column = lambda which: pl.BlockSpec((width, part), lambda i, d: (0, d[0] + which * heads))
    return kernel_call(
        body,
        (1,),
        ids,
        [(g, None) for g in grads] + [(weight, column(w)) for w in range(3)],
        [((tokens, width), kind, None) for kind in kinds],
    )


def projection_grad(ids, normed, grads, groups):
    blocks = len(normed)
    tokens, columns = grads[0].shape
    width = normed[0].shape[1]
    step, height = 256, width // groups
    pairs = step // height // 2

    def body(ids_ref, *refs):
        n_refs, g_refs = refs[:blocks], refs[blocks : 2 * blocks]
        kept_ref, sent_ref, held = refs[2 * blocks :]
        total = dot(n_refs[0][...], g_refs[0][...], TN)
        for j in range(1, blocks):
            total += dot(n_refs[j][...], g_refs[j][...], TN)
        held[...] = total
        odd = ids_ref[1] % 2
        for b in range(pairs):
            kept = pl.multiple_of(2 * b * height + odd * height, 8)
            sent = pl.multiple_of((2 * b + 1) * height - odd * height, 8)
            kept_ref[b] = held[pl.ds(kept, height), :]
            sent_ref[b] = held[pl.ds(sent, height), :].astype(bf16)

    block = pl.BlockSpec((pairs, height, columns), lambda i, d: (i, 0, 0))
    return kernel_call(
        body,
        (width // step,),
        ids,
        [(n, pl.BlockSpec((tokens, step), lambda i, d: (0, i))) for n in normed]
        + [(g, None) for g in grads],
        [((groups // 2, height, columns), f32, block), ((groups // 2, height, columns), bf16, block)],
        [pltpu.VMEM((step, columns), f32)],
    )


def sum_groups(ids, pieces, out_pieces, part):
    rows, width = pieces.shape[1:]
    groups, height, total = out_pieces.shape

    def body(ids_ref, in_ref, out_in_ref, mixed_ref, rest_ref):
        low = sum(in_ref[k].astype(f32) for k in range(pieces.shape[0])).astype(bf16)
        out = sum(out_in_ref[k].astype(f32) for k in range(groups))
        tall = [out[:, c * part : (c + 1) * part] for c in range(total // part)]
        tall = jnp.concatenate(tall, axis=0).astype(bf16)
        for k in range(groups):
            mixed_ref[k, :, :part] = low[:, :part]
            mixed_ref[k, :, part:] = tall
            rest_ref[k] = low[:, part:]

    return kernel_call(
        body,
        (1,),
        ids,
        [(pieces, None), (out_pieces, None)],
        [((groups, rows, 2 * part), bf16, None), ((groups, rows, width - part), bf16, None)],
        vmem=28,
    )


def across(value, alike=False):
    size = lax.axis_size("expert")
    sets = [list(range(p, size, 2)) for p in range(2)] if alike else None
    return lax.all_to_all(
        value, "expert", split_axis=0, concat_axis=0, tiled=True, axis_index_groups=sets
    )


def after(value, *earlier):
    return lax.optimization_barrier((value, *earlier))[0]


def after_all(values, *earlier):
    return lax.optimization_barrier((*values, *earlier))[: len(values)]


def spread_over_seq(value, *earlier):
    far = after(swap(value, "seq", 2), *earlier)
    return [value, swap(value, "seq", 1), far, swap(far, "seq", 1)]


def widen_columns(ids, pieces, first, count, total, out=None, half=None):
    blocks = len(pieces)
    rows, columns = pieces[0].shape
    height = rows if half is None else rows // 2
    part = total // 3 // blocks
    step = 256

    def body(ids_ref, *refs):
        me = ids_ref[0]
        for j in range(blocks):
            at = pl.multiple_of((me ^ j) * part, part)
            refs[-1][:, pl.ds(at, part)] = refs[j][...].astype(f32)

    begin = (half or 0) * height // step
    spec = pl.BlockSpec((step, part * blocks), lambda i, w, d: (begin + i, first + w))
    whole_rows = pl.BlockSpec((step, part), lambda i, w, d: (begin + i, w))
    half_rows = pl.BlockSpec((step, part), lambda i, w, d: (i, w))
    ins = [(p, whole_rows if p.shape[0] == rows else half_rows) for p in pieces]
    aliases = {}
    if out is not None:
        ins.append((out, pl.BlockSpec(memory_space=pl.ANY)))
        aliases = {len(ins): 0}
    return kernel_call(
        body,
        (height // step, count),
        ids,
        ins,
        [((rows, total), f32, spec)],
        aliases=aliases,
        vmem=28,
    )[0]


def widen_rows(ids, pieces, groups):
    blocks = len(pieces)
    width = pieces[0].shape[0]
    part = pieces[0].shape[1] // 2
    height, tall = part // groups, width // groups

    def body(ids_ref, *refs):
        me = ids_ref[0]
        for j in range(blocks):
            for e in range(groups):
                cut = refs[j][e * tall : (e + 1) * tall, :].astype(f32)
                at = pl.multiple_of((me ^ j) * part, part) + e * height
                for c in range(blocks):
                    refs[blocks][pl.ds(pl.multiple_of(at, 8), height), c * part : (c + 1) * part] = cut[
                        c * height : (c + 1) * height
                    ]

    return kernel_call(
        body,
        (1,),
        ids,
        [(p, pl.BlockSpec((width, part), lambda i, d: (0, 1))) for p in pieces],
        [((width, part * blocks), f32, None)],
        vmem=28,
    )[0]


def input_back(ids, rows, gain, grad_hidden, pieces):
    tokens, width = rows.shape

    def body(ids_ref, x_ref, gain_ref, gh_ref, a_ref, b_ref, c_ref, out_ref, gain_out):
        grads = a_ref[...] + b_ref[...].astype(f32) + c_ref[...].astype(f32)
        through, gain_grad = norm_back(x_ref[...].astype(f32), gain_ref[...], grads)
        out_ref[...] = gh_ref[...] + through
        gain_out[...] = gain_grad

    return kernel_call(
        body,
        (1,),
        ids,
        [(rows, None), (gain, None), (grad_hidden, None)] + [(a, None) for a in pieces],
        [((tokens, width), f32, None), ((1, width), f32, None)],
    )


def sum_along(value, axis):
    step = 1
    while step < lax.axis_size(axis):
        value = value + swap(value, axis, step)
        step *= 2
    return value


def shards(
    inputs,
    query_key_value_weight,
    output_weight,
    gain_attn,
    gain_ffn,
    w_up,
    w_down,
    expert_of,
    cotangent,
):
    groups = lax.axis_size("expert")
    blocks = lax.axis_size("seq")
    seq_count, local_len, width = inputs.shape
    tokens = seq_count * local_len
    capacity = max(2, 2 * tokens // groups)
    ids = jnp.stack([lax.axis_index("seq"), lax.axis_index("expert")]).astype(jnp.int32)
    gain_a, gain_f = gain_attn.reshape(1, width), gain_ffn.reshape(1, width)
    rows = inputs.reshape(tokens, width)
    cot = cotangent.reshape(tokens, width)

    down, up = w_down[0], w_up[0]
    rows_1 = swap(rows, "seq", 1)
    split = 5 * tokens // 8
    far_0, far_1 = swap(rows[:split], "seq", 2), swap(rows[split:], "seq", 2)
    down_near, up_near = swap(down, "seq", 1), swap(up, "seq", 1)
    first = project(ids, (rows, rows_1), gain_a, query_key_value_weight)
    slot, column, send = route(
        ids, expert_of.reshape(1, tokens), after(cot, first[0][0]), groups, capacity
    )
    send = after(send, far_0, down_near, up_near)
    rows_2 = after(jnp.concatenate([far_0, far_1], axis=0), send)
    grads_in = to_groups(send)
    rows_3 = swap(rows_2, "seq", 1)

    cut = up.shape[0] // 2
    up_far = swap(after(up[:cut], rows_2), "seq", 2)
    second = project(ids, (rows_2, rows_3), gain_a, query_key_value_weight)
    normed, queries, keys, values = (list(p) for p in zip(*first, *second))
    out, ot, lse = attention(ids, queries, keys, values)
    out = lax.optimization_barrier((*out, up_far))[:blocks]
    attended = [out[0]] + [swap(out[j], "seq", j) for j in range(1, blocks)]
    down_far = swap(after(down, *attended), "seq", 2)
    up_more = swap(after(up[cut:], *attended), "seq", 2)
    hidden, send = attention_out(
        ids, rows, attended, output_weight, gain_f, slot, groups, capacity
    )
    up_near_far = swap(after(up_far, send), "seq", 1)
    down_all = [down, down_near, down_far, swap(down_far, "seq", 1)]

    rows_in = to_groups(after(send, grads_in))
    grad_act = expert_grad_act(ids, grads_in, down_all)
    up_more = after(up_more, grad_act)
    up_all = [up, up_near, up_far, up_more, up_near_far, swap(up_more, "seq", 1)]
    activated, grad_pre, back = expert_main(ids, rows_in, grad_act, up_all)
    returned_grad = to_groups(back)
    left, right = (grad_pre, activated), (rows_in, grads_in)
    none = ((), ())
    near_3 = [swap(p, "seq", 1) for p in unit_grads(ids, left, right, 3, none, bf16)]
    near_1 = [swap(p, "seq", 1) for p in unit_grads(ids, left, right, 1, none, bf16)]
    up_0, up_1, down_0, down_1 = unit_grads(
        ids, left, right, 2, [(p,) for p in near_3], bf16, (1, 1)
    )
    up_0 = swap(up_0, "seq", 2)
    down_0 = swap(after(down_0, up_0), "seq", 2)
    result = expert_out(ids, after(activated, down_1), down_all)

    returned_grad = after(returned_grad, result, up_0, *near_1)
    returned = to_groups(after(result, returned_grad))
    grad_hidden, ffn_gain_part, grad_att, out_parts = hidden_back(
        ids, hidden, cot, gain_f, returned_grad, column, output_weight, attended
    )
    grad_att = after_all(grad_att, down_0)
    grad_att = [grad_att[0]] + [swap(grad_att[j], "seq", j) for j in range(1, blocks)]
    near_out = [swap(after(out_parts[j], grad_att[1]), "seq", 1) for j in (1, 3)]
    far_out = (out_parts[2] + near_out[1].astype(f32)).astype(bf16)
    far_out = swap(after(far_out, *grad_att), "seq", 2)
    up_1 = swap(after(up_1, *grad_att), "seq", 2)
    down_1 = swap(after(down_1, *grad_att), "seq", 2)
    grad_proj = attention_back(ids, queries, keys, values, grad_att, ot, lse)
    grad_proj = after_all(grad_proj, far_out)

    kept, sent = projection_grad(ids, normed, grad_proj, groups)
    other = swap(sent, "expert", 1)
    out_part = (out_parts[0] + near_out[0].astype(f32) + far_out.astype(f32)).astype(bf16)
    height = out_part.shape[0] // groups
    out_own = across(after(out_part, returned, sent).reshape(groups, height, width))
    pieces = projection_back(ids, after_all(grad_proj, sent), query_key_value_weight)
    near = [swap(pieces[j], "seq", 1) for j in (1, 3)]
    far_rows = (pieces[2] + near[1].astype(f32)).astype(bf16)
    out_own = after(out_own, up_1, pieces[0])
    summed = across(after((kept + other.astype(f32)).astype(bf16), out_own), alike=True)
    far_arrived = swap(far_rows, "seq", 2)
    up_left = after(grad_pre, out_own)
    up_grad = unit_grads(ids, [up_left], [rows_in], 0, [(near_1[0], (up_0, up_1))], f32)[0]
    summed = after(summed, up_grad, down_1, far_rows)
    part = width // blocks
    mixed, rest = sum_groups(ids, summed, out_own, part)
    mixed_own = across(mixed).reshape(width, 2 * part)
    block_out = block_result(ids, hidden, after(returned, rest), column)
    mixed_own = after(mixed_own, block_out, far_arrived)

    rest_own = across(after(rest, mixed_own)).reshape(width, 2 * part)
    input_grad, attn_gain_part = input_back(
        ids, rows, gain_a, grad_hidden, (pieces[0], near[0], after(far_arrived, mixed_own))
    )
    gains = jnp.concatenate([attn_gain_part, ffn_gain_part], axis=0)
    gains = sum_along(gains + swap(gains, "seq", 1), "expert")
    mixed_all = spread_over_seq(mixed_own, gains)
    qkv_grad = widen_columns(ids, mixed_all, 0, 1, 3 * width)
    out_grad = widen_rows(ids, after_all(mixed_all, qkv_grad), groups)
    rest_own = after(rest_own, out_grad)
    down_left = after(activated, rest_own)
    down_grad = unit_grads(ids, [down_left], [grads_in], 0, [(near_1[1], (down_0, down_1))], f32)[0]
    gains = gains + swap(after(gains, rest_own), "seq", 2)
    rest_near = swap(rest_own, "seq", 1)
    rest_far = [swap(r, "seq", 2) for r in (rest_own[: width // 2], rest_own[width // 2 :])]
    rest_far[0] = after(rest_far[0], gains, down_grad)
    for i in range(2):
        rest_all = [rest_own, rest_near, rest_far[i], swap(rest_far[i], "seq", 1)]
        qkv_grad = widen_columns(ids, rest_all, 1, 2, 3 * width, qkv_grad, i)

    return (
        block_out.reshape(inputs.shape),
        input_grad.reshape(inputs.shape),
        qkv_grad,
        out_grad,
        gains[0],
        gains[1],
        up_grad[None],
        down_grad[None],
    )


def solution(mesh):
    tokens = P("expert", "seq", None)
    units = P("expert", "seq", None)
    in_specs = (tokens, P(), P(), P(), P(), units, units, P("expert", "seq"), tokens)
    out_specs = (tokens, tokens, P(), P(), P(), P(), units, units)
    return jax.shard_map(shards, mesh=mesh, in_specs=in_specs, out_specs=out_specs, check_vma=False)
```
